32 devices in a mesh: section: 2 (over core), tensor: 4 (over y, x), dp: 4 (over z).
Axes of the slice: x: 2, y: 2, z: 4, core: 2. Of those that a mesh axis runs over, the one named last changes fastest.
Arguments:
- inputs: bfloat16 [8, 1024, 768], P('dp', 'tensor')
- norm_gains: float32 [2, 2, 768], P('section'), may hold values from 0.5 to 1.5
- attention_in: bfloat16 [2, 3, 768, 768], P('section', None, None, 'tensor'), may hold values from -0.21875 to 0.21875
- attention_out: bfloat16 [2, 768, 768], P('section', 'tensor'), may hold values from -1.25 to 1.25
- bias_table: float32 [2, 32, 12], P('section', None, 'tensor'), may hold values from -4 to 4
- router_weight: bfloat16 [2, 768, 4], P('section'), may hold values from -0.15625 to 0.15625
- up_weight: bfloat16 [2, 4, 768, 3072], P('section', None, None, 'tensor'), may hold values from -0.21875 to 0.21875
- down_weight: bfloat16 [2, 4, 3072, 768], P('section', None, 'tensor'), may hold values from -0.3125 to 0.3125
- routes: int32 [2, 8, 1024, 1], P('section', 'dp'), may hold values from 0 to 3; in each aligned block of 1024 rows (0 to 1023, 1024 to 2047, ..., all dimensions but the last counted through in order) at most 320 rows name the same one
- piece_starts: int32 [8, 2], P('dp'), may hold values from 0 to 768, as said below
- valid_mask: int32 [8, 1024], P('dp'), may hold values from 0 to 1, as said below
- cotangent: bfloat16 [8, 1024, 768], P('dp', 'tensor'), may hold values from -6 to 6
Outputs:
- layer_output: bfloat16 [2, 8, 1024, 768], P('section', 'dp', 'tensor')
- input_grad: float32 [2, 8, 1024, 768], P('section', 'dp', 'tensor')
- gain_grad: float32 [2, 2, 768], P('section')
- attention_in_grad: float32 [2, 3, 768, 768], P('section', None, 'dp', 'tensor')
- attention_out_grad: float32 [2, 768, 768], P('section', ('tensor', 'dp'))
- bias_grad: float32 [2, 32, 12], P('section', 'dp', 'tensor')
- router_grad: float32 [2, 768, 4], P('section')
- up_grad: float32 [2, 4, 768, 3072], P('section', None, 'dp', 'tensor')
- down_grad: float32 [2, 4, 3072, 768], P('section', None, ('tensor', 'dp'))
- root_means: float32 [2, 3], P('section')
The draws below stay inside these ranges and needn't reach their ends.
Inputs may be any that keep to these rules, and one draw needn't show every extreme that they name: `routes`: in each sequence of each layer, no expert is named by more than 320 tokens. `piece_starts`: the 2 starts of a sequence rise; each piece of 256 tokens lies inside the sequence and pieces do not intersect. `valid_mask`: the valid tokens of a sequence form a prefix that holds its first token.
All inputs are finite; a program needn't handle non-finite values.
Results may differ from the reference program's by a relative error of at most 0.03.
Values may be sent and summed in bfloat16 or wider, within the bound.
No kernel may reach another device: no remote copies, remote signals or barrier semaphores. Data moves between devices by JAX's collectives and lax.ppermute only.
A program may use at most 320 MiB of HBM per device.

```python
import math
import jax
import jax.numpy as jnp
import numpy as np
from jax import lax

D = 768
HEADS = 12
HEAD_DIM = 64
FF = 3072
BUCKETS = 32
EXPERTS = 4
CAP = 320
SEQ = 1024
PIECE = 256
PIECES = 2
LAYERS = 2
SEQS = 8


def draw_inputs(key, part):
    key = jax.random.fold_in(key, 11)
    seq_scale = 0.6 + 1.2 * jnp.arange(SEQS, dtype=jnp.float32)[:, None, None] / max(SEQS - 1, 1)
    base_draw = jax.random.normal(key, (SEQS, SEQ, D), jnp.float32)
    return (seq_scale * base_draw).astype(jnp.bfloat16)


def draw_piece_starts(key, part):
    key = jax.random.fold_in(key, 12)
    spare_room = SEQ - PIECES * PIECE
    offsets = jnp.sort(jax.random.randint(key, (SEQS, PIECES), 0, spare_room + 1), axis=-1)
    return (offsets + PIECE * jnp.arange(PIECES, dtype=jnp.int32)[None, :]).astype(jnp.int32)


def draw_valid_mask(key, part):
    key = jax.random.fold_in(key, 13)
    quarter = SEQ // 4
    base_length = quarter + 3 * quarter * jnp.arange(SEQS, dtype=jnp.int32) // SEQS
    extra_length = jax.random.randint(key, (SEQS,), 0, quarter + 1)
    lengths = jnp.minimum(base_length + extra_length, SEQ)
    return (jnp.arange(SEQ, dtype=jnp.int32)[None, :] < lengths[:, None]).astype(jnp.int32)


def shard_levels(own_key, shape, shards, low, largest):
    level = 1.0
    for dim, shards_of in shards:
        draws = jax.random.uniform(jax.random.fold_in(jax.random.fold_in(own_key, 6), dim), (shards_of,), jnp.float32, low / len(shards), largest / len(shards))
        level = level * jnp.repeat(jnp.exp(draws), shape[dim] // shards_of).reshape((-1,) + (1,) * (len(shape) - 1 - dim))
    return level


def shared_out(rng, own, number, rows, amount, top, reach, skew):
    ranking = jax.random.permutation(rng, amount)
    packed, ordinary = portions_of(amount, rows * top, reach, skew, True), portions_of(amount, rows * top, reach, skew, False)
    places = jnp.arange(amount)

    def named(tallies, rotation):
        used = int((tallies > 0).sum())
        fixed = max(1, used // 4)
        moved = fixed + (places - fixed + rotation * (used - fixed)) % max(1, amount - fixed)
        return jnp.zeros((amount,), jnp.int32).at[ranking[jnp.where(places < fixed, places, moved)]].set(jnp.asarray(tallies, jnp.int32))

    tallies = jnp.where(number % 4 == 0, named(packed, number // 4), named(ordinary, number - number // 4 - 1))
    mixed = jax.random.permutation(jax.random.fold_in(own, 3), amount)
    source_of, taker = mixed[0:amount // 2 * 2:2], mixed[1:amount // 2 * 2:2]
    margin = jnp.minimum(tallies[source_of] - 1, reach - tallies[taker]) // 2
    margin = jnp.where((source_of == ranking[0]) | (taker == ranking[0]) | (tallies[taker] == 0), 0, jnp.maximum(margin, 0))
    moved = jax.random.randint(jax.random.fold_in(own, 4), (amount // 2,), 0, 1 << 20) % (margin + 1)
    tallies = tallies.at[source_of].add(-moved).at[taker].add(moved)
    items = jnp.searchsorted(jnp.cumsum(tallies), jnp.arange(rows * top), side="right").astype(jnp.int32)
    listing = items.reshape(top, rows).T
    listing = listing[jax.random.permutation(jax.random.fold_in(own, 1), rows)]
    rotation = jax.random.randint(jax.random.fold_in(own, 2), (rows, 1), 0, top)
    return jnp.take_along_axis(listing, (jnp.arange(top)[None, :] + rotation) % top, axis=1)


def portions_of(number_of, total, bound, lean, full):
    portions = [(1 << 20) // math.isqrt(standing ** lean) + 1 for standing in range(1, number_of + 1)]
    largest = bound if full else min(bound, max(-(-total // number_of), total * portions[0] // sum(portions)))
    least = 1 if total - largest >= number_of - 1 else 0
    holding, rest = [largest] + [least] * (number_of - 1), total - largest - least * (number_of - 1)
    while rest > 0:
        free = [i for i in range(1, number_of) if holding[i] < largest] or [i for i in range(1, number_of) if holding[i] < bound]
        whole, remaining = sum([portions[i] for i in free]), rest
        for i in free:
            extra = min(bound - holding[i], max(1, remaining * portions[i] // whole), rest)
            holding[i] = holding[i] + extra
            rest = rest - extra
    return np.array(holding)


def bell_draw(key, dims, deviation, reach, shards=(), kind=jnp.bfloat16):
    array = deviation * jax.random.normal(key, dims, jnp.float32)
    if shards:
        array = array * shard_levels(key, dims, shards, -0.22, 0.18)
    return jnp.clip(array, -reach, reach).astype(kind)


def setup_inputs(seed: int = 0) -> dict:
    arg_keys = jax.random.split(jax.random.key(seed), 13)
    inputs = draw_inputs(jax.random.fold_in(arg_keys[12], 71), 0)
    norm_gains = jnp.clip(1.0 + 0.1 * jax.random.normal(arg_keys[1], (LAYERS, 2, D), jnp.float32), 0.5, 1.5)
    attention_in = bell_draw(arg_keys[2], (LAYERS, 3, D, HEADS * HEAD_DIM), D ** -0.5, 0.21875, ((0, 2), (3, 4)))
    attention_out = bell_draw(arg_keys[3], (LAYERS, HEADS * HEAD_DIM, D), (HEADS * HEAD_DIM // 32) ** -0.5, 1.25, ((0, 2), (1, 4)))
    bias_table = bell_draw(arg_keys[4], (LAYERS, BUCKETS, HEADS), 1.0, 4.0, ((0, 2), (2, 4)), jnp.float32)
    router_weight = bell_draw(arg_keys[5], (LAYERS, D, EXPERTS), (2 * D) ** -0.5, 0.15625, ((0, 2),))
    up_weight = bell_draw(arg_keys[6], (LAYERS, EXPERTS, D, FF), D ** -0.5, 0.21875, ((0, 2), (3, 4)))
    down_weight = bell_draw(arg_keys[7], (LAYERS, EXPERTS, FF, D), (FF // 8) ** -0.5, 0.3125, ((0, 2), (2, 4)))
    routes_keys = jax.random.split(jax.random.fold_in(arg_keys[8], 1), LAYERS * SEQS * SEQ // SEQ)
    routes_turns = jax.random.permutation(jax.random.fold_in(arg_keys[8], 3), LAYERS * SEQS * SEQ // SEQ)
    routes = jax.vmap(lambda own, number: shared_out(jax.random.fold_in(arg_keys[8], 2), own, number, SEQ, EXPERTS, 1, CAP, 1))(routes_keys, routes_turns).reshape((LAYERS, SEQS, SEQ, 1))
    piece_starts = draw_piece_starts(jax.random.fold_in(arg_keys[12], 71), 0)
    valid_mask = draw_valid_mask(jax.random.fold_in(arg_keys[12], 71), 0)
    cotangent = bell_draw(arg_keys[11], (SEQS, SEQ, D), 1.0, 6.0, ((0, 4), (1, 4)))
    return {"inputs": inputs, "norm_gains": norm_gains, "attention_in": attention_in, "attention_out": attention_out, "bias_table": bias_table, "router_weight": router_weight, "up_weight": up_weight, "down_weight": down_weight, "routes": routes, "piece_starts": piece_starts, "valid_mask": valid_mask, "cotangent": cotangent}


epsilon = 1e-06
bucket_edges = (12, 16, 23, 32, 46, 64, 91)
masked_score = -1000000000.0

@jax.custom_vjp
def low(v):
    return lax.optimization_barrier(v.astype(jnp.bfloat16)).astype(jnp.float32)

@jax.custom_vjp
def low_back(v):
    return v

def low_keep(v):
    return (low(v), None)

def low_pass(kept, grad):
    return (grad,)

def back_keep(v):
    return (v, None)

def back_low(kept, grad):
    return (low(grad),)
low.defvjp(low_keep, low_pass)
low_back.defvjp(back_keep, back_low)

def offset_buckets(offsets):
    distance = jnp.abs(offsets)
    far_bucket = jnp.full(offsets.shape, 8, jnp.int32)
    for edge_value in bucket_edges:
        far_bucket = far_bucket + (distance >= edge_value).astype(jnp.int32)
    bucket_near = jnp.where(distance < 8, distance, far_bucket).astype(jnp.int32)
    return bucket_near + jnp.where(offsets > 0, 16, 0).astype(jnp.int32)

def root_norm(vector, gain_row):
    return vector * lax.rsqrt(lax.optimization_barrier(jnp.mean(vector * vector, axis=-1, keepdims=True)) + epsilon) * gain_row

def matmul_high(left, right):
    return jnp.dot(left, right, precision=lax.Precision.HIGHEST, preferred_element_type=jnp.float32)

def piece_labels(starts):
    position = jnp.arange(SEQ, dtype=jnp.int32)[:, None]
    inside = (position >= starts[None, :]) & (position < starts[None, :] + PIECE)
    labels = jnp.arange(1, PIECES + 1, dtype=jnp.int32)[None, :]
    return (lax.optimization_barrier(jnp.sum(jnp.where(inside, labels, 0), axis=1)) - 1).astype(jnp.int32)

def attend(queries, keys_all, values_all, bias_table, pieces, valid_row):
    block_rows = min(512, SEQ)
    scale_factor = HEAD_DIM ** (-0.5)
    columns = jnp.arange(SEQ, dtype=jnp.int32)

    def one_block(block_args):
        query_block, first_row = block_args
        positions = first_row + jnp.arange(block_rows, dtype=jnp.int32)
        offsets = columns[None, :] - positions[:, None]
        bias_block = jnp.transpose(bias_table[offset_buckets(offsets)], (2, 0, 1))
        scores = jnp.einsum('qhd,khd->hqk', query_block, keys_all, precision=lax.Precision.HIGHEST) * scale_factor + bias_block
        scores = low_back(scores)
        row_piece = pieces[positions]
        allowed = (valid_row[None, :] > 0) & ((columns[None, :] <= positions[:, None]) | (row_piece[:, None] == pieces[None, :]) & (row_piece[:, None] >= 0))
        scores = jnp.where(allowed[None], scores, masked_score)
        weights_block = low(jax.nn.softmax(scores, axis=-1))
        return jnp.einsum('hqk,khd->qhd', weights_block, values_all, precision=lax.Precision.HIGHEST)
    blocks = queries.reshape(SEQ // block_rows, block_rows, HEADS, HEAD_DIM)
    block_starts = jnp.arange(SEQ // block_rows, dtype=jnp.int32) * block_rows
    attended = lax.map(jax.checkpoint(one_block), (blocks, block_starts))
    return attended.reshape(SEQ, HEADS * HEAD_DIM)

def run_sequence(hidden, norm_gains, attention_in, attention_out, bias_table, router_weight, up_weight, down_weight, route_row, pieces, valid_row):
    normed = low(root_norm(hidden, norm_gains[0]))
    queries = low_back(low(matmul_high(normed, attention_in[0]))).reshape(SEQ, HEADS, HEAD_DIM)
    keys_all = low_back(low(matmul_high(normed, attention_in[1]))).reshape(SEQ, HEADS, HEAD_DIM)
    values_all = low_back(low(matmul_high(normed, attention_in[2]))).reshape(SEQ, HEADS, HEAD_DIM)
    attended = low_back(low(attend(queries, keys_all, values_all, bias_table, pieces, valid_row)))
    attn_branch = low_back(matmul_high(attended, attention_out))
    middle = hidden + attn_branch
    normed_mid = low(root_norm(middle, norm_gains[1]))
    logits = low_back(matmul_high(normed_mid, router_weight))
    router_probs = jax.nn.softmax(logits, axis=-1)
    route_hits = route_row[:, None] == jnp.arange(EXPERTS, dtype=jnp.int32)[None, :]
    gate_value = lax.optimization_barrier(jnp.sum(jnp.where(route_hits, router_probs, 0.0), axis=-1))
    hits_count = route_hits.astype(jnp.int32)
    slot_index = lax.optimization_barrier(jnp.sum(hits_count * (jnp.cumsum(hits_count, axis=0) - 1), axis=1)).astype(jnp.int32)
    target = route_row * CAP + slot_index
    table_disp = (target[:, None] == jnp.arange(EXPERTS * CAP, dtype=jnp.int32)[None, :]).astype(hidden.dtype)
    expert_in = low_back(jnp.einsum('sj,sd->jd', table_disp, normed_mid, precision=lax.Precision.HIGHEST)).reshape(EXPERTS, CAP, D)
    hidden_up = low_back(jnp.einsum('ecd,edf->ecf', expert_in, up_weight, precision=lax.Precision.HIGHEST))
    activated = low(jax.nn.gelu(hidden_up, approximate=True))
    expert_out = low(jnp.einsum('ecf,efd->ecd', activated, down_weight, precision=lax.Precision.HIGHEST)).reshape(EXPERTS * CAP, D)
    combined = low_back(jnp.einsum('sj,jd->sd', table_disp, expert_out, precision=lax.Precision.HIGHEST))
    expert_branch = gate_value[:, None] * combined
    return (middle + expert_branch, attn_branch, expert_branch)

def reference(inputs, norm_gains, attention_in, attention_out, bias_table, router_weight, up_weight, down_weight, routes, piece_starts, valid_mask, cotangent):
    weights = tuple((value_in.astype(jnp.float32) for value_in in (norm_gains, attention_in, attention_out, bias_table, router_weight, up_weight, down_weight)))
    start_state = inputs.astype(jnp.float32)
    probe_zero = jnp.zeros((LAYERS, SEQS, SEQ, D), start_state.dtype)
    pieces = jax.vmap(piece_labels)(piece_starts)
    valid_weight = valid_mask.astype(start_state.dtype)
    valid_count = jnp.sum(valid_weight)

    def squares(field_value):
        return jnp.sum(valid_weight[:, :, None] * field_value * field_value)

    def whole_model(probe_in, *layer_weights):
        state_now = start_state + probe_in[0]
        results = []
        measured = []
        for layer_index in range(LAYERS):
            params = tuple((weight_all[layer_index] for weight_all in layer_weights))

            def per_sequence(sequence_args):
                return run_sequence(sequence_args[0], *params, sequence_args[1], sequence_args[2], sequence_args[3])
            out_state, attn_branch, expert_branch = lax.map(per_sequence, (state_now, routes[layer_index, :, :, 0], pieces, valid_mask))
            measured.append(jnp.stack([squares(state_now), squares(attn_branch), squares(expert_branch)]))
            rounded = low(out_state)
            results.append(rounded)
            if layer_index + 1 < LAYERS:
                state_now = low_back(rounded + probe_in[layer_index + 1])
        return (tuple(results), jnp.stack(measured))
    results, backward, measured = jax.vjp(whole_model, probe_zero, *weights, has_aux=True)
    cotangents = tuple((jnp.zeros_like(entry) for entry in results[:-1])) + (cotangent.astype(start_state.dtype),)
    grads = backward(cotangents)
    root_means = jnp.sqrt(measured / (valid_count * D))
    return (jnp.stack(results).astype(jnp.bfloat16), grads[0], grads[1], grads[2], grads[3], grads[4], grads[5], grads[6], grads[7], root_means)
```

```python
import functools

import jax
import jax.numpy as jnp
import numpy as np
from jax import lax
from jax.experimental import pallas as pl
from jax.experimental.pallas import tpu as pltpu
from jax.sharding import PartitionSpec as P

D = 768
HEAD_DIM = 64
BUCKETS = 32
EXPERTS = 4
CAP = 320
SEQ = 1024
PIECE = 256
PIECES = 2
SLOTS = EXPERTS * CAP

QB = PIECE
BAND = 128
WIDE = 2 * QB + BAND
DIAGS = 6

epsilon = 1e-06
bucket_edges = (12, 16, 23, 32, 46, 64, 91)
masked_score = -1000000000.0
far_bucket_behind = 15

BF = jnp.bfloat16
F32 = jnp.float32
VMEM_LIMIT = 56 * 1024 * 1024


def dot(a, b, ca=1, cb=0):
    return lax.dot_general(a, b, (((ca,), (cb,)), ((), ())), preferred_element_type=F32)


def vm(count):
    return [pl.BlockSpec(memory_space=pltpu.VMEM)] * count


def smem():
    return pl.BlockSpec(memory_space=pltpu.SMEM)


def cost(flops, size):
    return pl.CostEstimate(flops=int(flops), bytes_accessed=int(size), transcendentals=0)


def shape(dims, kind):
    return jax.ShapeDtypeStruct(dims, kind)


def exchange(value, axis, mask):
    count = lax.axis_size(axis)
    return lax.ppermute(value, axis, [(i, i ^ mask) for i in range(count)])


def gather_parts(value):
    return [value] + [exchange(value, "tensor", k) for k in range(1, lax.axis_size("tensor"))]


def swap_parts(parts):
    return [parts[0]] + [exchange(p, "tensor", k) for k, p in enumerate(parts) if k]


def natural(t, k, size):
    return pl.ds(pl.multiple_of(jnp.bitwise_xor(t, k) * size, size), size)


def offset_buckets(offsets):
    distance = np.abs(offsets)
    far = np.full(offsets.shape, 8, np.int32)
    for edge_value in bucket_edges:
        far = far + (distance >= edge_value)
    return np.where(distance < 8, distance, far) + np.where(offsets > 0, 16, 0)


def diagonal_one_hot():
    lane = np.arange(2 * BAND)
    y = np.where(lane < BAND, lane, lane - 2 * BAND)
    offsets = BAND * (np.arange(DIAGS)[:, None] - 2) - y[None, :]
    hot = offset_buckets(offsets)[:, :, None] == np.arange(BUCKETS)
    hot = hot & (lane != BAND)[None, :, None]
    return hot.astype(np.float32)


def bias_body(rows_ref, out_ref):
    heads = out_ref.shape[1]
    for layer in range(out_ref.shape[0]):
        for h in range(heads):
            for d in range(DIAGS):
                row = rows_ref[layer, pl.ds(h * DIAGS + d, 1), :]
                tile = pltpu.roll(
                    jnp.broadcast_to(row, (BAND, 2 * BAND)), 0, 1, stride=1, stride_axis=0
                )[:, :BAND]
                for i in range(WIDE // BAND):
                    for j in range(QB // BAND):
                        if i - j == d - 1:
                            out_ref[
                                layer, h, i * BAND : (i + 1) * BAND, j * BAND : (j + 1) * BAND
                            ] = tile


def bias_tiles(rows):
    heads = rows.shape[1] // DIAGS
    return pl.pallas_call(
        bias_body,
        out_shape=shape((rows.shape[0], heads, WIDE, QB), F32),
        in_specs=vm(1),
        out_specs=vm(1)[0],
        compiler_params=pltpu.CompilerParams(vmem_limit_bytes=VMEM_LIMIT),
        cost_estimate=cost(1e6, 4e6),
        name="bias_tiles",
    )(rows)


def block_range(j):
    last = min(SEQ, QB * (j + 2))
    left = max(0, QB * j - BAND)
    return left, last, left - (QB * j - BAND)


def fill_mask(mask_ref, valid_ref, s0, s1, j):
    left, last, _ = block_range(j)
    width = last - left
    key = left + lax.broadcasted_iota(jnp.int32, (width, 1), 0)
    query = QB * j + lax.broadcasted_iota(jnp.int32, (1, QB), 1)

    def label(position, outside):
        second = jnp.where((position >= s1) & (position < s1 + PIECE), 1, outside)
        return jnp.where((position >= s0) & (position < s0 + PIECE), 0, second)

    allowed = (key <= query) | (label(key, -1) == label(query, -2))
    mask_ref[:width, :] = jnp.where(allowed, valid_ref[left:last, :], masked_score)


def fwd_attention_body(parts, norm_inside, *refs):
    info, valid_col, gain, w_ref, bias_ref = refs[:5]
    x_refs = refs[5 : 5 + parts]
    xn_ref, qkv_ref, turned_ref, lse_ref = refs[5 + parts : 9 + parts]
    out_refs = refs[9 + parts : 9 + 2 * parts]
    vt_ref, att_ref, mask_ref, valid_ref = refs[9 + 2 * parts :]
    t, s0, s1 = info[0], info[1], info[2]
    rows = SEQ // parts
    heads = qkv_ref.shape[1]

    valid_ref[...] = jnp.broadcast_to(valid_col[...], (SEQ, QB))
    for k in range(parts):
        where = natural(t, k, rows)
        x = x_refs[k][...]
        if norm_inside:
            xf = x.astype(F32)
            scale = lax.rsqrt(jnp.mean(xf * xf, axis=-1, keepdims=True) + epsilon)
            x = (xf * scale * gain[...]).astype(BF)
        xn_ref[where, :] = x
        for i in range(3):
            product = dot(x, w_ref[i])
            if i == 0:
                product = product * HEAD_DIM**-0.5
            turned = product.T.astype(BF)
            if i < 2:
                turned_ref[i, :, where] = turned
            else:
                vt_ref[:, where] = turned
            product = product.astype(BF)
            for h in range(heads):
                qkv_ref[i, h, where, :] = product[:, h * HEAD_DIM : (h + 1) * HEAD_DIM]

    for j in range(SEQ // QB):
        left, last, skip = block_range(j)
        width = last - left
        columns = slice(j * QB, (j + 1) * QB)
        fill_mask(mask_ref, valid_ref, s0, s1, j)

        def one_head(h, carry):
            lanes = pl.ds(pl.multiple_of(h * HEAD_DIM, HEAD_DIM), HEAD_DIM)
            scores = dot(qkv_ref[1, h, :last, :], turned_ref[0, lanes, columns])
            near = scores[left:] + bias_ref[h, skip : skip + width, :] + mask_ref[:width, :]
            highest = jnp.max(near, axis=0, keepdims=True)
            if left:
                far = scores[:left] + valid_ref[:left, :]
                highest = jnp.maximum(highest, jnp.max(far, axis=0, keepdims=True))
            near = jnp.exp(near - highest)
            total = jnp.sum(near, axis=0, keepdims=True)
            out = dot(vt_ref[lanes, left:last], near.astype(BF))
            if left:
                far = jnp.exp(far - highest)
                total = total + jnp.sum(far, axis=0, keepdims=True)
                out = out + dot(vt_ref[lanes, :left], far.astype(BF))
            lse_ref[h, :, columns] = highest + jnp.log(total)
            att_ref[lanes, columns] = (out * (1.0 / total)).astype(BF)
            return carry

        lax.fori_loop(0, heads, one_head, 0)

    for k in range(parts):
        out_refs[k][...] = att_ref[:, natural(t, k, rows)]


def fwd_attention(info, valid_col, gain, w, bias, x_parts, norm_inside):
    parts = len(x_parts)
    rows = SEQ // parts
    wide = w.shape[2]
    heads = wide // HEAD_DIM
    outs = pl.pallas_call(
        functools.partial(fwd_attention_body, parts, norm_inside),
        out_shape=[
            shape((SEQ, D), BF),
            shape((3, heads, SEQ, HEAD_DIM), BF),
            shape((2, wide, SEQ), BF),
            shape((heads, 1, SEQ), F32),
        ]
        + [shape((wide, rows), BF)] * parts,
        in_specs=[smem()] + vm(4 + parts),
        out_specs=vm(4 + parts),
        scratch_shapes=[
            pltpu.VMEM((wide, SEQ), BF),
            pltpu.VMEM((wide, SEQ), BF),
            pltpu.VMEM((WIDE, QB), F32),
            pltpu.VMEM((SEQ, QB), F32),
        ],
        compiler_params=pltpu.CompilerParams(vmem_limit_bytes=VMEM_LIMIT),
        cost_estimate=cost(9e9, 1e7),
        name="fwd_attention",
    )(info, valid_col, gain, w, bias, *x_parts)
    return outs[:4], list(outs[4:])


def bwd_attention_body(parts, *refs):
    info, valid_col, w_ref, bias_ref, qkv_ref, turned_ref, lse_ref = refs[:7]
    d_refs = refs[7 : 7 + parts]
    proj_ref, diag_ref, far_ref = refs[7 + parts : 10 + parts]
    out_refs = refs[10 + parts : 10 + 2 * parts]
    (
        d_ref,
        dt_ref,
        dq_ref,
        dk_ref,
        dv_ref,
        sum_ref,
        mask_ref,
        valid_ref,
    ) = refs[10 + 2 * parts :]
    t, s0, s1 = info[0], info[1], info[2]
    rows = SEQ // parts
    heads = qkv_ref.shape[1]

    valid_ref[...] = jnp.broadcast_to(valid_col[...], (SEQ, QB))
    for k in range(parts):
        where = natural(t, k, rows)
        block = d_refs[k][...]
        dt_ref[:, where] = block.astype(F32).T.astype(BF)
        for h in range(heads):
            d_ref[h, where, :] = block[:, h * HEAD_DIM : (h + 1) * HEAD_DIM]
    dk_ref[...] = jnp.zeros_like(dk_ref)
    dv_ref[...] = jnp.zeros_like(dv_ref)
    sum_ref[...] = jnp.zeros_like(sum_ref)
    far_ref[...] = jnp.zeros_like(far_ref)

    for j in range(SEQ // QB):
        left, last, skip = block_range(j)
        width = last - left
        columns = slice(j * QB, (j + 1) * QB)
        fill_mask(mask_ref, valid_ref, s0, s1, j)

        def one_head(h, carry):
            lanes = pl.ds(pl.multiple_of(h * HEAD_DIM, HEAD_DIM), HEAD_DIM)
            q_block = qkv_ref[0, h, columns, :]
            d_block = d_ref[h, columns, :]
            lse = lse_ref[h, :, columns]
            scores = dot(qkv_ref[1, h, :last, :], turned_ref[0, lanes, columns])
            slopes = dot(qkv_ref[2, h, :last, :], dt_ref[lanes, columns])
            near = scores[left:] + bias_ref[h, skip : skip + width, :] + mask_ref[:width, :]
            near = jnp.exp(near - lse)
            near_slope = near * slopes[left:]
            row_dot = jnp.sum(near_slope, axis=0, keepdims=True)
            if left:
                far = jnp.exp(scores[:left] + valid_ref[:left, :] - lse)
                far_slope = far * slopes[:left]
                row_dot = row_dot + jnp.sum(far_slope, axis=0, keepdims=True)
            near_slope = near_slope - near * row_dot
            sum_ref[h, skip : skip + width, :] += near_slope
            near_slope = near_slope.astype(BF)
            dk_ref[h, left:last, :] += dot(near_slope, q_block)
            dv_ref[h, left:last, :] += dot(near.astype(BF), d_block)
            dq = dot(turned_ref[1, lanes, left:last], near_slope)
            if left:
                far_slope = far_slope - far * row_dot
                far_ref[h] += jnp.sum(far_slope.reshape(left // 8, 8, QB), axis=0)
                far_slope = far_slope.astype(BF)
                dk_ref[h, :left, :] += dot(far_slope, q_block)
                dv_ref[h, :left, :] += dot(far.astype(BF), d_block)
                dq = dq + dot(turned_ref[1, lanes, :left], far_slope)
            dq_ref[lanes, columns] = dq * HEAD_DIM**-0.5
            return carry

        lax.fori_loop(0, heads, one_head, 0)

    for first in range(0, SEQ, rows):
        where = slice(first, first + rows)
        proj_ref[0, where, :] = dq_ref[:, where].T.astype(BF)
        for i, source in ((1, dk_ref), (2, dv_ref)):
            proj_ref[i, where, :] = jnp.concatenate(
                [source[h, where, :].astype(BF) for h in range(heads)], axis=1
            )
    for k in range(parts):
        where = natural(t, k, rows)
        total = dot(proj_ref[0, where, :], w_ref[0], 1, 1)
        for i in (1, 2):
            total = total + dot(proj_ref[i, where, :], w_ref[i], 1, 1)
        out_refs[k][...] = total.astype(BF)

    for h in range(heads):
        for d in range(DIAGS):
            tile = None
            for i in range(WIDE // BAND):
                for j in range(QB // BAND):
                    if i - j == d - 1:
                        more = sum_ref[
                            h, i * BAND : (i + 1) * BAND, j * BAND : (j + 1) * BAND
                        ]
                        tile = more if tile is None else tile + more
            diag_ref[h * DIAGS + d] = tile


def diagonal_body(tiles_ref, out_ref):
    row = lax.broadcasted_iota(jnp.int32, (BAND, BAND), 0)
    column = lax.broadcasted_iota(jnp.int32, (BAND, BAND), 1)
    flip = (row + column == BAND - 1).astype(F32)
    for i in range(tiles_ref.shape[0]):
        tile = lax.dot_general(
            flip,
            tiles_ref[i],
            (((1,), (0,)), ((), ())),
            precision=lax.Precision.HIGHEST,
            preferred_element_type=F32,
        )
        tile = jnp.concatenate([tile, jnp.zeros_like(tile)], axis=1)
        tile = pltpu.roll(tile, BAND + 1, 1, stride=1, stride_axis=0)
        out_ref[i : i + 1, :] = jnp.sum(tile, axis=0, keepdims=True)


def diagonal_sums(tiles):
    return pl.pallas_call(
        diagonal_body,
        out_shape=shape((tiles.shape[0], 2 * BAND), F32),
        in_specs=vm(1),
        out_specs=vm(1)[0],
        compiler_params=pltpu.CompilerParams(vmem_limit_bytes=VMEM_LIMIT),
        cost_estimate=cost(1e8, 1e6),
        name="diagonal_sums",
    )(tiles)


def bwd_attention(info, valid_col, w, bias, saved, d_parts):
    parts = len(d_parts)
    rows = SEQ // parts
    wide = w.shape[2]
    heads = wide // HEAD_DIM
    qkv, turned, lse = saved
    outs = pl.pallas_call(
        functools.partial(bwd_attention_body, parts),
        out_shape=[
            shape((3, SEQ, wide), BF),
            shape((heads * DIAGS, BAND, BAND), F32),
            shape((heads, 8, QB), F32),
        ]
        + [shape((rows, D), BF)] * parts,
        in_specs=[smem()] + vm(6 + parts),
        out_specs=vm(3 + parts),
        scratch_shapes=[
            pltpu.VMEM((heads, SEQ, HEAD_DIM), BF),
            pltpu.VMEM((wide, SEQ), BF),
            pltpu.VMEM((wide, SEQ), F32),
            pltpu.VMEM((heads, SEQ, HEAD_DIM), F32),
            pltpu.VMEM((heads, SEQ, HEAD_DIM), F32),
            pltpu.VMEM((heads, WIDE, QB), F32),
            pltpu.VMEM((WIDE, QB), F32),
            pltpu.VMEM((SEQ, QB), F32),
        ],
        compiler_params=pltpu.CompilerParams(vmem_limit_bytes=VMEM_LIMIT),
        cost_estimate=cost(1.8e10, 1e7),
        name="bwd_attention",
    )(info, valid_col, w, bias, qkv, turned, lse, *d_parts)
    return outs[:3], list(outs[3:])


def choose(select, own_ref, other_ref, to_ref):
    @pl.when(select == 0)
    def _():
        to_ref[...] = own_ref[0]

    @pl.when(select != 0)
    def _():
        to_ref[...] = other_ref[0]


def combine(parts, rows, target_col, slots_ref, out_refs):
    slot = lax.broadcasted_iota(jnp.int32, (rows, SLOTS), 1)
    for k in list(range(1, parts)) + [0]:
        hot = (target_col[k * rows : (k + 1) * rows, :] == slot).astype(BF)
        out_refs[k][...] = dot(hot, slots_ref[...]).astype(BF)


def dispatch(e, target_row, tokens_ref):
    slot = e * CAP + lax.broadcasted_iota(jnp.int32, (CAP, SEQ), 0)
    return dot((target_row[...] == slot).astype(BF), tokens_ref[...]).astype(BF)


def fwd_experts_body(parts, *refs):
    sel, target_row, target_col, router, up_own, up_other, down_own, down_other = refs[:8]
    x_refs = refs[8 : 8 + parts]
    in_ref, act_ref, slope_ref, gate_ref, probs_ref = refs[8 + parts : 13 + parts]
    out_refs = refs[13 + parts : 13 + 2 * parts]
    x_ref, slots_ref, up_ref, down_ref = refs[13 + 2 * parts :]
    rows = SEQ // parts
    e = pl.program_id(0)

    @pl.when(e == 0)
    def _():
        lane = lax.broadcasted_iota(jnp.int32, (rows, 128), 1)
        for k in range(parts):
            where = slice(k * rows, (k + 1) * rows)
            x = x_refs[k][...]
            x_ref[where, :] = x
            logits = jnp.where(lane < EXPERTS, dot(x, router[...], 1, 1), -1e30)
            probs = jnp.exp(logits - jnp.max(logits, axis=-1, keepdims=True))
            probs = probs / jnp.sum(probs, axis=-1, keepdims=True)
            target = target_col[where, :]
            hit = (target >= lane * CAP) & (target < lane * CAP + CAP)
            gate_ref[where, :] = jnp.sum(jnp.where(hit, probs, 0.0), axis=-1, keepdims=True)
            if k == 0:
                probs_ref[...] = probs

    choose(sel[0], up_own, up_other, up_ref)
    choose(sel[0], down_own, down_other, down_ref)
    expert_in = dispatch(e, target_row, x_ref)
    in_ref[0] = expert_in
    up = dot(expert_in, up_ref[...])
    inner = np.sqrt(2 / np.pi).astype(np.float32)
    square = up * up
    bend = jnp.tanh(inner * (up * (1.0 + 0.044715 * square)))
    half = 0.5 * (1.0 + bend)
    act = (up * half).astype(BF)
    act_ref[0] = act
    slope_ref[0] = half + 0.5 * up * (1.0 - bend * bend) * (
        inner * (1.0 + 3 * 0.044715 * square)
    )
    slots_ref[pl.ds(pl.multiple_of(e * CAP, CAP), CAP), :] = dot(act, down_ref[...]).astype(BF)

    @pl.when(e == EXPERTS - 1)
    def _():
        combine(parts, rows, target_col, slots_ref, out_refs)


def expert_specs(block):
    own = pl.BlockSpec(block, lambda e, sel: (e * (1 - sel[0]), 0, 0))
    other = pl.BlockSpec(block, lambda e, sel: (e * sel[0], 0, 0))
    return [own, other]


def whole(dims):
    return pl.BlockSpec(dims, lambda e, sel: (0,) * len(dims))


def fwd_experts(select, target_row, target_col, router, up_pair, down_pair, x_parts):
    parts = len(x_parts)
    rows = SEQ // parts
    hidden = up_pair[0].shape[2]
    each = pl.BlockSpec((1, CAP, D), lambda e, sel: (e, 0, 0))
    each_hidden = pl.BlockSpec((1, CAP, hidden), lambda e, sel: (e, 0, 0))
    outs = pl.pallas_call(
        functools.partial(fwd_experts_body, parts),
        grid_spec=pltpu.PrefetchScalarGridSpec(
            num_scalar_prefetch=1,
            grid=(EXPERTS,),
            in_specs=[whole((1, SEQ)), whole((SEQ, 1)), whole((128, D))]
            + expert_specs((1, D, hidden))
            + expert_specs((1, hidden, D))
            + [whole((rows, D))] * parts,
            out_specs=[each, each_hidden, each_hidden, whole((SEQ, 1)), whole((rows, 128))]
            + [whole((rows, D))] * parts,
            scratch_shapes=[
                pltpu.VMEM((SEQ, D), BF),
                pltpu.VMEM((SLOTS, D), BF),
                pltpu.VMEM((D, hidden), BF),
                pltpu.VMEM((hidden, D), BF),
            ],
        ),
        out_shape=[
            shape((EXPERTS, CAP, D), BF),
            shape((EXPERTS, CAP, hidden), BF),
            shape((EXPERTS, CAP, hidden), F32),
            shape((SEQ, 1), F32),
            shape((rows, 128), F32),
        ]
        + [shape((rows, D), BF)] * parts,
        compiler_params=pltpu.CompilerParams(vmem_limit_bytes=VMEM_LIMIT),
        cost_estimate=cost(1.2e10, 3e7),
        name="fwd_experts",
    )(select, target_row, target_col, router, *up_pair, *down_pair, *x_parts)
    return outs[:5], list(outs[5:])


def bwd_experts_body(parts, *refs):
    sel, target_row, target_col, gate, slope_ref, up_own, up_other, down_own, down_other = refs[:9]
    g_refs = refs[9 : 9 + parts]
    dout_ref, dup_ref = refs[9 + parts : 11 + parts]
    out_refs = refs[11 + parts : 11 + 2 * parts]
    g_ref, slots_ref, up_ref, down_ref = refs[11 + 2 * parts :]
    rows = SEQ // parts
    e = pl.program_id(0)

    @pl.when(e == 0)
    def _():
        for k in range(parts):
            where = slice(k * rows, (k + 1) * rows)
            g_ref[where, :] = (gate[where, :] * g_refs[k][...].astype(F32)).astype(BF)

    choose(sel[0], up_own, up_other, up_ref)
    choose(sel[0], down_own, down_other, down_ref)
    d_out = dispatch(e, target_row, g_ref)
    dout_ref[0] = d_out
    d_up = (slope_ref[0] * dot(d_out, down_ref[...], 1, 1)).astype(BF)
    dup_ref[0] = d_up
    slots_ref[pl.ds(pl.multiple_of(e * CAP, CAP), CAP), :] = dot(d_up, up_ref[...], 1, 1).astype(
        BF
    )

    @pl.when(e == EXPERTS - 1)
    def _():
        combine(parts, rows, target_col, slots_ref, out_refs)


def bwd_experts(select, target_row, target_col, gate, slope, up_pair, down_pair, g_parts):
    parts = len(g_parts)
    rows = SEQ // parts
    hidden = up_pair[0].shape[2]
    each = pl.BlockSpec((1, CAP, D), lambda e, sel: (e, 0, 0))
    each_hidden = pl.BlockSpec((1, CAP, hidden), lambda e, sel: (e, 0, 0))
    outs = pl.pallas_call(
        functools.partial(bwd_experts_body, parts),
        grid_spec=pltpu.PrefetchScalarGridSpec(
            num_scalar_prefetch=1,
            grid=(EXPERTS,),
            in_specs=[whole((1, SEQ)), whole((SEQ, 1)), whole((SEQ, 1)), each_hidden]
            + expert_specs((1, D, hidden))
            + expert_specs((1, hidden, D))
            + [whole((rows, D))] * parts,
            out_specs=[each, each_hidden] + [whole((rows, D))] * parts,
            scratch_shapes=[
                pltpu.VMEM((SEQ, D), BF),
                pltpu.VMEM((SLOTS, D), BF),
                pltpu.VMEM((D, hidden), BF),
                pltpu.VMEM((hidden, D), BF),
            ],
        ),
        out_shape=[shape((EXPERTS, CAP, D), BF), shape((EXPERTS, CAP, hidden), BF)]
        + [shape((rows, D), BF)] * parts,
        compiler_params=pltpu.CompilerParams(vmem_limit_bytes=VMEM_LIMIT),
        cost_estimate=cost(1.2e10, 3e7),
        name="bwd_experts",
    )(select, target_row, target_col, gate, slope, *up_pair, *down_pair, *g_parts)
    return outs[:2], list(outs[2:])


def norm(vector, gain):
    return vector * lax.rsqrt(jnp.mean(vector * vector, axis=-1, keepdims=True) + epsilon) * gain


def norm_back(vector, gain, grad):
    scale = lax.rsqrt(jnp.mean(vector * vector, axis=-1, keepdims=True) + epsilon)
    unit = vector * scale
    scaled = grad * gain
    inner = jnp.mean(unit * scaled, axis=-1, keepdims=True)
    return scale * (scaled - unit * inner), grad * unit


def total_of(value):
    return jnp.sum(jnp.sum(value, axis=0, keepdims=True), axis=1, keepdims=True)


def after_attention_body(parts, *refs):
    h_ref, gain, valid = refs[:3]
    p_refs, w_refs = refs[3 : 3 + parts], refs[3 + parts : 3 + 2 * parts]
    mid_ref, xn_ref, stat_ref = refs[3 + 2 * parts :]
    branch = dot(p_refs[0][...], w_refs[0][...], 0, 0)
    for k in range(1, parts):
        branch = branch + dot(p_refs[k][...], w_refs[k][...], 0, 0)
    h = h_ref[...].astype(F32)
    mid = h + branch
    mid_ref[...] = mid
    xn_ref[...] = norm(mid, gain[...]).astype(BF)
    weight = valid[...]
    lane = lax.broadcasted_iota(jnp.int32, (1, 128), 1)
    sums = jnp.where(lane == 0, total_of(weight * h * h), 0.0)
    sums = jnp.where(lane == 1, total_of(weight * branch * branch), sums)
    stat_ref[...] = jnp.where(lane == 3, total_of(weight), sums)


def after_attention(h, gain, valid, pieces, w_parts):
    parts = len(pieces)
    rows = h.shape[0]
    return pl.pallas_call(
        functools.partial(after_attention_body, parts),
        out_shape=[shape((rows, D), F32), shape((rows, D), BF), shape((1, 128), F32)],
        in_specs=vm(3 + 2 * parts),
        out_specs=vm(3),
        compiler_params=pltpu.CompilerParams(vmem_limit_bytes=VMEM_LIMIT),
        cost_estimate=cost(2e9, 4e6),
        name="after_attention",
    )(h, gain, valid, *pieces, *w_parts)


def after_experts_body(parts, *refs):
    mid_ref, gate, gain, valid = refs[:4]
    y_refs = refs[4 : 4 + parts]
    comb_ref, out_ref, xn_ref, stat_ref = refs[4 + parts :]
    total = y_refs[0][...].astype(F32)
    for k in range(1, parts):
        total = total + y_refs[k][...].astype(F32)
    combined = total.astype(BF)
    comb_ref[...] = combined
    branch = gate[...] * combined.astype(F32)
    out = (mid_ref[...] + branch).astype(BF)
    out_ref[...] = out
    xn_ref[...] = norm(out.astype(F32), gain[...]).astype(BF)
    lane = lax.broadcasted_iota(jnp.int32, (1, 128), 1)
    stat_ref[...] = jnp.where(lane == 2, total_of(valid[...] * branch * branch), 0.0)


def after_experts(mid, gate, gain, valid, y_parts):
    parts = len(y_parts)
    rows = mid.shape[0]
    return pl.pallas_call(
        functools.partial(after_experts_body, parts),
        out_shape=[shape((rows, D), BF)] * 3 + [shape((1, 128), F32)],
        in_specs=vm(4 + parts),
        out_specs=vm(4),
        compiler_params=pltpu.CompilerParams(vmem_limit_bytes=VMEM_LIMIT),
        cost_estimate=cost(1e8, 4e6),
        name="after_experts",
    )(mid, gate, gain, valid, *y_parts)


def middle_back_body(parts, *refs):
    g_ref, comb_ref, probs_ref, target_col, router, mid_ref, gain, xn_ref = refs[:8]
    y_refs, w_refs = refs[8 : 8 + parts], refs[8 + parts : 8 + 2 * parts]
    dmid_ref, da_ref, gain_ref, router_ref = refs[8 + 2 * parts : 12 + 2 * parts]
    out_refs = refs[12 + 2 * parts :]
    rows = g_ref.shape[0]
    g = g_ref[...].astype(F32)
    total = y_refs[0][...].astype(F32)
    for k in range(1, parts):
        total = total + y_refs[k][...].astype(F32)
    d_in = total.astype(BF).astype(F32)
    d_gate = jnp.sum(g * comb_ref[...].astype(F32), axis=-1, keepdims=True)
    lane = lax.broadcasted_iota(jnp.int32, (rows, 128), 1)
    target = target_col[...]
    hit = (target >= lane * CAP) & (target < lane * CAP + CAP)
    probs = probs_ref[...]
    chosen = jnp.where(hit, d_gate, 0.0)
    inner = jnp.sum(probs * chosen, axis=-1, keepdims=True)
    d_logits = (probs * (chosen - inner)).astype(BF)
    router_ref[...] = dot(d_logits, xn_ref[...], 0, 0)[:8]
    d_xn = d_in + dot(d_logits, router[...])
    d_norm, d_gain = norm_back(mid_ref[...], gain[...], d_xn)
    gain_ref[...] = jnp.sum(d_gain, axis=0, keepdims=True)
    d_mid = g + d_norm
    dmid_ref[...] = d_mid
    d_a = d_mid.astype(BF)
    da_ref[...] = d_a
    for k in list(range(1, parts)) + [0]:
        out_refs[k][...] = dot(d_a, w_refs[k][...], 1, 1).astype(BF)


def middle_back(g, combined, probs, target_col, router, mid, gain, xn, y_parts, w_parts):
    parts = len(y_parts)
    rows = g.shape[0]
    wide = w_parts[0].shape[0]
    outs = pl.pallas_call(
        functools.partial(middle_back_body, parts),
        out_shape=[shape((rows, D), F32), shape((rows, D), BF), shape((1, D), F32)]
        + [shape((8, D), F32)]
        + [shape((rows, wide), BF)] * parts,
        in_specs=vm(8 + 2 * parts),
        out_specs=vm(4 + parts),
        compiler_params=pltpu.CompilerParams(vmem_limit_bytes=VMEM_LIMIT),
        cost_estimate=cost(2e9, 6e6),
        name="middle_back",
    )(g, combined, probs, target_col, router, mid, gain, xn, *y_parts, *w_parts)
    return outs[:4], list(outs[4:])


def input_back_body(parts, *refs):
    dmid_ref, h_ref, gain = refs[:3]
    y_refs = refs[3 : 3 + parts]
    wide_ref, low_ref, gain_ref = refs[3 + parts :]
    total = y_refs[0][...].astype(F32)
    for k in range(1, parts):
        total = total + y_refs[k][...].astype(F32)
    d_norm, d_gain = norm_back(h_ref[...].astype(F32), gain[...], total)
    gain_ref[...] = jnp.sum(d_gain, axis=0, keepdims=True)
    d_h = dmid_ref[...] + d_norm
    wide_ref[...] = d_h
    low_ref[...] = d_h.astype(BF)


def input_back(d_mid, h, gain, y_parts):
    parts = len(y_parts)
    rows = h.shape[0]
    return pl.pallas_call(
        functools.partial(input_back_body, parts),
        out_shape=[shape((rows, D), F32), shape((rows, D), BF), shape((1, D), F32)],
        in_specs=vm(3 + parts),
        out_specs=vm(3),
        compiler_params=pltpu.CompilerParams(vmem_limit_bytes=VMEM_LIMIT),
        cost_estimate=cost(1e8, 4e6),
        name="input_back",
    )(d_mid, h, gain, *y_parts)


def scatter_sum(value, dim):
    count = lax.axis_size("dp")
    if count != 4:
        return lax.psum_scatter(value, "dp", scatter_dimension=dim, tiled=True).astype(F32)
    z = lax.axis_index("dp")
    size = value.shape[dim] // count
    half = size // 2

    def chunk(i, start, length):
        return lax.dynamic_slice_in_dim(value, ((z + i) % count) * size + start, length, dim)

    def send(x, step):
        return lax.ppermute(x, "dp", [(i, (i + step) % count) for i in range(count)])

    ahead = send(chunk(2, 0, half), 1)
    behind = send(chunk(2, half, half), -1)
    low = jnp.concatenate(
        [
            (chunk(1, 0, half).astype(F32) + ahead.astype(F32)).astype(BF),
            chunk(1, half, half),
        ],
        axis=dim,
    )
    high = jnp.concatenate(
        [
            chunk(3, 0, half),
            (chunk(3, half, half).astype(F32) + behind.astype(F32)).astype(BF),
        ],
        axis=dim,
    )
    return (
        chunk(0, 0, size).astype(F32) + send(low, 1).astype(F32) + send(high, -1).astype(F32)
    )


def sum_small(value, axis):
    count = lax.axis_size(axis)
    if count != 4:
        return lax.psum(value, axis)
    return (value + exchange(value, axis, 1)) + (
        exchange(value, axis, 2) + exchange(value, axis, 3)
    )


def local(
    inputs,
    norm_gains,
    attention_in,
    attention_out,
    bias_table,
    router_weight,
    up_weight,
    down_weight,
    routes,
    piece_starts,
    valid_mask,
    cotangent,
):
    s = lax.axis_index("section")
    t = lax.axis_index("tensor")
    z = lax.axis_index("dp")
    tensor = lax.axis_size("tensor")
    rows = inputs.shape[1]
    wide = attention_in.shape[3]
    heads = wide // HEAD_DIM
    first = s == 0

    def mine(array):
        return lax.dynamic_index_in_dim(array, s, 0, keepdims=False)

    def by_layer(own, other):
        return jnp.where(first, own, other), jnp.where(first, other, own)

    def swap(value):
        return exchange(value, "section", 1)

    h0 = mine(inputs)
    g1 = mine(cotangent)
    h0_parts = gather_parts(h0)

    def pack(route_row):
        table = jnp.pad(bias_table[0].reshape(1, -1), ((0, 0), (0, D - BUCKETS * heads)))
        route_rows = jnp.pad(route_row.astype(F32), (0, 2 * D - SEQ)).reshape(2, D)
        return jnp.concatenate(
            [norm_gains[0], router_weight[0].T.astype(F32), table, route_rows], axis=0
        )

    route_own = lax.dynamic_index_in_dim(routes[0], s, 0, keepdims=False)[:, 0]
    route_sent = lax.dynamic_index_in_dim(routes[0], 1 - s, 0, keepdims=False)[:, 0]
    smalls = by_layer(pack(route_own), swap(pack(route_sent)))
    w_in = by_layer(attention_in[0], swap(attention_in[0]))
    w_out = by_layer(attention_out[0], swap(attention_out[0]))
    up_pair = (up_weight[0], swap(up_weight[0]))
    down_pair = (down_weight[0], swap(down_weight[0]))
    w_out_parts = [gather_parts(w_out[0]), gather_parts(w_out[1])]

    valid = mine(valid_mask)
    valid_col = jnp.where(valid > 0, 0.0, masked_score).astype(F32)[:, None]
    valid_own = lax.dynamic_slice_in_dim(valid, t * rows, rows, 0).astype(F32)[:, None]
    starts = mine(piece_starts)
    info = jnp.concatenate([t[None], starts]).astype(jnp.int32)

    hot = diagonal_one_hot()
    tables = jnp.stack([sm[6, : BUCKETS * heads].reshape(BUCKETS, heads) for sm in smalls])
    tables = tables - tables[:, far_bucket_behind : far_bucket_behind + 1]
    bias_rows = jnp.einsum("dyb,lbh->lhdy", hot, tables, precision=lax.Precision.HIGHEST)
    bias = bias_tiles(bias_rows.reshape(2, heads * DIAGS, 2 * BAND))

    gains = [(sm[0:1], sm[1:2]) for sm in smalls]
    routers = [jnp.pad(sm[2:6], ((0, 124), (0, 0))).astype(BF) for sm in smalls]
    order = jnp.bitwise_xor(t, jnp.arange(tensor, dtype=jnp.int32))
    targets = []
    for sm in smalls:
        route = sm[7:9].reshape(-1)[:SEQ].astype(jnp.int32)
        hits = (route[:, None] == jnp.arange(EXPERTS, dtype=jnp.int32)[None, :]).astype(jnp.int32)
        slot = jnp.sum(hits * (jnp.cumsum(hits, axis=0) - 1), axis=1)
        target = (route * CAP + slot).reshape(tensor, rows)
        target = jnp.take(target, order, axis=0).reshape(SEQ)
        targets.append((target[None, :], target[:, None]))
    selects = [jnp.where(s == layer, 0, 1).astype(jnp.int32)[None] for layer in range(2)]

    hidden = [h0, None]
    x_parts = h0_parts
    saved = []
    outputs = []
    stats = []
    for layer in range(2):
        row, col = targets[layer]
        gain_in, gain_mid = gains[layer]
        kept, att_parts = fwd_attention(
            info, valid_col, gain_in, w_in[layer], bias[layer], x_parts, layer == 0
        )
        pieces = swap_parts(att_parts)
        mid, xn_mid, stat = after_attention(
            hidden[layer], gain_mid, valid_own, pieces, w_out_parts[layer]
        )
        ex, y_parts = fwd_experts(
            selects[layer],
            row,
            col,
            routers[layer],
            up_pair,
            down_pair,
            gather_parts(xn_mid),
        )
        gate = ex[3]
        combined, out, xn_next, stat_more = after_experts(
            mid, gate[:rows], gains[1][0], valid_own, swap_parts(y_parts)
        )
        outputs.append(out)
        stats.append(stat + stat_more)
        saved.append((kept, pieces, mid, xn_mid, ex, combined))
        if layer == 0:
            hidden[1] = out
            x_parts = gather_parts(xn_next)

    g = g1
    half = EXPERTS // 2
    grads = [None, None]
    for layer in (1, 0):
        row, col = targets[layer]
        gain_in, gain_mid = gains[layer]
        kept, pieces, mid, xn_mid, ex, combined = saved[layer]
        expert_in, act, slope, gate, probs = ex
        (d_out, d_up), y_parts = bwd_experts(
            selects[layer], row, col, gate, slope, up_pair, down_pair, gather_parts(g)
        )

        def weight_grad(left, right):
            def one(which):
                return jnp.einsum(
                    "eca,ecb->eab",
                    lax.dynamic_slice_in_dim(left, which * half, half, 0),
                    lax.dynamic_slice_in_dim(right, which * half, half, 0),
                    preferred_element_type=F32,
                )

            received = swap(one(1 - s).astype(BF))
            return scatter_sum((one(s) + received.astype(F32)).astype(BF), 1)

        grad_down = weight_grad(act, d_out)
        grad_up = weight_grad(expert_in, d_up)
        (d_mid, d_a, grad_gain_mid, grad_router), d_pieces = middle_back(
            g,
            combined,
            probs,
            col[:rows],
            routers[layer],
            mid,
            gain_mid,
            xn_mid,
            swap_parts(y_parts),
            w_out_parts[layer],
        )
        out_terms = swap_parts([dot(piece, d_a).astype(BF) for piece in pieces])
        grad_w_out = functools.reduce(jnp.add, [term.astype(F32) for term in out_terms])
        xn, qkv, turned, lse = kept
        (d_proj, diag, far), x_terms = bwd_attention(
            info, valid_col, w_in[layer], bias[layer], (qkv, turned, lse), swap_parts(d_pieces)
        )
        grad_w_in = jnp.einsum("sd,jsf->jdf", xn, d_proj, preferred_element_type=F32)
        grad_table = jnp.einsum(
            "dyb,hdy->bh",
            hot,
            diagonal_sums(diag).reshape(heads, DIAGS, 2 * BAND),
            precision=lax.Precision.HIGHEST,
        )
        grad_table = grad_table.at[far_bucket_behind].add(jnp.sum(far, axis=(1, 2)))
        d_h, d_h_low, grad_gain_in = input_back(
            d_mid, hidden[layer], gain_in, swap_parts(x_terms)
        )
        g = d_h_low
        small = jnp.concatenate(
            [
                grad_gain_in,
                grad_gain_mid,
                grad_router[:EXPERTS],
                jnp.pad(stats[layer], ((0, 0), (0, D - 128))),
                jnp.pad(grad_table.reshape(1, -1), ((0, 0), (0, D - BUCKETS * heads))),
            ],
            axis=0,
        )
        grads[layer] = (
            d_h,
            grad_down,
            grad_up,
            grad_w_in.astype(BF),
            grad_w_out.astype(BF),
            small,
        )

    def kept_sent(pair):
        return jnp.where(first, pair[0], pair[1]), jnp.where(first, pair[1], pair[0])

    def placed(own, received):
        return jnp.where(
            first,
            jnp.concatenate([own, received], axis=0),
            jnp.concatenate([received, own], axis=0),
        )

    keep, sent = kept_sent(outputs)
    layer_out = placed(keep[None], swap(sent)[None])
    keep, sent = kept_sent((grads[0][0], grads[1][0].astype(BF).astype(F32)))
    input_grad = placed(keep[None], swap(sent.astype(BF)).astype(F32)[None])
    expert_grads = []
    for which in (1, 2):
        keep, sent = kept_sent((grads[0][which], grads[1][which]))
        expert_grads.append(placed(keep, swap(sent.astype(BF)).astype(F32)))
    keep, sent = kept_sent((grads[0][3], grads[1][3]))
    grad_w_in = scatter_sum((keep.astype(F32) + swap(sent).astype(F32)).astype(BF), 1)
    keep, sent = kept_sent((grads[0][4], grads[1][4]))
    grad_w_out = scatter_sum((keep.astype(F32) + swap(sent).astype(F32)).astype(BF), 0)
    keep, sent = kept_sent((grads[0][5], grads[1][5]))
    small = keep + swap(sent)
    shared = sum_small(small[:7], "tensor")
    small = sum_small(jnp.concatenate([shared, small[7:]], axis=0), "dp")
    table = small[7, : BUCKETS * heads].reshape(BUCKETS, heads)
    share = BUCKETS // lax.axis_size("dp")
    stat = small[6]
    root_means = jnp.sqrt(stat[:3] / (stat[3] * D))
    return (
        layer_out[None],
        input_grad[None],
        small[None, 0:2],
        grad_w_in[None],
        grad_w_out[None],
        lax.dynamic_slice_in_dim(table, z * share, share, 0)[None],
        small[2:6].T[None],
        expert_grads[1][None],
        expert_grads[0][None],
        root_means[None],
    )


def solution(mesh):
    placed = (
        P("dp", "tensor", None),
        P("section", None, None),
        P("section", None, None, "tensor"),
        P("section", "tensor", None),
        P("section", None, "tensor"),
        P("section", None, None),
        P("section", None, None, "tensor"),
        P("section", None, "tensor", None),
        P("section", "dp", None, None),
        P("dp", None),
        P("dp", None),
        P("dp", "tensor", None),
    )
    return jax.shard_map(
        local,
        mesh=mesh,
        in_specs=placed,
        out_specs=(
            P("section", "dp", "tensor", None),
            P("section", "dp", "tensor", None),
            P("section", None, None),
            P("section", None, "dp", "tensor"),
            P("section", ("tensor", "dp"), None),
            P("section", "dp", "tensor"),
            P("section", None, None),
            P("section", None, "dp", "tensor"),
            P("section", None, ("tensor", "dp"), None),
            P("section", None),
        ),
        check_vma=False,
    )
```

```python
import functools

import jax
import jax.numpy as jnp
import numpy as np
from jax import lax
from jax.experimental import pallas as pl
from jax.experimental.pallas import tpu as pltpu
from jax.sharding import PartitionSpec as P

D = 768
HEAD_DIM = 64
BUCKETS = 32
EXPERTS = 4
CAP = 320
SEQ = 1024
PIECE = 256
PIECES = 2
SLOTS = EXPERTS * CAP

QB = PIECE
BAND = 128
WIDE = 2 * QB + BAND
DIAGS = 6

epsilon = 1e-06
bucket_edges = (12, 16, 23, 32, 46, 64, 91)
masked_score = -1000000000.0
far_bucket_behind = 15

BF = jnp.bfloat16
F32 = jnp.float32
MIB = 1024 * 1024


def dot(a, b, ca=1, cb=0):
    return lax.dot_general(a, b, (((ca,), (cb,)), ((), ())), preferred_element_type=F32)


def vm(count):
    return [pl.BlockSpec(memory_space=pltpu.VMEM)] * count


def smem():
    return pl.BlockSpec(memory_space=pltpu.SMEM)


def any_space(count):
    return [pl.BlockSpec(memory_space=pl.ANY)] * count


def limit(mib):
    return pltpu.CompilerParams(vmem_limit_bytes=mib * MIB)


def cost(flops, size):
    return pl.CostEstimate(flops=int(flops), bytes_accessed=int(size), transcendentals=0)


def shape(dims, kind):
    return jax.ShapeDtypeStruct(dims, kind)


def in_hbm(dims, kind):
    return pltpu.HBM(dims, kind)


def from_hbm(value):
    return pltpu.with_memory_space_constraint(value, pltpu.HBM)


def choose(select, own_ref, other_ref, to_ref):
    @pl.when(select == 0)
    def _():
        to_ref[...] = own_ref[...]

    @pl.when(select != 0)
    def _():
        to_ref[...] = other_ref[...]


def exchange(value, axis, mask):
    count = lax.axis_size(axis)
    return lax.ppermute(value, axis, [(i, i ^ mask) for i in range(count)])


def gather_parts(value):
    return [value] + [exchange(value, "tensor", k) for k in range(1, lax.axis_size("tensor"))]


def swap_parts(parts):
    return [parts[0]] + [exchange(p, "tensor", k) for k, p in enumerate(parts) if k]


def natural(t, k, size):
    return pl.ds(pl.multiple_of(jnp.bitwise_xor(t, k) * size, size), size)


def norm(vector, gain):
    return vector * lax.rsqrt(jnp.mean(vector * vector, axis=-1, keepdims=True) + epsilon) * gain


def total_of(value):
    return jnp.sum(jnp.sum(value, axis=0, keepdims=True), axis=1, keepdims=True)


def offset_buckets(offsets):
    distance = np.abs(offsets)
    far = np.full(offsets.shape, 8, np.int32)
    for edge_value in bucket_edges:
        far = far + (distance >= edge_value)
    return np.where(distance < 8, distance, far) + np.where(offsets > 0, 16, 0)


def diagonal_one_hot():
    lane = np.arange(2 * BAND)
    y = np.where(lane < BAND, lane, lane - 2 * BAND)
    offsets = BAND * (np.arange(DIAGS)[:, None] - 2) - y[None, :]
    hot = offset_buckets(offsets)[:, :, None] == np.arange(BUCKETS)
    hot = hot & (lane != BAND)[None, :, None]
    return hot.astype(np.float32)


def prepare_body(layer, place, own_gain, other_gain, own_table, other_table, hot, valid_ref, *refs):
    s = place[1]
    refs = refs[-5:] if layer == 0 else refs[-3:]
    gain_ref, tile_ref = refs[:2]
    heads = own_table.shape[0]
    own = s == layer
    gain_ref[...] = jnp.where(own, own_gain[...], other_gain[...])
    table = jnp.where(own, own_table[...], other_table[...])
    table = table - table[:, far_bucket_behind : far_bucket_behind + 1]
    by_offset = lax.dot_general(
        table,
        hot[...],
        (((1,), (0,)), ((), ())),
        precision=lax.Precision.HIGHEST,
        preferred_element_type=F32,
    )
    for h in range(heads):
        for d in range(DIAGS):
            row = by_offset[h : h + 1, d * 2 * BAND : (d + 1) * 2 * BAND]
            tile_ref[h * DIAGS + d] = pltpu.roll(
                jnp.broadcast_to(row, (BAND, 2 * BAND)), 0, 1, stride=1, stride_axis=0
            )[:, :BAND]
    if layer == 0:
        key_ref, own_ref, scratch = refs[2], refs[3], refs[4]
        rows = own_ref.shape[0]
        valid = jnp.where(s == 0, valid_ref[0:1, :], valid_ref[1:2, :]).astype(F32)
        column = jnp.broadcast_to(valid, (128, SEQ)).T[:, :1]
        scratch[...] = column
        key_ref[...] = jnp.where(column > 0, 0.0, masked_score)
        own_ref[...] = scratch[pl.ds(pl.multiple_of(place[0] * rows, rows), rows), :]


def prepare(layer, place, gains, tables, hot, valid, rows):
    outs = [shape((2, D), F32), shape((tables[0].shape[0] * DIAGS, BAND, BAND), F32)]
    if layer == 0:
        outs += [shape((SEQ, 1), F32), shape((rows, 1), F32)]
    return pl.pallas_call(
        functools.partial(prepare_body, layer),
        out_shape=outs,
        in_specs=[smem()] + vm(6),
        out_specs=vm(len(outs)),
        scratch_shapes=[pltpu.VMEM((SEQ, 1), F32)],
        compiler_params=limit(16),
        cost_estimate=cost(1e6, 1e5),
        name="prepare",
    )(place, *gains, *tables, hot, valid)


def targets_body(parts, place, own_route, other_route, own_router, other_router, *outs):
    row_refs, col_refs, router_refs, scratch = outs[:2], outs[2:4], outs[4:6], outs[6]
    t, s = place[0], place[1]
    rows = SEQ // parts
    before = lax.broadcasted_iota(jnp.int32, (SEQ, SEQ), 0)
    upto = (before <= lax.broadcasted_iota(jnp.int32, (SEQ, SEQ), 1)).astype(BF)
    expert = lax.broadcasted_iota(jnp.int32, (8, SEQ), 0)
    for layer in range(2):
        own = s == layer
        route = jnp.where(own, own_route[...], other_route[...])
        route = jnp.where(s == 0, route[0:1, :], route[1:2, :])
        hit = route == expert
        count = dot(hit.astype(BF), upto)
        slot = jnp.where(hit, count - 1.0 + (expert * CAP).astype(F32), 0.0)
        scratch[...] = jnp.sum(slot, axis=0, keepdims=True)
        for k in range(parts):
            row_refs[layer][:, k * rows : (k + 1) * rows] = scratch[:, natural(t, k, rows)].astype(
                jnp.int32
            )
        scratch[...] = row_refs[layer][...].astype(F32)
        turned = jnp.broadcast_to(scratch[...], (128, SEQ)).T
        col_refs[layer][...] = turned[:, :1].astype(jnp.int32)
        router_refs[layer][...] = jnp.zeros_like(router_refs[layer])
        router_refs[layer][:EXPERTS, :] = jnp.where(
            own, own_router[...].astype(F32), other_router[...].astype(F32)
        ).astype(BF)


def make_targets(place, routes, routers, parts):
    row, col = shape((1, SEQ), jnp.int32), shape((SEQ, 1), jnp.int32)
    router = shape((128, D), BF)
    return pl.pallas_call(
        functools.partial(targets_body, parts),
        out_shape=[row, row, col, col, router, router],
        in_specs=[smem()] + vm(4),
        out_specs=vm(6),
        scratch_shapes=[pltpu.VMEM((1, SEQ), F32)],
        compiler_params=limit(16),
        cost_estimate=cost(1e6, 1e5),
        name="make_targets",
    )(place, *routes, *routers)


def near_bias(tiles_ref, h, skip, width):
    first, last = skip // BAND, (skip + width) // BAND
    columns = [
        jnp.concatenate([tiles_ref[h * DIAGS + i - j + 1] for i in range(first, last)], axis=0)
        for j in range(QB // BAND)
    ]
    return jnp.concatenate(columns, axis=1)


def block_range(j):
    last = min(SEQ, QB * (j + 2))
    left = max(0, QB * j - BAND)
    return left, last, left - (QB * j - BAND)


def fill_mask(mask_ref, valid_ref, s0, s1, j):
    left, last, _ = block_range(j)
    width = last - left
    key = left + lax.broadcasted_iota(jnp.int32, (width, 1), 0)
    query = QB * j + lax.broadcasted_iota(jnp.int32, (1, QB), 1)

    def label(position, outside):
        second = jnp.where((position >= s1) & (position < s1 + PIECE), 1, outside)
        return jnp.where((position >= s0) & (position < s0 + PIECE), 0, second)

    allowed = (key <= query) | (label(key, -1) == label(query, -2))
    mask_ref[:width, :] = jnp.where(allowed, valid_ref[left:last, :], masked_score)


def fwd_attention_body(parts, norm_inside, *refs):
    place, starts, valid_col, gain, w_own, w_other, tiles_ref = refs[:7]
    x_refs = refs[7 : 7 + parts]
    xn_out, qkv_out, turned_out, lse_ref = refs[7 + parts : 11 + parts]
    out_refs = refs[11 + parts : 11 + 2 * parts]
    w_ref, xn_ref, qkv_ref, turned_ref, vt_ref, att_ref, mask_ref, valid_ref, sems = refs[
        11 + 2 * parts :
    ]
    t, s = place[0], place[1]
    s0, s1 = starts[s, 0], starts[s, 1]
    rows = SEQ // parts
    heads = qkv_ref.shape[1]
    wide = heads * HEAD_DIM

    choose(place[2], w_own, w_other, w_ref)
    valid_ref[...] = jnp.broadcast_to(valid_col[...], (SEQ, QB))
    for k in range(parts):
        where = natural(t, k, rows)
        x = x_refs[k][...]
        if norm_inside:
            x = norm(x.astype(F32), gain[0:1, :]).astype(BF)
        xn_ref[where, :] = x
        projected = dot(x, w_ref[...], 1, 1)
        for i in range(3):
            product = projected[:, i * wide : (i + 1) * wide]
            if i == 0:
                product = product * HEAD_DIM**-0.5
            turned = product.T.astype(BF)
            if i < 2:
                turned_ref[i, :, where] = turned
            else:
                vt_ref[:, where] = turned
            product = product.astype(BF)
            for h in range(heads):
                qkv_ref[i, h, where, :] = product[:, h * HEAD_DIM : (h + 1) * HEAD_DIM]

    copies = [
        pltpu.make_async_copy(a, b, sems.at[i])
        for i, (a, b) in enumerate(
            ((xn_ref, xn_out), (qkv_ref, qkv_out), (turned_ref, turned_out))
        )
    ]
    for copy in copies:
        copy.start()

    for j in range(SEQ // QB):
        left, last, skip = block_range(j)
        width = last - left
        columns = slice(j * QB, (j + 1) * QB)
        fill_mask(mask_ref, valid_ref, s0, s1, j)

        def one_head(h, carry):
            lanes = pl.ds(pl.multiple_of(h * HEAD_DIM, HEAD_DIM), HEAD_DIM)
            scores = dot(qkv_ref[1, h, :last, :], turned_ref[0, lanes, columns])
            near = scores[left:] + near_bias(tiles_ref, h, skip, width) + mask_ref[:width, :]
            highest = jnp.max(near, axis=0, keepdims=True)
            if left:
                far = scores[:left] + valid_ref[:left, :]
                highest = jnp.maximum(highest, jnp.max(far, axis=0, keepdims=True))
            near = jnp.exp(near - highest)
            total = jnp.sum(near, axis=0, keepdims=True)
            out = dot(vt_ref[lanes, left:last], near.astype(BF))
            if left:
                far = jnp.exp(far - highest)
                total = total + jnp.sum(far, axis=0, keepdims=True)
                out = out + dot(vt_ref[lanes, :left], far.astype(BF))
            lse_ref[h, :, columns] = highest + jnp.log(total)
            att_ref[lanes, columns] = (out * (1.0 / total)).astype(BF)
            return carry

        lax.fori_loop(0, heads, one_head, 0)

    for k in range(parts):
        out_refs[k][...] = att_ref[:, natural(t, k, rows)]
    for copy in copies:
        copy.wait()


def fwd_attention(place, starts, valid_col, gain, w_pair, tiles, x_parts, norm_inside):
    parts = len(x_parts)
    rows = SEQ // parts
    wide = w_pair[0].shape[0] // 3
    heads = wide // HEAD_DIM
    kept = [
        shape((SEQ, D), BF),
        shape((3, heads, SEQ, HEAD_DIM), BF),
        shape((2, wide, SEQ), BF),
    ]
    outs = pl.pallas_call(
        functools.partial(fwd_attention_body, parts, norm_inside),
        out_shape=[in_hbm(a.shape, a.dtype) for a in kept]
        + [shape((heads, 1, SEQ), F32)] + [shape((wide, rows), BF)] * parts,
        in_specs=[smem()] * 2 + vm(5 + parts),
        out_specs=any_space(3) + vm(1 + parts),
        scratch_shapes=[pltpu.VMEM((3 * wide, D), BF)]
        + [pltpu.VMEM(a.shape, a.dtype) for a in kept]
        + [
            pltpu.VMEM((wide, SEQ), BF),
            pltpu.VMEM((wide, SEQ), BF),
            pltpu.VMEM((WIDE, QB), F32),
            pltpu.VMEM((SEQ, QB), F32),
            pltpu.SemaphoreType.DMA((3,)),
        ],
        compiler_params=limit(32),
        cost_estimate=cost(9e9, 1e7),
        name="fwd_attention",
    )(place, starts, valid_col, gain, *w_pair, tiles, *x_parts)
    return outs[:4], list(outs[4:])


def bwd_attention_body(parts, *refs):
    place, starts, valid_col, gain, w_own, w_other, tiles_ref, xn_ref = refs[:8]
    qkv_ref, turned_ref, lse_ref = refs[8:11]
    d_refs = refs[11 : 11 + parts]
    refs = refs[11 + parts :]
    proj_ref, sum_ref, far_ref, gain_ref = refs[:4]
    out_refs = refs[4 : 4 + parts]
    w_ref, d_ref, dt_ref, dq_ref, dk_ref, dv_ref, mask_ref, valid_ref = refs[4 + parts :]
    t, s = place[0], place[1]
    s0, s1 = starts[s, 0], starts[s, 1]
    rows = SEQ // parts
    heads = qkv_ref.shape[1]

    choose(place[2], w_own, w_other, w_ref)
    valid_ref[...] = jnp.broadcast_to(valid_col[...], (SEQ, QB))
    for k in range(parts):
        where = natural(t, k, rows)
        block = d_refs[k][...]
        dt_ref[:, where] = block.astype(F32).T.astype(BF)
        for h in range(heads):
            d_ref[h, where, :] = block[:, h * HEAD_DIM : (h + 1) * HEAD_DIM]
    dk_ref[...] = jnp.zeros_like(dk_ref)
    dv_ref[...] = jnp.zeros_like(dv_ref)
    sum_ref[...] = jnp.zeros_like(sum_ref)
    far_ref[...] = jnp.zeros_like(far_ref)

    for j in range(SEQ // QB):
        left, last, skip = block_range(j)
        width = last - left
        columns = slice(j * QB, (j + 1) * QB)
        fill_mask(mask_ref, valid_ref, s0, s1, j)

        def one_head(h, carry):
            lanes = pl.ds(pl.multiple_of(h * HEAD_DIM, HEAD_DIM), HEAD_DIM)
            q_block = qkv_ref[0, h, columns, :]
            d_block = d_ref[h, columns, :]
            lse = lse_ref[h, :, columns]
            scores = dot(qkv_ref[1, h, :last, :], turned_ref[0, lanes, columns])
            slopes = dot(qkv_ref[2, h, :last, :], dt_ref[lanes, columns])
            near = scores[left:] + near_bias(tiles_ref, h, skip, width) + mask_ref[:width, :]
            near = jnp.exp(near - lse)
            near_slope = near * slopes[left:]
            row_dot = jnp.sum(near_slope, axis=0, keepdims=True)
            if left:
                far = jnp.exp(scores[:left] + valid_ref[:left, :] - lse)
                far_slope = far * slopes[:left]
                row_dot = row_dot + jnp.sum(far_slope, axis=0, keepdims=True)
            near_slope = near_slope - near * row_dot
            for i in range(width // BAND):
                for c in range(QB // BAND):
                    sum_ref[h * DIAGS + skip // BAND + i - c + 1] += near_slope[
                        i * BAND : (i + 1) * BAND, c * BAND : (c + 1) * BAND
                    ]
            near_slope = near_slope.astype(BF)
            dk_ref[h, left:last, :] += dot(near_slope, q_block)
            dv_ref[h, left:last, :] += dot(near.astype(BF), d_block)
            dq = dot(turned_ref[1, lanes, left:last], near_slope)
            if left:
                far_slope = far_slope - far * row_dot
                far_ref[h] += jnp.sum(far_slope.reshape(left // 8, 8, QB), axis=0)
                far_slope = far_slope.astype(BF)
                dk_ref[h, :left, :] += dot(far_slope, q_block)
                dv_ref[h, :left, :] += dot(far.astype(BF), d_block)
                dq = dq + dot(turned_ref[1, lanes, :left], far_slope)
            dq_ref[lanes, columns] = dq * HEAD_DIM**-0.5
            return carry

        lax.fori_loop(0, heads, one_head, 0)

    for first in range(0, SEQ, rows):
        where = slice(first, first + rows)
        blocks = [dq_ref[:, where].T.astype(BF)]
        for source in (dk_ref, dv_ref):
            blocks += [source[h, where, :].astype(BF) for h in range(heads)]
        proj_ref[where, :] = jnp.concatenate(blocks, axis=1)
    gain_sum = jnp.zeros((1, D), F32)
    for k in range(parts):
        where = natural(t, k, rows)
        total = dot(proj_ref[where, :], w_ref[...])
        out_refs[k][...] = total.astype(BF)
        gain_sum = gain_sum + jnp.sum(total * xn_ref[where, :].astype(F32), axis=0, keepdims=True)
    gain_ref[...] = gain_sum / gain[0:1, :]


def bwd_attention(place, starts, valid_col, gain, w_pair, tiles, saved, d_parts):
    parts = len(d_parts)
    rows = SEQ // parts
    wide = w_pair[0].shape[0] // 3
    heads = wide // HEAD_DIM
    outs = pl.pallas_call(
        functools.partial(bwd_attention_body, parts),
        out_shape=[
            shape((SEQ, 3 * wide), BF),
            shape((heads * DIAGS, BAND, BAND), F32),
            shape((heads, 8, QB), F32),
            shape((1, D), F32),
        ]
        + [shape((rows, D), BF)] * parts,
        in_specs=[smem()] * 2 + vm(9 + parts),
        out_specs=vm(4 + parts),
        scratch_shapes=[
            pltpu.VMEM((3 * wide, D), BF),
            pltpu.VMEM((heads, SEQ, HEAD_DIM), BF),
            pltpu.VMEM((wide, SEQ), BF),
            pltpu.VMEM((wide, SEQ), F32),
            pltpu.VMEM((heads, SEQ, HEAD_DIM), F32),
            pltpu.VMEM((heads, SEQ, HEAD_DIM), F32),
            pltpu.VMEM((WIDE, QB), F32),
            pltpu.VMEM((SEQ, QB), F32),
        ],
        compiler_params=limit(36),
        cost_estimate=cost(1.8e10, 1e7),
        name="bwd_attention",
    )(place, starts, valid_col, gain, *w_pair, tiles, *saved, *d_parts)
    return outs[:4], list(outs[4:])


def small_sums_body(paired, place, tiles_ref, far_ref, hot, gain_in, gain_mid, router, *refs):
    stats, refs = refs[:2], refs[2:]
    heads = far_ref.shape[0]
    row = lax.broadcasted_iota(jnp.int32, (BAND, BAND), 0)
    column = lax.broadcasted_iota(jnp.int32, (BAND, BAND), 1)
    flip = (row + column == BAND - 1).astype(F32)
    out = refs[-1]
    out[...] = jnp.zeros_like(out)
    out[0:1, :] = gain_in[...]
    out[1:2, :] = gain_mid[...]
    out[2 : 2 + EXPERTS, :] = router[:EXPERTS, :]
    out[6:7, :128] = stats[0][...] + stats[1][...]
    by_offset = []
    for h in range(heads):
        sums = []
        for d in range(DIAGS):
            tile = lax.dot_general(
                flip,
                tiles_ref[h * DIAGS + d],
                (((1,), (0,)), ((), ())),
                precision=lax.Precision.HIGHEST,
                preferred_element_type=F32,
            )
            tile = jnp.concatenate([tile, jnp.zeros_like(tile)], axis=1)
            tile = pltpu.roll(tile, BAND + 1, 1, stride=1, stride_axis=0)
            sums.append(jnp.sum(tile, axis=0, keepdims=True))
        by_offset.append(jnp.concatenate(sums, axis=1))
    table = lax.dot_general(
        jnp.concatenate(by_offset, axis=0),
        hot[...],
        (((1,), (1,)), ((), ())),
        precision=lax.Precision.HIGHEST,
        preferred_element_type=F32,
    )
    bucket = lax.broadcasted_iota(jnp.int32, (1, BUCKETS), 1)
    for h in range(heads):
        behind = jnp.where(bucket == far_bucket_behind, total_of(far_ref[h]), 0.0)
        out[8 + h : 9 + h, :BUCKETS] = table[h : h + 1, :] + behind
    if paired:
        other, keep, sent = refs[:3]
        first = place[1] == 0
        keep[...] = jnp.where(first, out[...], other[...])
        sent[...] = jnp.where(first, other[...], out[...])


def small_sums(place, tiles, far, hot, gain_in, gain_mid, router, stats, other):
    paired = other is not None
    array = shape((16, D), F32)
    outs = pl.pallas_call(
        functools.partial(small_sums_body, paired),
        out_shape=[array] * (2 if paired else 1),
        in_specs=[smem()] + vm(8 + paired),
        out_specs=vm(2 if paired else 1),
        scratch_shapes=[pltpu.VMEM((16, D), F32)] if paired else [],
        compiler_params=limit(16),
        cost_estimate=cost(1e6, 1e5),
        name="small_sums",
    )(place, tiles, far, hot, gain_in, gain_mid, router, *stats, *([other] if paired else []))
    return outs if paired else outs[0]


def combine(parts, rows, target_col, slots_ref, out_refs):
    slot = lax.broadcasted_iota(jnp.int32, (rows, SLOTS), 1)
    for k in list(range(1, parts)) + [0]:
        hot = (target_col[k * rows : (k + 1) * rows, :] == slot).astype(BF)
        out_refs[k][...] = dot(hot, slots_ref[...]).astype(BF)


def dispatch(e, target_row, tokens_ref):
    slot = e * CAP + lax.broadcasted_iota(jnp.int32, (CAP, SEQ), 0)
    return dot((target_row[...] == slot).astype(BF), tokens_ref[...]).astype(BF)


def fwd_experts_body(parts, *refs):
    sel, target_row, target_col, router, up_own, up_other, down_own, down_other = refs[:8]
    x_refs = refs[8 : 8 + parts]
    in_ref, act_ref, slope_ref, gate_ref, probs_ref = refs[8 + parts : 13 + parts]
    out_refs = refs[13 + parts : 13 + 2 * parts]
    x_ref, slots_ref, up_ref, down_ref = refs[13 + 2 * parts :]
    rows = SEQ // parts
    e = pl.program_id(0)

    @pl.when(e == 0)
    def _():
        lane = lax.broadcasted_iota(jnp.int32, (rows, 128), 1)
        for k in range(parts):
            where = slice(k * rows, (k + 1) * rows)
            x = x_refs[k][...]
            x_ref[where, :] = x
            logits = jnp.where(lane < EXPERTS, dot(x, router[...], 1, 1), -1e30)
            probs = jnp.exp(logits - jnp.max(logits, axis=-1, keepdims=True))
            probs = probs / jnp.sum(probs, axis=-1, keepdims=True)
            target = target_col[where, :]
            hit = (target >= lane * CAP) & (target < lane * CAP + CAP)
            gate_ref[where, :] = jnp.sum(jnp.where(hit, probs, 0.0), axis=-1, keepdims=True)
            if k == 0:
                probs_ref[...] = probs

    choose(sel[0], up_own.at[0], up_other.at[0], up_ref)
    choose(sel[0], down_own.at[0], down_other.at[0], down_ref)
    expert_in = dispatch(e, target_row, x_ref)
    in_ref[0] = expert_in
    up = dot(expert_in, up_ref[...])
    inner = np.sqrt(2 / np.pi).astype(np.float32)
    square = up * up
    bend = jnp.tanh(inner * (up * (1.0 + 0.044715 * square)))
    half = 0.5 * (1.0 + bend)
    act = (up * half).astype(BF)
    act_ref[0] = act
    slope_ref[0] = half + 0.5 * up * (1.0 - bend * bend) * (
        inner * (1.0 + 3 * 0.044715 * square)
    )
    slots_ref[pl.ds(pl.multiple_of(e * CAP, CAP), CAP), :] = dot(act, down_ref[...]).astype(BF)

    @pl.when(e == EXPERTS - 1)
    def _():
        combine(parts, rows, target_col, slots_ref, out_refs)


def expert_specs(block):
    own = pl.BlockSpec(block, lambda e, sel: (e * (1 - sel[0]), 0, 0))
    other = pl.BlockSpec(block, lambda e, sel: (e * sel[0], 0, 0))
    return [own, other]


def whole(dims):
    return pl.BlockSpec(dims, lambda e, sel: (0,) * len(dims))


def fwd_experts(select, target_row, target_col, router, up_pair, down_pair, x_parts):
    parts = len(x_parts)
    rows = SEQ // parts
    hidden = up_pair[0].shape[2]
    each = pl.BlockSpec((1, CAP, D), lambda e, sel: (e, 0, 0))
    each_hidden = pl.BlockSpec((1, CAP, hidden), lambda e, sel: (e, 0, 0))
    outs = pl.pallas_call(
        functools.partial(fwd_experts_body, parts),
        grid_spec=pltpu.PrefetchScalarGridSpec(
            num_scalar_prefetch=1,
            grid=(EXPERTS,),
            in_specs=[whole((1, SEQ)), whole((SEQ, 1)), whole((128, D))]
            + expert_specs((1, D, hidden))
            + expert_specs((1, hidden, D))
            + [whole((rows, D))] * parts,
            out_specs=[each, each_hidden, each_hidden, whole((SEQ, 1)), whole((rows, 128))]
            + [whole((rows, D))] * parts,
            scratch_shapes=[
                pltpu.VMEM((SEQ, D), BF),
                pltpu.VMEM((SLOTS, D), BF),
                pltpu.VMEM((D, hidden), BF),
                pltpu.VMEM((hidden, D), BF),
            ],
        ),
        out_shape=[
            in_hbm((EXPERTS, CAP, D), BF),
            in_hbm((EXPERTS, CAP, hidden), BF),
            in_hbm((EXPERTS, CAP, hidden), F32),
            shape((SEQ, 1), F32),
            shape((rows, 128), F32),
        ]
        + [shape((rows, D), BF)] * parts,
        compiler_params=limit(44),
        cost_estimate=cost(1.2e10, 3e7),
        name="fwd_experts",
    )(
        select,
        target_row,
        target_col,
        router,
        *[from_hbm(a) for a in (*up_pair, *down_pair)],
        *x_parts,
    )
    return outs[:5], list(outs[5:])


def bwd_experts_body(parts, *refs):
    sel, target_row, target_col, gate, slope_ref, up_own, up_other, down_own, down_other = refs[:9]
    g_refs = refs[9 : 9 + parts]
    refs = refs[9 + parts :]
    dout_ref, dup_ref = refs[:2]
    out_refs = refs[2 : 2 + parts]
    g_ref, slots_ref, up_ref, down_ref = refs[2 + parts :]
    rows = SEQ // parts
    e = pl.program_id(0)

    @pl.when(e == 0)
    def _():
        for k in range(parts):
            where = slice(k * rows, (k + 1) * rows)
            g_ref[where, :] = (gate[where, :] * g_refs[k][...].astype(F32)).astype(BF)

    choose(sel[0], up_own.at[0], up_other.at[0], up_ref)
    choose(sel[0], down_own.at[0], down_other.at[0], down_ref)
    d_out = dispatch(e, target_row, g_ref)
    dout_ref[0] = d_out
    d_up = (slope_ref[0] * dot(d_out, down_ref[...], 1, 1)).astype(BF)
    dup_ref[0] = d_up
    slots_ref[pl.ds(pl.multiple_of(e * CAP, CAP), CAP), :] = dot(d_up, up_ref[...], 1, 1).astype(
        BF
    )

    @pl.when(e == EXPERTS - 1)
    def _():
        combine(parts, rows, target_col, slots_ref, out_refs)


def bwd_experts(select, target_row, target_col, gate, slope, up_pair, down_pair, g_parts):
    parts = len(g_parts)
    rows = SEQ // parts
    hidden = up_pair[0].shape[2]
    each = pl.BlockSpec((1, CAP, D), lambda e, sel: (e, 0, 0))
    each_hidden = pl.BlockSpec((1, CAP, hidden), lambda e, sel: (e, 0, 0))
    outs = pl.pallas_call(
        functools.partial(bwd_experts_body, parts),
        grid_spec=pltpu.PrefetchScalarGridSpec(
            num_scalar_prefetch=1,
            grid=(EXPERTS,),
            in_specs=[whole((1, SEQ)), whole((SEQ, 1)), whole((SEQ, 1)), each_hidden]
            + expert_specs((1, D, hidden))
            + expert_specs((1, hidden, D))
            + [whole((rows, D))] * parts,
            out_specs=[each, each_hidden] + [whole((rows, D))] * parts,
            scratch_shapes=[
                pltpu.VMEM((SEQ, D), BF),
                pltpu.VMEM((SLOTS, D), BF),
                pltpu.VMEM((D, hidden), BF),
                pltpu.VMEM((hidden, D), BF),
            ],
        ),
        out_shape=[in_hbm((EXPERTS, CAP, D), BF), in_hbm((EXPERTS, CAP, hidden), BF)]
        + [shape((rows, D), BF)] * parts,
        compiler_params=limit(44),
        cost_estimate=cost(1.2e10, 3e7),
        name="bwd_experts",
    )(
        select,
        target_row,
        target_col,
        gate,
        *[from_hbm(a) for a in (slope, *up_pair, *down_pair)],
        *g_parts,
    )
    return outs[:2], list(outs[2:])


def norm_back(vector, gain, grad):
    scale = lax.rsqrt(jnp.mean(vector * vector, axis=-1, keepdims=True) + epsilon)
    unit = vector * scale
    scaled = grad * gain
    inner = jnp.mean(unit * scaled, axis=-1, keepdims=True)
    return scale * (scaled - unit * inner), grad * unit


def after_attention_body(parts, *refs):
    h_ref, gain, valid = refs[:3]
    p_refs, w_refs = refs[3 : 3 + parts], refs[3 + parts : 3 + 2 * parts]
    mid_ref, xn_ref, stat_ref = refs[3 + 2 * parts :]
    branch = dot(p_refs[0][...], w_refs[0][...], 0, 0)
    for k in range(1, parts):
        branch = branch + dot(p_refs[k][...], w_refs[k][...], 0, 0)
    h = h_ref[...].astype(F32)
    mid = h + branch
    mid_ref[...] = mid
    xn_ref[...] = norm(mid, gain[1:2, :]).astype(BF)
    weight = valid[...]
    lane = lax.broadcasted_iota(jnp.int32, (1, 128), 1)
    sums = jnp.where(lane == 0, total_of(weight * h * h), 0.0)
    sums = jnp.where(lane == 1, total_of(weight * branch * branch), sums)
    stat_ref[...] = jnp.where(lane == 3, total_of(weight), sums)


def after_attention(h, gain, valid, pieces, w_parts):
    parts = len(pieces)
    rows = h.shape[0]
    return pl.pallas_call(
        functools.partial(after_attention_body, parts),
        out_shape=[shape((rows, D), F32), shape((rows, D), BF), shape((1, 128), F32)],
        in_specs=vm(3 + 2 * parts),
        out_specs=vm(3),
        compiler_params=limit(24),
        cost_estimate=cost(2e9, 4e6),
        name="after_attention",
    )(h, gain, valid, *pieces, *w_parts)


def after_experts_body(parts, *refs):
    mid_ref, gate, gain, valid = refs[:4]
    y_refs = refs[4 : 4 + parts]
    comb_ref, out_ref, xn_ref, stat_ref = refs[4 + parts :]
    total = y_refs[0][...].astype(F32)
    for k in range(1, parts):
        total = total + y_refs[k][...].astype(F32)
    combined = total.astype(BF)
    comb_ref[...] = combined
    branch = gate[: mid_ref.shape[0], :] * combined.astype(F32)
    out = (mid_ref[...] + branch).astype(BF)
    out_ref[...] = out
    xn_ref[...] = norm(out.astype(F32), gain[0:1, :]).astype(BF)
    lane = lax.broadcasted_iota(jnp.int32, (1, 128), 1)
    stat_ref[...] = jnp.where(lane == 2, total_of(valid[...] * branch * branch), 0.0)


def after_experts(mid, gate, gain, valid, y_parts):
    parts = len(y_parts)
    rows = mid.shape[0]
    return pl.pallas_call(
        functools.partial(after_experts_body, parts),
        out_shape=[shape((rows, D), BF)] * 3 + [shape((1, 128), F32)],
        in_specs=vm(4 + parts),
        out_specs=vm(4),
        compiler_params=limit(24),
        cost_estimate=cost(1e8, 4e6),
        name="after_experts",
    )(mid, gate, gain, valid, *y_parts)


def middle_back_body(parts, *refs):
    g_ref, comb_ref, probs_ref, target_col, router, mid_ref, gain, xn_ref = refs[:8]
    y_refs, w_refs = refs[8 : 8 + parts], refs[8 + parts : 8 + 2 * parts]
    refs = refs[8 + 2 * parts :]
    dmid_ref, da_ref, gain_ref, router_ref = refs[:4]
    out_refs = refs[4:]
    rows = g_ref.shape[0]
    g = g_ref[...].astype(F32)
    total = y_refs[0][...].astype(F32)
    for k in range(1, parts):
        total = total + y_refs[k][...].astype(F32)
    d_in = total.astype(BF).astype(F32)
    d_gate = jnp.sum(g * comb_ref[...].astype(F32), axis=-1, keepdims=True)
    lane = lax.broadcasted_iota(jnp.int32, (rows, 128), 1)
    target = target_col[:rows, :]
    hit = (target >= lane * CAP) & (target < lane * CAP + CAP)
    probs = probs_ref[...]
    chosen = jnp.where(hit, d_gate, 0.0)
    inner = jnp.sum(probs * chosen, axis=-1, keepdims=True)
    d_logits = (probs * (chosen - inner)).astype(BF)
    router_ref[...] = dot(d_logits, xn_ref[...], 0, 0)[:8]
    d_xn = d_in + dot(d_logits, router[...])
    d_norm, d_gain = norm_back(mid_ref[...], gain[1:2, :], d_xn)
    gain_ref[...] = jnp.sum(d_gain, axis=0, keepdims=True)
    d_mid = g + d_norm
    dmid_ref[...] = d_mid
    d_a = d_mid.astype(BF)
    da_ref[...] = d_a
    for k in list(range(1, parts)) + [0]:
        out_refs[k][...] = dot(d_a, w_refs[k][...], 1, 1).astype(BF)


def middle_back(g, combined, probs, target_col, router, mid, gain, xn, y_parts, w_parts):
    parts = len(y_parts)
    rows = g.shape[0]
    wide = w_parts[0].shape[0]
    outs = pl.pallas_call(
        functools.partial(middle_back_body, parts),
        out_shape=[shape((rows, D), F32), shape((rows, D), BF), shape((1, D), F32)]
        + [shape((8, D), F32)]
        + [shape((rows, wide), BF)] * parts,
        in_specs=vm(8 + 2 * parts),
        out_specs=vm(4 + parts),
        compiler_params=limit(24),
        cost_estimate=cost(2e9, 6e6),
        name="middle_back",
    )(g, combined, probs, target_col, router, mid, gain, xn, *y_parts, *w_parts)
    return outs[:4], list(outs[4:])


def input_back_body(parts, *refs):
    dmid_ref, h_ref, gain = refs[:3]
    y_refs = refs[3 : 3 + parts]
    wide_ref, low_ref = refs[3 + parts :]
    total = y_refs[0][...].astype(F32)
    for k in range(1, parts):
        total = total + y_refs[k][...].astype(F32)
    d_h = dmid_ref[...] + norm_back(h_ref[...].astype(F32), gain[0:1, :], total)[0]
    wide_ref[...] = d_h
    low_ref[...] = d_h.astype(BF)


def input_back(d_mid, h, gain, y_parts):
    parts = len(y_parts)
    rows = h.shape[0]
    return pl.pallas_call(
        functools.partial(input_back_body, parts),
        out_shape=[shape((rows, D), F32), shape((rows, D), BF)],
        in_specs=vm(3 + parts),
        out_specs=vm(2),
        compiler_params=limit(24),
        cost_estimate=cost(1e8, 4e6),
        name="input_back",
    )(d_mid, h, gain, *y_parts)


def expert_grads_body(order, act, d_out, expert_in, d_up, send_ref, keep_ref):
    del order
    for place, out in enumerate((send_ref, keep_ref)):

        @pl.when(pl.program_id(0) // (EXPERTS // 2) == place)
        def _():
            out[0, 0] = dot(act[0], d_out[0], 0, 0).astype(BF)
            out[1, 0] = dot(expert_in[0], d_up[0], 0, 0).astype(BF)


def expert_grads(order, act, d_out, expert_in, d_up):
    half = EXPERTS // 2
    hidden = act.shape[2]
    values = (act, d_out, expert_in, d_up)
    block = (2, 1, hidden, D)
    outs = pl.pallas_call(
        expert_grads_body,
        grid_spec=pltpu.PrefetchScalarGridSpec(
            num_scalar_prefetch=1,
            grid=(EXPERTS,),
            in_specs=[
                pl.BlockSpec((1,) + a.shape[1:], lambda e, order: (order[e], 0, 0)) for a in values
            ],
            out_specs=[
                pl.BlockSpec(block, lambda e, order: (0, jnp.minimum(e, half - 1), 0, 0)),
                pl.BlockSpec(block, lambda e, order: (0, jnp.maximum(e - half, 0), 0, 0)),
            ],
        ),
        out_shape=[in_hbm((2, half, hidden, D), BF)] * 2,
        compiler_params=limit(28),
        cost_estimate=cost(1e6, 1e5),
        name="expert_grads",
    )(order, *[from_hbm(a) for a in values])
    return [a.reshape(2 * half, hidden, D) for a in outs]


def out_grads_body(parts, *refs):
    pieces, d_a, outs = refs[:parts], refs[parts], refs[parts + 1 :]
    for k in list(range(1, parts)) + [0]:
        outs[k][...] = dot(pieces[k][...], d_a[...]).astype(BF)


def out_grads(pieces, d_a):
    parts = len(pieces)
    wide = pieces[0].shape[0]
    return pl.pallas_call(
        functools.partial(out_grads_body, parts),
        out_shape=[shape((wide, D), BF)] * parts,
        in_specs=vm(parts + 1),
        out_specs=vm(parts),
        compiler_params=limit(16),
        cost_estimate=cost(1e6, 1e5),
        name="out_grads",
    )(*pieces, d_a)


def attention_grads_body(parts, chunks, paired, place, xn_ref, proj_ref, *refs):
    terms, refs = refs[:parts], refs[parts:]
    out = refs[-1]
    wide = terms[0].shape[0]
    rows, taken = D // chunks, wide // chunks
    out[0, :, : 3 * wide] = dot(xn_ref[...], proj_ref[...], 0, 0).astype(out.dtype)
    total = terms[0][...].astype(F32)
    for k in range(1, parts):
        total = total + terms[k][...].astype(F32)
    for c in range(chunks):
        for b in range(D // wide):
            out[0, c * rows + b * taken : c * rows + (b + 1) * taken, 3 * wide :] = total[
                c * taken : (c + 1) * taken, b * wide : (b + 1) * wide
            ].astype(out.dtype)
    if paired:
        other, keep, sent = refs[:3]
        first = place[1] == 0
        keep[...] = jnp.where(first, out[...].astype(F32), other[...].astype(F32)).astype(BF)
        sent[...] = jnp.where(first, other[...].astype(F32), out[...].astype(F32)).astype(BF)


def attention_grads(place, xn, proj, terms, other):
    parts = len(terms)
    paired = other is not None
    array = shape((1, D, D), BF)
    outs = pl.pallas_call(
        functools.partial(attention_grads_body, parts, lax.axis_size("dp"), paired),
        out_shape=[array] * (2 if paired else 1),
        in_specs=[smem()] + vm(2 + parts + paired),
        out_specs=vm(2 if paired else 1),
        scratch_shapes=[pltpu.VMEM((1, D, D), F32)] if paired else [],
        compiler_params=limit(24),
        cost_estimate=cost(1e6, 1e5),
        name="attention_grads",
    )(place, xn, proj, *terms, *([other] if paired else []))
    return outs if paired else outs[0]


def attention_results(value, wide):
    rows = value.shape[0]
    taken = rows // (D // wide)
    return (
        jnp.stack([value[:, i * wide : (i + 1) * wide] for i in range(3)]),
        jnp.concatenate(
            [value[b * taken : (b + 1) * taken, 3 * wide :] for b in range(D // wide)], axis=1
        ),
    )


def shift(value, step):
    count = lax.axis_size("dp")
    return lax.ppermute(value, "dp", [(i, (i + step) % count) for i in range(count)])


def ring_call(body, name, at, groups, inputs, outputs):
    step = 2 if groups % 2 == 0 else 1
    in_specs = []
    for a, lead, entry in inputs:
        size = a.shape[1] if entry is None else a.shape[1] // 4
        in_specs.append(
            pl.BlockSpec(
                (step, size, a.shape[2]),
                lambda i, at, lead=lead, entry=entry: (
                    i + lead // step,
                    0 if entry is None else at[entry],
                    0,
                ),
            )
        )
    columns = inputs[0][0].shape[2]
    return pl.pallas_call(
        body,
        grid_spec=pltpu.PrefetchScalarGridSpec(
            num_scalar_prefetch=1,
            grid=(groups // step,),
            in_specs=in_specs,
            out_specs=[
                pl.BlockSpec((step, rows, columns), lambda i, at: (i, 0, 0)) for rows, _ in outputs
            ],
        ),
        out_shape=[shape((groups, rows, columns), kind) for rows, kind in outputs],
        compiler_params=limit(24),
        cost_estimate=cost(1e6, 1e5),
        name=name,
    )(at, *[a for a, _, _ in inputs])


def added(*refs):
    return functools.reduce(jnp.add, [r[...].astype(F32) for r in refs])


def ring_first_body(at, a, b, low, high):
    total = added(a, b).astype(BF)
    half = low.shape[1]
    low[...] = total[:, :half]
    high[...] = total[:, half:]


def ring_first(at, terms):
    if lax.axis_size("dp") != 4:
        return []
    size = terms[0].shape[1] // 4
    inputs = [(a, 0, 0) for a in terms]
    return ring_call(
        ring_first_body, "ring_first", at, terms[0].shape[0], inputs, [(size // 2, BF)] * 2
    )


def ring_second_body(at, a, b, c, d, ahead, behind, low, high):
    half = ahead.shape[1]
    total = added(a, b)
    low[:, :half] = (total[:, :half] + ahead[...].astype(F32)).astype(BF)
    low[:, half:] = total[:, half:].astype(BF)
    total = added(c, d)
    high[:, :half] = total[:, :half].astype(BF)
    high[:, half:] = (total[:, half:] + behind[...].astype(F32)).astype(BF)


def ring_second(at, terms, arrived, lead, groups):
    if not arrived:
        return []
    size = terms[0].shape[1] // 4
    inputs = [(a, lead, entry) for entry in (1, 2) for a in terms]
    inputs += [(a, lead, None) for a in arrived]
    return ring_call(ring_second_body, "ring_second", at, groups, inputs, [(size, BF)] * 2)


def ring_move(sent):
    return [shift(a, step) for a, step in zip(sent, (1, -1))]


def scattered(terms, lead, groups):
    total = functools.reduce(jnp.add, [a[lead : lead + groups].astype(F32) for a in terms])
    return lax.psum_scatter(total.astype(BF), "dp", scatter_dimension=1, tiled=True).astype(F32)


def ring_end_body(at, a, b, c, d, out):
    out[...] = added(a, b, c, d)


def ring_end(at, terms, arrived):
    groups = terms[0].shape[0]
    if not arrived:
        return scattered(terms, 0, groups)
    inputs = [(a, 0, 3) for a in terms] + [(a, 0, None) for a in arrived]
    return ring_call(
        ring_end_body, "ring_end", at, groups, inputs, [(terms[0].shape[1] // 4, F32)]
    )[0]


def ring_ends_body(at, *refs):
    keep, sent = refs[8:]
    sums = [added(*refs[:4]), added(*refs[4:8])]
    first = at[4] == 0
    keep[...] = jnp.where(first, sums[0], sums[1])
    sent[...] = jnp.where(first, sums[1], sums[0]).astype(BF)


def ring_ends(at, terms, arrived, lead, groups):
    if not arrived[0]:
        sums = [scattered(a, lead, groups) for a in terms]
        first = at[4] == 0
        return (
            jnp.where(first, sums[0], sums[1]),
            jnp.where(first, sums[1], sums[0]).astype(BF),
        )
    inputs = []
    for layer in range(2):
        inputs += [(a, lead, 3) for a in terms[layer]] + [(a, 0, None) for a in arrived[layer]]
    size = terms[0][0].shape[1] // 4
    return ring_call(ring_ends_body, "ring_ends", at, groups, inputs, [(size, F32), (size, BF)])


def phase(*values):
    return lax.optimization_barrier(values)


def sum_small(value, axis):
    count = lax.axis_size(axis)
    if count != 4:
        return lax.psum(value, axis)
    return (value + exchange(value, axis, 1)) + (
        exchange(value, axis, 2) + exchange(value, axis, 3)
    )


def local(
    inputs,
    norm_gains,
    attention_in,
    attention_out,
    bias_table,
    router_weight,
    up_weight,
    down_weight,
    routes,
    piece_starts,
    valid_mask,
    cotangent,
):
    s = lax.axis_index("section")
    t = lax.axis_index("tensor")
    z = lax.axis_index("dp")
    tensor = lax.axis_size("tensor")
    rows = inputs.shape[1]
    wide = attention_in.shape[3]
    heads = wide // HEAD_DIM
    first = s == 0

    def mine(array):
        return lax.dynamic_index_in_dim(array, s, 0, keepdims=False)

    def by_layer(own, other):
        return jnp.where(first, own, other), jnp.where(first, other, own)

    def swap(value):
        return jax.tree.map(lambda a: exchange(a, "section", 1), value)

    def pair(value):
        return value, swap(value)

    h0 = mine(inputs)
    g1 = mine(cotangent)
    place = [
        jnp.stack([t, s, jnp.where(s == layer, 0, 1)]).astype(jnp.int32) for layer in range(2)
    ]
    selects = [place[layer][2:] for layer in range(2)]
    dp_size = lax.axis_size("dp")
    at = jnp.stack([(z + i) % dp_size for i in (2, 1, 3, 0)] + [s]).astype(jnp.int32)
    order = jnp.where(first, jnp.array([2, 3, 0, 1]), jnp.array([0, 1, 2, 3])).astype(jnp.int32)
    hot = diagonal_one_hot()
    hot_rows = hot.transpose(2, 0, 1).reshape(BUCKETS, -1)

    gain_pair, table_pair = pair(norm_gains[0]), pair(bias_table[0].T)
    w_out_pair = pair(attention_out[0])

    def prepared(layer):
        return prepare(layer, place[layer], gain_pair, table_pair, hot_rows, valid_mask, rows)

    x_parts, first_prepared, gain_pair, table_pair, w_in_pair, w_out, route_pair, router_pair, up, down = phase(
        gather_parts(h0),
        prepared(0),
        gain_pair,
        table_pair,
        pair(jnp.swapaxes(attention_in[0], 1, 2).reshape(3 * wide, D)),
        by_layer(*w_out_pair),
        pair(routes[0, :, :, 0]),
        pair(router_weight[0].T),
        up_weight[0],
        down_weight[0],
    )

    gain, tile, valid_col, valid_own = first_prepared
    gains, tiles = [gain], [tile]
    hidden = [h0, None]
    saved, outputs, stats, w_out_parts = [], [], [], []
    for layer in range(2):
        kept, att_parts = fwd_attention(
            place[layer],
            piece_starts,
            valid_col,
            gains[layer],
            w_in_pair,
            tiles[layer],
            x_parts,
            layer == 0,
        )
        if layer == 0:
            w_out_parts.append(gather_parts(w_out[0]))
            up_pair, down_pair = pair(up), pair(down)
            att_parts, w_out_parts[0] = phase(att_parts, w_out_parts[0])
        else:
            g_parts = [g1] + [exchange(g1, "tensor", k) for k in range(1, tensor - 1)]
            att_parts, g_parts = phase(att_parts, g_parts)
        pieces = swap_parts(att_parts)
        mid, xn_mid, stat = after_attention(
            hidden[layer], gains[layer], valid_own, pieces, w_out_parts[layer]
        )
        if layer == 0:
            xn_mid, route_pair, router_pair, gain_pair, table_pair = phase(
                xn_mid, route_pair, router_pair, gain_pair, table_pair
            )
            targets = make_targets(place[0], route_pair, router_pair, tensor)
            gain, tile = prepared(1)
            gains.append(gain)
            tiles.append(tile)
        xn_parts = gather_parts(xn_mid)
        if layer == 0:
            xn_parts, targets, gains, tiles, up_pair, down_pair, w_out = phase(
                xn_parts, targets, gains, tiles, up_pair, down_pair, w_out
            )
        else:
            xn_parts, g1 = phase(xn_parts, g1)
        row, col, router = targets[layer::2]
        ex, y_parts = fwd_experts(selects[layer], row, col, router, up_pair, down_pair, xn_parts)
        saved.append([kept, pieces, mid, xn_mid, ex])
        if layer == 0:
            w_out_parts.append(gather_parts(w_out[1]))
            y_parts, w_out_parts[1] = phase(y_parts, w_out_parts[1])
            y_parts = swap_parts(y_parts)
            combined, out, xn_next, stat_more = after_experts(
                mid, ex[3], gains[1], valid_own, y_parts
            )
            outputs.append(out)
            stats.append((stat, stat_more))
            saved[0].append(combined)
            hidden[1] = out
            x_parts = gather_parts(xn_next)
        else:
            g_parts.append(exchange(g1, "tensor", tensor - 1))
            y_parts, g_parts, ex = phase(y_parts, g_parts, ex)

    fwd_y_parts = y_parts
    half = EXPERTS // 2
    small_1 = square_1 = None
    for layer in (1, 0):
        row, col, router = targets[layer::2]
        kept, pieces, mid, xn_mid, ex = saved[layer][:5]
        expert_in, act, slope, gate, probs = ex
        g = g_parts[0]
        (d_out, d_up), y_parts = bwd_experts(
            selects[layer], row, col, gate, slope, up_pair, down_pair, g_parts
        )
        if layer == 1:
            fwd_y_parts = swap_parts(fwd_y_parts)
            y_parts, d_out, d_up, fwd_y_parts = phase(y_parts, d_out, d_up, fwd_y_parts)
            combined, out, _, stat_more = after_experts(
                mid, gate, gains[1], valid_own, fwd_y_parts
            )
            outputs.append(out)
            stats.append((stat, stat_more))
        else:
            y_parts, d_out, d_up, out_terms_1, up_ring_1 = phase(
                y_parts, d_out, d_up, swap_parts(out_terms), ring_move(up_ring_1)
            )
            combined = saved[0][5]
            square_1 = attention_grads(place[1], saved[1][0][0], d_proj, out_terms_1, None)

        sent, keep = expert_grads(order, act, d_out, expert_in, d_up)
        y_parts, sent, keep, combined, square_1 = phase(
            swap_parts(y_parts), sent, keep, combined, square_1
        )

        (d_mid, d_a, grad_gain_mid, grad_router), d_pieces = middle_back(
            g,
            combined,
            probs,
            col,
            router,
            mid,
            gains[layer],
            xn_mid,
            y_parts,
            w_out_parts[layer],
        )
        d_pieces = swap_parts(d_pieces)
        out_terms = out_grads(pieces, d_a)
        terms = (keep, swap(sent))
        ring = ring_first(at, terms)
        d_pieces, out_terms, ring, terms = phase(d_pieces, out_terms, ring, terms)

        xn, qkv, turned, lse = kept
        (d_proj, diag, far, grad_gain_in), x_terms = bwd_attention(
            place[layer],
            piece_starts,
            valid_col,
            gains[layer],
            w_in_pair,
            tiles[layer],
            (xn, qkv, turned, lse),
            d_pieces,
        )
        if layer == 0:
            out_terms = swap_parts(out_terms)
        x_terms, ring, d_proj, diag, far, out_terms = phase(
            x_terms, ring_move(ring), d_proj, diag, far, out_terms
        )

        down_ring = ring_second(at, terms, ring, 0, half)
        up_ring = ring_second(at, terms, ring, half, half)
        if layer == 0:
            x_terms, down_ring = phase(x_terms, down_ring)
            down_ring = ring_move(down_ring)
        x_terms = swap_parts(x_terms)
        small = small_sums(
            place[0],
            diag,
            far,
            hot_rows,
            grad_gain_in,
            grad_gain_mid,
            grad_router,
            stats[layer],
            small_1,
        )
        if layer == 1:
            x_terms, down_ring, up_ring_1, small_1 = phase(x_terms, down_ring, up_ring, small)
            d_h_1, d_h_low = input_back(d_mid, hidden[1], gains[1], x_terms)
            g_parts = gather_parts(d_h_low)
            g_parts, down_ring_1, out_terms = phase(g_parts, ring_move(down_ring), out_terms)
            d_h_1, terms_1 = d_h_low, terms

    def kept_sent(values):
        return jnp.where(first, values[0], values[1]), jnp.where(first, values[1], values[0])

    def placed(own, received):
        return jnp.where(
            first,
            jnp.concatenate([own, received], axis=0),
            jnp.concatenate([received, own], axis=0),
        )

    square, sent = attention_grads(place[0], xn, d_proj, out_terms, square_1)
    x_terms, down_ring, up_ring, square, small = phase(
        x_terms, down_ring, up_ring, (square, swap(sent)), (small[0], swap(small[1]))
    )

    d_h = input_back(d_mid, hidden[0], gains[0], x_terms)[0]
    square_ring = ring_move(ring_first(at, square))
    small = small[0] + small[1]
    shared = sum_small(small[:8], "tensor")
    out_keep, sent = kept_sent(outputs)
    d_h_keep, d_h_sent = kept_sent((d_h, d_h_1.astype(F32)))
    up_ring, square_ring, shared, out_moved, d_h_moved = phase(
        ring_move(up_ring), square_ring, shared, swap(sent), swap(d_h_sent.astype(BF))
    )

    small = sum_small(jnp.concatenate([shared, small[8:]], axis=0), "dp")
    square_ring = ring_move(ring_second(at, square, square_ring, 0, 1))
    grad_w_in, grad_w_out = attention_results(ring_end(at, square, square_ring)[0], wide)
    layer_out = placed(out_keep[None], out_moved[None])
    input_grad = placed(d_h_keep[None], d_h_moved.astype(F32)[None])
    expert_results = []
    for lead, ring_0, ring_1 in ((0, down_ring, down_ring_1), (half, up_ring, up_ring_1)):
        keep, sent = ring_ends(at, (terms, terms_1), (ring_0, ring_1), lead, half)
        expert_results.append(placed(keep, swap(sent).astype(F32)))
    table = small[8 : 8 + heads, :BUCKETS].T
    share = BUCKETS // lax.axis_size("dp")
    stat = small[6]
    root_means = jnp.sqrt(stat[:3] / (stat[3] * D))
    return (
        layer_out[None],
        input_grad[None],
        small[None, 0:2],
        grad_w_in[None],
        grad_w_out[None],
        lax.dynamic_slice_in_dim(table, z * share, share, 0)[None],
        small[2:6].T[None],
        expert_results[1][None],
        expert_results[0][None],
        root_means[None],
    )


def solution(mesh):
    placed = (
        P("dp", "tensor", None),
        P("section", None, None),
        P("section", None, None, "tensor"),
        P("section", "tensor", None),
        P("section", None, "tensor"),
        P("section", None, None),
        P("section", None, None, "tensor"),
        P("section", None, "tensor", None),
        P("section", "dp", None, None),
        P("dp", None),
        P("dp", None),
        P("dp", "tensor", None),
    )
    return jax.shard_map(
        local,
        mesh=mesh,
        in_specs=placed,
        out_specs=(
            P("section", "dp", "tensor", None),
            P("section", "dp", "tensor", None),
            P("section", None, None),
            P("section", None, "dp", "tensor"),
            P("section", ("tensor", "dp"), None),
            P("section", "dp", "tensor"),
            P("section", None, None),
            P("section", None, "dp", "tensor"),
            P("section", None, ("tensor", "dp"), None),
            P("section", None),
        ),
        check_vma=False,
    )
```

```python
import functools

import jax
import jax.numpy as jnp
import numpy as np
from jax import lax
from jax.experimental import pallas as pl
from jax.experimental.pallas import tpu as pltpu
from jax.sharding import PartitionSpec as P

D = 768
HEAD_DIM = 64
BUCKETS = 32
EXPERTS = 4
CAP = 320
SEQ = 1024
PIECE = 256
PIECES = 2
SLOTS = EXPERTS * CAP

QB = PIECE
BAND = 128
WIDE = 2 * QB + BAND
DIAGS = 6

epsilon = 1e-06
bucket_edges = (12, 16, 23, 32, 46, 64, 91)
masked_score = -1000000000.0
far_bucket_behind = 15

BF = jnp.bfloat16
F32 = jnp.float32
MIB = 1024 * 1024


def dot(a, b, ca=1, cb=0):
    return lax.dot_general(a, b, (((ca,), (cb,)), ((), ())), preferred_element_type=F32)


def vm(count):
    return [pl.BlockSpec(memory_space=pltpu.VMEM)] * count


def smem():
    return pl.BlockSpec(memory_space=pltpu.SMEM)


def any_space(count):
    return [pl.BlockSpec(memory_space=pl.ANY)] * count


def limit(mib):
    return pltpu.CompilerParams(vmem_limit_bytes=mib * MIB)


def cost(flops, size):
    return pl.CostEstimate(flops=int(flops), bytes_accessed=int(size), transcendentals=0)


def shape(dims, kind):
    return jax.ShapeDtypeStruct(dims, kind)


def in_hbm(dims, kind):
    return pltpu.HBM(dims, kind)


def from_hbm(value):
    return pltpu.with_memory_space_constraint(value, pltpu.HBM)


def choose(select, own_ref, other_ref, to_ref):
    @pl.when(select == 0)
    def _():
        to_ref[...] = own_ref[...]

    @pl.when(select != 0)
    def _():
        to_ref[...] = other_ref[...]


def exchange(value, axis, mask):
    count = lax.axis_size(axis)
    return lax.ppermute(value, axis, [(i, i ^ mask) for i in range(count)])


def gather_parts(value):
    return [value] + [exchange(value, "tensor", k) for k in range(1, lax.axis_size("tensor"))]


def swap_parts(parts):
    return [parts[0]] + [exchange(p, "tensor", k) for k, p in enumerate(parts) if k]


def natural(t, k, size):
    return pl.ds(pl.multiple_of(jnp.bitwise_xor(t, k) * size, size), size)


def norm(vector, gain):
    return vector * lax.rsqrt(jnp.mean(vector * vector, axis=-1, keepdims=True) + epsilon) * gain


def total_of(value):
    return jnp.sum(jnp.sum(value, axis=0, keepdims=True), axis=1, keepdims=True)


def offset_buckets(offsets):
    distance = np.abs(offsets)
    far = np.full(offsets.shape, 8, np.int32)
    for edge_value in bucket_edges:
        far = far + (distance >= edge_value)
    return np.where(distance < 8, distance, far) + np.where(offsets > 0, 16, 0)


def diagonal_one_hot():
    lane = np.arange(2 * BAND)
    y = np.where(lane < BAND, lane, lane - 2 * BAND)
    offsets = BAND * (np.arange(DIAGS)[:, None] - 2) - y[None, :]
    hot = offset_buckets(offsets)[:, :, None] == np.arange(BUCKETS)
    hot = hot & (lane != BAND)[None, :, None]
    return hot.astype(np.float32)


def prepare_body(layer, place, own_gain, other_gain, own_table, other_table, hot, valid_ref, *refs):
    s = place[1]
    refs = refs[-5:] if layer == 0 else refs[-3:]
    gain_ref, tile_ref = refs[:2]
    heads = own_table.shape[0]
    own = s == layer
    gain_ref[...] = jnp.where(own, own_gain[...], other_gain[...])
    table = jnp.where(own, own_table[...], other_table[...])
    table = table - table[:, far_bucket_behind : far_bucket_behind + 1]
    by_offset = lax.dot_general(
        table,
        hot[...],
        (((1,), (0,)), ((), ())),
        precision=lax.Precision.HIGHEST,
        preferred_element_type=F32,
    )
    for h in range(heads):
        for d in range(DIAGS):
            row = by_offset[h : h + 1, d * 2 * BAND : (d + 1) * 2 * BAND]
            tile_ref[h * DIAGS + d] = pltpu.roll(
                jnp.broadcast_to(row, (BAND, 2 * BAND)), 0, 1, stride=1, stride_axis=0
            )[:, :BAND]
    if layer == 0:
        key_ref, own_ref, scratch = refs[2], refs[3], refs[4]
        rows = own_ref.shape[0]
        valid = jnp.where(s == 0, valid_ref[0:1, :], valid_ref[1:2, :]).astype(F32)
        column = jnp.broadcast_to(valid, (128, SEQ)).T[:, :1]
        scratch[...] = column
        key_ref[...] = jnp.where(column > 0, 0.0, masked_score)
        own_ref[...] = scratch[pl.ds(pl.multiple_of(place[0] * rows, rows), rows), :]


def prepare(layer, place, gains, tables, hot, valid, rows):
    outs = [shape((2, D), F32), shape((tables[0].shape[0] * DIAGS, BAND, BAND), F32)]
    if layer == 0:
        outs += [shape((SEQ, 1), F32), shape((rows, 1), F32)]
    return pl.pallas_call(
        functools.partial(prepare_body, layer),
        out_shape=outs,
        in_specs=[smem()] + vm(6),
        out_specs=vm(len(outs)),
        scratch_shapes=[pltpu.VMEM((SEQ, 1), F32)],
        compiler_params=limit(16),
        cost_estimate=cost(1e6, 1e5),
        name="prepare",
    )(place, *gains, *tables, hot, valid)


def targets_body(parts, place, own_route, other_route, own_router, other_router, *outs):
    row_refs, col_refs, router_refs, scratch = outs[:2], outs[2:4], outs[4:6], outs[6]
    t, s = place[0], place[1]
    rows = SEQ // parts
    before = lax.broadcasted_iota(jnp.int32, (SEQ, SEQ), 0)
    upto = (before <= lax.broadcasted_iota(jnp.int32, (SEQ, SEQ), 1)).astype(BF)
    expert = lax.broadcasted_iota(jnp.int32, (8, SEQ), 0)
    for layer in range(2):
        own = s == layer
        route = jnp.where(own, own_route[...], other_route[...])
        route = jnp.where(s == 0, route[0:1, :], route[1:2, :])
        hit = route == expert
        count = dot(hit.astype(BF), upto)
        slot = jnp.where(hit, count - 1.0 + (expert * CAP).astype(F32), 0.0)
        scratch[...] = jnp.sum(slot, axis=0, keepdims=True)
        for k in range(parts):
            row_refs[layer][:, k * rows : (k + 1) * rows] = scratch[:, natural(t, k, rows)].astype(
                jnp.int32
            )
        scratch[...] = row_refs[layer][...].astype(F32)
        turned = jnp.broadcast_to(scratch[...], (128, SEQ)).T
        col_refs[layer][...] = turned[:, :1].astype(jnp.int32)
        router_refs[layer][...] = jnp.zeros_like(router_refs[layer])
        router_refs[layer][:EXPERTS, :] = jnp.where(
            own, own_router[...].astype(F32), other_router[...].astype(F32)
        ).astype(BF)


def make_targets(place, routes, routers, parts):
    row, col = shape((1, SEQ), jnp.int32), shape((SEQ, 1), jnp.int32)
    router = shape((128, D), BF)
    return pl.pallas_call(
        functools.partial(targets_body, parts),
        out_shape=[row, row, col, col, router, router],
        in_specs=[smem()] + vm(4),
        out_specs=vm(6),
        scratch_shapes=[pltpu.VMEM((1, SEQ), F32)],
        compiler_params=limit(16),
        cost_estimate=cost(1e6, 1e5),
        name="make_targets",
    )(place, *routes, *routers)


def near_bias(tiles_ref, h, skip, width):
    first, last = skip // BAND, (skip + width) // BAND
    columns = [
        jnp.concatenate([tiles_ref[h * DIAGS + i - j + 1] for i in range(first, last)], axis=0)
        for j in range(QB // BAND)
    ]
    return jnp.concatenate(columns, axis=1)


def block_range(j):
    last = min(SEQ, QB * (j + 2))
    left = max(0, QB * j - BAND)
    return left, last, left - (QB * j - BAND)


def fill_mask(mask_ref, valid_ref, s0, s1, j):
    left, last, _ = block_range(j)
    width = last - left
    key = left + lax.broadcasted_iota(jnp.int32, (width, 1), 0)
    query = QB * j + lax.broadcasted_iota(jnp.int32, (1, QB), 1)

    def label(position, outside):
        second = jnp.where((position >= s1) & (position < s1 + PIECE), 1, outside)
        return jnp.where((position >= s0) & (position < s0 + PIECE), 0, second)

    allowed = (key <= query) | (label(key, -1) == label(query, -2))
    mask_ref[:width, :] = jnp.where(allowed, valid_ref[left:last, :], masked_score)


def fwd_attention_body(parts, norm_inside, *refs):
    place, starts, valid_col, gain, w_own, w_other, tiles_ref = refs[:7]
    x_refs = refs[7 : 7 + parts]
    xn_out, qkv_out, turned_out, lse_ref = refs[7 + parts : 11 + parts]
    out_refs = refs[11 + parts : 11 + 2 * parts]
    w_ref, xn_ref, qkv_ref, turned_ref, vt_ref, att_ref, mask_ref, valid_ref, sems = refs[
        11 + 2 * parts :
    ]
    t, s = place[0], place[1]
    s0, s1 = starts[s, 0], starts[s, 1]
    rows = SEQ // parts
    heads = qkv_ref.shape[1]
    wide = heads * HEAD_DIM

    choose(place[2], w_own, w_other, w_ref)
    valid_ref[...] = jnp.broadcast_to(valid_col[...], (SEQ, QB))
    for k in range(parts):
        where = natural(t, k, rows)
        x = x_refs[k][...]
        if norm_inside:
            x = norm(x.astype(F32), gain[0:1, :]).astype(BF)
        xn_ref[where, :] = x
        projected = dot(x, w_ref[...], 1, 1)
        for i in range(3):
            product = projected[:, i * wide : (i + 1) * wide]
            if i == 0:
                product = product * HEAD_DIM**-0.5
            turned = product.T.astype(BF)
            if i < 2:
                turned_ref[i, :, where] = turned
            else:
                vt_ref[:, where] = turned
            product = product.astype(BF)
            for h in range(heads):
                qkv_ref[i, h, where, :] = product[:, h * HEAD_DIM : (h + 1) * HEAD_DIM]

    copies = [
        pltpu.make_async_copy(a, b, sems.at[i])
        for i, (a, b) in enumerate(
            ((xn_ref, xn_out), (qkv_ref, qkv_out), (turned_ref, turned_out))
        )
    ]
    for copy in copies:
        copy.start()

    for j in range(SEQ // QB):
        left, last, skip = block_range(j)
        width = last - left
        columns = slice(j * QB, (j + 1) * QB)
        fill_mask(mask_ref, valid_ref, s0, s1, j)

        def one_head(h, carry):
            lanes = pl.ds(pl.multiple_of(h * HEAD_DIM, HEAD_DIM), HEAD_DIM)
            scores = dot(qkv_ref[1, h, :last, :], turned_ref[0, lanes, columns])
            near = scores[left:] + near_bias(tiles_ref, h, skip, width) + mask_ref[:width, :]
            highest = jnp.max(near, axis=0, keepdims=True)
            if left:
                far = scores[:left] + valid_ref[:left, :]
                highest = jnp.maximum(highest, jnp.max(far, axis=0, keepdims=True))
            near = jnp.exp(near - highest)
            total = jnp.sum(near, axis=0, keepdims=True)
            out = dot(vt_ref[lanes, left:last], near.astype(BF))
            if left:
                far = jnp.exp(far - highest)
                total = total + jnp.sum(far, axis=0, keepdims=True)
                out = out + dot(vt_ref[lanes, :left], far.astype(BF))
            lse_ref[h, :, columns] = highest + jnp.log(total)
            att_ref[lanes, columns] = (out * (1.0 / total)).astype(BF)
            return carry

        lax.fori_loop(0, heads, one_head, 0)

    for k in range(parts):
        out_refs[k][...] = att_ref[:, natural(t, k, rows)]
    for copy in copies:
        copy.wait()


def fwd_attention(place, starts, valid_col, gain, w_pair, tiles, x_parts, norm_inside):
    parts = len(x_parts)
    rows = SEQ // parts
    wide = w_pair[0].shape[0] // 3
    heads = wide // HEAD_DIM
    kept = [
        shape((SEQ, D), BF),
        shape((3, heads, SEQ, HEAD_DIM), BF),
        shape((2, wide, SEQ), BF),
    ]
    outs = pl.pallas_call(
        functools.partial(fwd_attention_body, parts, norm_inside),
        out_shape=[in_hbm(a.shape, a.dtype) for a in kept]
        + [shape((heads, 1, SEQ), F32)] + [shape((wide, rows), BF)] * parts,
        in_specs=[smem()] * 2 + vm(5 + parts),
        out_specs=any_space(3) + vm(1 + parts),
        scratch_shapes=[pltpu.VMEM((3 * wide, D), BF)]
        + [pltpu.VMEM(a.shape, a.dtype) for a in kept]
        + [
            pltpu.VMEM((wide, SEQ), BF),
            pltpu.VMEM((wide, SEQ), BF),
            pltpu.VMEM((WIDE, QB), F32),
            pltpu.VMEM((SEQ, QB), F32),
            pltpu.SemaphoreType.DMA((3,)),
        ],
        compiler_params=limit(32),
        cost_estimate=cost(9e9, 1e7),
        name="fwd_attention",
    )(place, starts, valid_col, gain, *[from_hbm(a) for a in (*w_pair, tiles)], *x_parts)
    return outs[:4], list(outs[4:])


def bwd_attention_body(parts, *refs):
    place, starts, valid_col, gain, w_own, w_other, tiles_ref, xn_ref = refs[:8]
    qkv_ref, turned_ref, lse_ref = refs[8:11]
    d_refs = refs[11 : 11 + parts]
    refs = refs[11 + parts :]
    proj_ref, sum_ref, far_ref, gain_ref = refs[:4]
    out_refs = refs[4 : 4 + parts]
    w_ref, d_ref, dt_ref, dq_ref, dk_ref, dv_ref, mask_ref, valid_ref = refs[4 + parts :]
    t, s = place[0], place[1]
    s0, s1 = starts[s, 0], starts[s, 1]
    rows = SEQ // parts
    heads = qkv_ref.shape[1]

    choose(place[2], w_own, w_other, w_ref)
    valid_ref[...] = jnp.broadcast_to(valid_col[...], (SEQ, QB))
    for k in range(parts):
        where = natural(t, k, rows)
        block = d_refs[k][...]
        dt_ref[:, where] = block.astype(F32).T.astype(BF)
        for h in range(heads):
            d_ref[h, where, :] = block[:, h * HEAD_DIM : (h + 1) * HEAD_DIM]
    dk_ref[...] = jnp.zeros_like(dk_ref)
    dv_ref[...] = jnp.zeros_like(dv_ref)
    sum_ref[...] = jnp.zeros_like(sum_ref)
    far_ref[...] = jnp.zeros_like(far_ref)

    for j in range(SEQ // QB):
        left, last, skip = block_range(j)
        width = last - left
        columns = slice(j * QB, (j + 1) * QB)
        fill_mask(mask_ref, valid_ref, s0, s1, j)

        def one_head(h, carry):
            lanes = pl.ds(pl.multiple_of(h * HEAD_DIM, HEAD_DIM), HEAD_DIM)
            q_block = qkv_ref[0, h, columns, :]
            d_block = d_ref[h, columns, :]
            lse = lse_ref[h, :, columns]
            scores = dot(qkv_ref[1, h, :last, :], turned_ref[0, lanes, columns])
            slopes = dot(qkv_ref[2, h, :last, :], dt_ref[lanes, columns])
            near = scores[left:] + near_bias(tiles_ref, h, skip, width) + mask_ref[:width, :]
            near = jnp.exp(near - lse)
            near_slope = near * slopes[left:]
            row_dot = jnp.sum(near_slope, axis=0, keepdims=True)
            if left:
                far = jnp.exp(scores[:left] + valid_ref[:left, :] - lse)
                far_slope = far * slopes[:left]
                row_dot = row_dot + jnp.sum(far_slope, axis=0, keepdims=True)
            near_slope = near_slope - near * row_dot
            for i in range(width // BAND):
                for c in range(QB // BAND):
                    sum_ref[h * DIAGS + skip // BAND + i - c + 1] += near_slope[
                        i * BAND : (i + 1) * BAND, c * BAND : (c + 1) * BAND
                    ]
            near_slope = near_slope.astype(BF)
            dk_ref[h, left:last, :] += dot(near_slope, q_block)
            dv_ref[h, left:last, :] += dot(near.astype(BF), d_block)
            dq = dot(turned_ref[1, lanes, left:last], near_slope)
            if left:
                far_slope = far_slope - far * row_dot
                far_ref[h] += jnp.sum(far_slope.reshape(left // 8, 8, QB), axis=0)
                far_slope = far_slope.astype(BF)
                dk_ref[h, :left, :] += dot(far_slope, q_block)
                dv_ref[h, :left, :] += dot(far.astype(BF), d_block)
                dq = dq + dot(turned_ref[1, lanes, :left], far_slope)
            dq_ref[lanes, columns] = dq * HEAD_DIM**-0.5
            return carry

        lax.fori_loop(0, heads, one_head, 0)

    for first in range(0, SEQ, rows):
        where = slice(first, first + rows)
        blocks = [dq_ref[:, where].T.astype(BF)]
        for source in (dk_ref, dv_ref):
            blocks += [source[h, where, :].astype(BF) for h in range(heads)]
        proj_ref[where, :] = jnp.concatenate(blocks, axis=1)
    gain_sum = jnp.zeros((1, D), F32)
    for k in range(parts):
        where = natural(t, k, rows)
        total = dot(proj_ref[where, :], w_ref[...])
        out_refs[k][...] = total.astype(BF)
        gain_sum = gain_sum + jnp.sum(total * xn_ref[where, :].astype(F32), axis=0, keepdims=True)
    gain_ref[...] = gain_sum / gain[0:1, :]


def bwd_attention(place, starts, valid_col, gain, w_pair, tiles, saved, d_parts):
    parts = len(d_parts)
    rows = SEQ // parts
    wide = w_pair[0].shape[0] // 3
    heads = wide // HEAD_DIM
    outs = pl.pallas_call(
        functools.partial(bwd_attention_body, parts),
        out_shape=[
            in_hbm((SEQ, 3 * wide), BF),
            in_hbm((heads * DIAGS, BAND, BAND), F32),
            shape((heads, 8, QB), F32),
            shape((1, D), F32),
        ]
        + [in_hbm((rows, D), BF)] * parts,
        in_specs=[smem()] * 2 + vm(9 + parts),
        out_specs=vm(4 + parts),
        scratch_shapes=[
            pltpu.VMEM((3 * wide, D), BF),
            pltpu.VMEM((heads, SEQ, HEAD_DIM), BF),
            pltpu.VMEM((wide, SEQ), BF),
            pltpu.VMEM((wide, SEQ), F32),
            pltpu.VMEM((heads, SEQ, HEAD_DIM), F32),
            pltpu.VMEM((heads, SEQ, HEAD_DIM), F32),
            pltpu.VMEM((WIDE, QB), F32),
            pltpu.VMEM((SEQ, QB), F32),
        ],
        compiler_params=limit(36),
        cost_estimate=cost(1.8e10, 1e7),
        name="bwd_attention",
    )(
        place,
        starts,
        valid_col,
        gain,
        *w_pair,
        tiles,
        *saved,
        *d_parts,
    )
    return outs[:4], list(outs[4:])


def small_sums_body(paired, place, tiles_ref, far_ref, hot, gain_in, gain_mid, router, *refs):
    stats, refs = refs[:2], refs[2:]
    heads = far_ref.shape[0]
    row = lax.broadcasted_iota(jnp.int32, (BAND, BAND), 0)
    column = lax.broadcasted_iota(jnp.int32, (BAND, BAND), 1)
    flip = (row + column == BAND - 1).astype(F32)
    out = refs[-1]
    out[...] = jnp.zeros_like(out)
    out[0:1, :] = gain_in[...]
    out[1:2, :] = gain_mid[...]
    out[2 : 2 + EXPERTS, :] = router[:EXPERTS, :]
    out[6:7, :128] = stats[0][...] + stats[1][...]
    by_offset = []
    for h in range(heads):
        sums = []
        for d in range(DIAGS):
            tile = lax.dot_general(
                flip,
                tiles_ref[h * DIAGS + d],
                (((1,), (0,)), ((), ())),
                precision=lax.Precision.HIGHEST,
                preferred_element_type=F32,
            )
            tile = jnp.concatenate([tile, jnp.zeros_like(tile)], axis=1)
            tile = pltpu.roll(tile, BAND + 1, 1, stride=1, stride_axis=0)
            sums.append(jnp.sum(tile, axis=0, keepdims=True))
        by_offset.append(jnp.concatenate(sums, axis=1))
    table = lax.dot_general(
        jnp.concatenate(by_offset, axis=0),
        hot[...],
        (((1,), (1,)), ((), ())),
        precision=lax.Precision.HIGHEST,
        preferred_element_type=F32,
    )
    bucket = lax.broadcasted_iota(jnp.int32, (1, BUCKETS), 1)
    for h in range(heads):
        behind = jnp.where(bucket == far_bucket_behind, total_of(far_ref[h]), 0.0)
        out[8 + h : 9 + h, :BUCKETS] = table[h : h + 1, :] + behind
    if paired:
        other, keep, sent = refs[:3]
        first = place[1] == 0
        keep[...] = jnp.where(first, out[...], other[...])
        sent[...] = jnp.where(first, other[...], out[...])


def small_sums(place, tiles, far, hot, gain_in, gain_mid, router, stats, other):
    paired = other is not None
    array = shape((16, D), F32)
    outs = pl.pallas_call(
        functools.partial(small_sums_body, paired),
        out_shape=[array] * (2 if paired else 1),
        in_specs=[smem()] + vm(8 + paired),
        out_specs=vm(2 if paired else 1),
        scratch_shapes=[pltpu.VMEM((16, D), F32)] if paired else [],
        compiler_params=limit(16),
        cost_estimate=cost(1e6, 1e5),
        name="small_sums",
    )(place, from_hbm(tiles), far, hot, gain_in, gain_mid, router, *stats, *([other] if paired else []))
    return outs if paired else outs[0]


def combine(parts, rows, target_col, slots_ref, out_refs):
    slot = lax.broadcasted_iota(jnp.int32, (rows, SLOTS), 1)
    for k in list(range(1, parts)) + [0]:
        hot = (target_col[k * rows : (k + 1) * rows, :] == slot).astype(BF)
        out_refs[k][...] = dot(hot, slots_ref[...]).astype(BF)


def dispatch(e, target_row, tokens_ref):
    slot = e * CAP + lax.broadcasted_iota(jnp.int32, (CAP, SEQ), 0)
    return dot((target_row[...] == slot).astype(BF), tokens_ref[...]).astype(BF)


HALF = EXPERTS // 2


def fwd_experts_body(parts, *refs):
    sel, order, target_row, target_col, router, up_own, up_other, down_own, down_other = refs[:9]
    x_refs = refs[9 : 9 + parts]
    half_ref, slope_ref, gate_ref, probs_ref = refs[9 + parts : 13 + parts]
    out_refs = refs[13 + parts : 13 + 2 * parts]
    x_ref, slots_ref, up_ref, down_ref = refs[13 + 2 * parts :]
    rows = SEQ // parts
    step = pl.program_id(0)
    e = order[step]

    @pl.when(step == 0)
    def _():
        lane = lax.broadcasted_iota(jnp.int32, (rows, 128), 1)
        for k in range(parts):
            where = slice(k * rows, (k + 1) * rows)
            x = x_refs[k][...]
            x_ref[where, :] = x
            logits = jnp.where(lane < EXPERTS, dot(x, router[...], 1, 1), -1e30)
            probs = jnp.exp(logits - jnp.max(logits, axis=-1, keepdims=True))
            probs = probs / jnp.sum(probs, axis=-1, keepdims=True)
            target = target_col[where, :]
            hit = (target >= lane * CAP) & (target < lane * CAP + CAP)
            gate_ref[where, :] = jnp.sum(jnp.where(hit, probs, 0.0), axis=-1, keepdims=True)
            if k == 0:
                probs_ref[...] = probs

    choose(sel[0], up_own.at[0], up_other.at[0], up_ref)
    choose(sel[0], down_own.at[0], down_other.at[0], down_ref)
    expert_in = dispatch(e, target_row, x_ref)
    half_ref[0, 1] = expert_in
    up = dot(expert_in, up_ref[...])
    inner = np.sqrt(2 / np.pi).astype(np.float32)
    square = up * up
    bend = jnp.tanh(inner * (up * (1.0 + 0.044715 * square)))
    half = 0.5 * (1.0 + bend)
    act = (up * half).astype(BF)
    half_ref[0, 0] = act
    slope_ref[0] = half + 0.5 * up * (1.0 - bend * bend) * (
        inner * (1.0 + 3 * 0.044715 * square)
    )
    slots_ref[pl.ds(pl.multiple_of(e * CAP, CAP), CAP), :] = dot(act, down_ref[...]).astype(BF)

    @pl.when(step == EXPERTS - 1)
    def _():
        combine(parts, rows, target_col, slots_ref, out_refs)


def expert_specs(block):
    own = pl.BlockSpec(block, lambda i, sel, order: (order[i] * (1 - sel[0]), 0, 0))
    other = pl.BlockSpec(block, lambda i, sel, order: (order[i] * sel[0], 0, 0))
    return [own, other]


def half_spec(columns):
    return pl.BlockSpec((1, 2, CAP, columns), lambda i, sel, order: (i, 0, 0, 0))


def whole(dims):
    return pl.BlockSpec(dims, lambda i, sel, order: (0,) * len(dims))


def fwd_experts(select, order, target_row, target_col, router, up_pair, down_pair, x_parts):
    parts = len(x_parts)
    rows = SEQ // parts
    hidden = up_pair[0].shape[2]
    each_hidden = pl.BlockSpec((1, CAP, hidden), lambda i, sel, order: (i, 0, 0))
    outs = pl.pallas_call(
        functools.partial(fwd_experts_body, parts),
        grid_spec=pltpu.PrefetchScalarGridSpec(
            num_scalar_prefetch=2,
            grid=(EXPERTS,),
            in_specs=[whole((1, SEQ)), whole((SEQ, 1)), whole((128, D))]
            + expert_specs((1, D, hidden))
            + expert_specs((1, hidden, D))
            + [whole((rows, D))] * parts,
            out_specs=[half_spec(D)]
            + [each_hidden, whole((SEQ, 1)), whole((rows, 128))]
            + [whole((rows, D))] * parts,
            scratch_shapes=[
                pltpu.VMEM((SEQ, D), BF),
                pltpu.VMEM((SLOTS, D), BF),
                pltpu.VMEM((D, hidden), BF),
                pltpu.VMEM((hidden, D), BF),
            ],
        ),
        out_shape=[in_hbm((EXPERTS, 2, CAP, D), BF)]
        + [
            in_hbm((EXPERTS, CAP, hidden), F32),
            shape((SEQ, 1), F32),
            shape((rows, 128), F32),
        ]
        + [shape((rows, D), BF)] * parts,
        compiler_params=limit(36),
        cost_estimate=cost(1.2e10, 3e7),
        name="fwd_experts",
    )(
        select,
        order,
        target_row,
        target_col,
        router,
        *[from_hbm(a) for a in (*up_pair, *down_pair)],
        *x_parts,
    )
    return outs[:4], list(outs[4:])


def bwd_experts_body(parts, *refs):
    sel, order, target_row, target_col, gate, slope_ref = refs[:6]
    up_own, up_other, down_own, down_other = refs[6:10]
    g_refs = refs[10 : 10 + parts]
    refs = refs[10 + parts :]
    half_ref = refs[0]
    out_refs = refs[1 : 1 + parts]
    g_ref, slots_ref, up_ref, down_ref = refs[1 + parts :]
    rows = SEQ // parts
    step = pl.program_id(0)
    e = order[step]

    @pl.when(step == 0)
    def _():
        for k in range(parts):
            where = slice(k * rows, (k + 1) * rows)
            g_ref[where, :] = (gate[where, :] * g_refs[k][...].astype(F32)).astype(BF)

    choose(sel[0], up_own.at[0], up_other.at[0], up_ref)
    choose(sel[0], down_own.at[0], down_other.at[0], down_ref)
    d_out = dispatch(e, target_row, g_ref)
    half_ref[0, 0] = d_out
    d_up = (slope_ref[0] * dot(d_out, down_ref[...], 1, 1)).astype(BF)
    half_ref[0, 1] = d_up
    slots_ref[pl.ds(pl.multiple_of(e * CAP, CAP), CAP), :] = dot(d_up, up_ref[...], 1, 1).astype(
        BF
    )

    @pl.when(step == EXPERTS - 1)
    def _():
        combine(parts, rows, target_col, slots_ref, out_refs)


def bwd_experts(select, order, target_row, target_col, gate, slope, up_pair, down_pair, g_parts):
    parts = len(g_parts)
    rows = SEQ // parts
    hidden = up_pair[0].shape[2]
    each_hidden = pl.BlockSpec((1, CAP, hidden), lambda i, sel, order: (i, 0, 0))
    outs = pl.pallas_call(
        functools.partial(bwd_experts_body, parts),
        grid_spec=pltpu.PrefetchScalarGridSpec(
            num_scalar_prefetch=2,
            grid=(EXPERTS,),
            in_specs=[whole((1, SEQ)), whole((SEQ, 1)), whole((SEQ, 1)), each_hidden]
            + expert_specs((1, D, hidden))
            + expert_specs((1, hidden, D))
            + [whole((rows, D))] * parts,
            out_specs=[half_spec(D)] + [whole((rows, D))] * parts,
            scratch_shapes=[
                pltpu.VMEM((SEQ, D), BF),
                pltpu.VMEM((SLOTS, D), BF),
                pltpu.VMEM((D, hidden), BF),
                pltpu.VMEM((hidden, D), BF),
            ],
        ),
        out_shape=[in_hbm((EXPERTS, 2, CAP, D), BF)] + [shape((rows, D), BF)] * parts,
        compiler_params=limit(36),
        cost_estimate=cost(1.2e10, 3e7),
        name="bwd_experts",
    )(
        select,
        order,
        target_row,
        target_col,
        gate,
        *[from_hbm(a) for a in (slope, *up_pair, *down_pair)],
        *g_parts,
    )
    return outs[0], list(outs[1:])


def norm_back(vector, gain, grad):
    scale = lax.rsqrt(jnp.mean(vector * vector, axis=-1, keepdims=True) + epsilon)
    unit = vector * scale
    scaled = grad * gain
    inner = jnp.mean(unit * scaled, axis=-1, keepdims=True)
    return scale * (scaled - unit * inner), grad * unit


def after_attention_body(parts, *refs):
    h_ref, gain, valid = refs[:3]
    p_refs, w_refs = refs[3 : 3 + parts], refs[3 + parts : 3 + 2 * parts]
    mid_ref, xn_ref, stat_ref = refs[3 + 2 * parts :]
    branch = dot(p_refs[0][...], w_refs[0][...], 0, 0)
    for k in range(1, parts):
        branch = branch + dot(p_refs[k][...], w_refs[k][...], 0, 0)
    h = h_ref[...].astype(F32)
    mid = h + branch
    mid_ref[...] = mid
    xn_ref[...] = norm(mid, gain[1:2, :]).astype(BF)
    weight = valid[...]
    lane = lax.broadcasted_iota(jnp.int32, (1, 128), 1)
    sums = jnp.where(lane == 0, total_of(weight * h * h), 0.0)
    sums = jnp.where(lane == 1, total_of(weight * branch * branch), sums)
    stat_ref[...] = jnp.where(lane == 3, total_of(weight), sums)


def after_attention(h, gain, valid, pieces, w_parts):
    parts = len(pieces)
    rows = h.shape[0]
    return pl.pallas_call(
        functools.partial(after_attention_body, parts),
        out_shape=[shape((rows, D), F32), shape((rows, D), BF), shape((1, 128), F32)],
        in_specs=vm(3 + 2 * parts),
        out_specs=vm(3),
        compiler_params=limit(24),
        cost_estimate=cost(2e9, 4e6),
        name="after_attention",
    )(h, gain, valid, *pieces, *w_parts)


def after_experts_body(parts, *refs):
    mid_ref, gate, gain, valid = refs[:4]
    y_refs = refs[4 : 4 + parts]
    comb_ref, out_ref, xn_ref, stat_ref = refs[4 + parts :]
    total = y_refs[0][...].astype(F32)
    for k in range(1, parts):
        total = total + y_refs[k][...].astype(F32)
    combined = total.astype(BF)
    comb_ref[...] = combined
    branch = gate[: mid_ref.shape[0], :] * combined.astype(F32)
    out = (mid_ref[...] + branch).astype(BF)
    out_ref[...] = out
    xn_ref[...] = norm(out.astype(F32), gain[0:1, :]).astype(BF)
    lane = lax.broadcasted_iota(jnp.int32, (1, 128), 1)
    stat_ref[...] = jnp.where(lane == 2, total_of(valid[...] * branch * branch), 0.0)


def after_experts(mid, gate, gain, valid, y_parts):
    parts = len(y_parts)
    rows = mid.shape[0]
    return pl.pallas_call(
        functools.partial(after_experts_body, parts),
        out_shape=[shape((rows, D), BF)] * 3 + [shape((1, 128), F32)],
        in_specs=vm(4 + parts),
        out_specs=vm(4),
        compiler_params=limit(24),
        cost_estimate=cost(1e8, 4e6),
        name="after_experts",
    )(mid, gate, gain, valid, *y_parts)


def middle_back_body(parts, *refs):
    g_ref, comb_ref, probs_ref, target_col, router, mid_ref, gain, xn_ref = refs[:8]
    y_refs, w_refs = refs[8 : 8 + parts], refs[8 + parts : 8 + 2 * parts]
    refs = refs[8 + 2 * parts :]
    dmid_ref, da_ref, gain_ref, router_ref = refs[:4]
    out_refs = refs[4:]
    rows = g_ref.shape[0]
    g = g_ref[...].astype(F32)
    total = y_refs[0][...].astype(F32)
    for k in range(1, parts):
        total = total + y_refs[k][...].astype(F32)
    d_in = total.astype(BF).astype(F32)
    d_gate = jnp.sum(g * comb_ref[...].astype(F32), axis=-1, keepdims=True)
    lane = lax.broadcasted_iota(jnp.int32, (rows, 128), 1)
    target = target_col[:rows, :]
    hit = (target >= lane * CAP) & (target < lane * CAP + CAP)
    probs = probs_ref[...]
    chosen = jnp.where(hit, d_gate, 0.0)
    inner = jnp.sum(probs * chosen, axis=-1, keepdims=True)
    d_logits = (probs * (chosen - inner)).astype(BF)
    router_ref[...] = dot(d_logits, xn_ref[...], 0, 0)[:8]
    d_xn = d_in + dot(d_logits, router[...])
    d_norm, d_gain = norm_back(mid_ref[...], gain[1:2, :], d_xn)
    gain_ref[...] = jnp.sum(d_gain, axis=0, keepdims=True)
    d_mid = g + d_norm
    dmid_ref[...] = d_mid
    d_a = d_mid.astype(BF)
    da_ref[...] = d_a
    for k in list(range(1, parts)) + [0]:
        out_refs[k][...] = dot(d_a, w_refs[k][...], 1, 1).astype(BF)


def middle_back(g, combined, probs, target_col, router, mid, gain, xn, y_parts, w_parts):
    parts = len(y_parts)
    rows = g.shape[0]
    wide = w_parts[0].shape[0]
    outs = pl.pallas_call(
        functools.partial(middle_back_body, parts),
        out_shape=[shape((rows, D), F32), shape((rows, D), BF), shape((1, D), F32)]
        + [shape((8, D), F32)]
        + [shape((rows, wide), BF)] * parts,
        in_specs=vm(8 + 2 * parts),
        out_specs=vm(4 + parts),
        compiler_params=limit(24),
        cost_estimate=cost(2e9, 6e6),
        name="middle_back",
    )(
        *[
            from_hbm(a)
            for a in (
                g,
                combined,
                probs,
                target_col,
                router,
                mid,
                gain,
                xn,
                *y_parts,
                *w_parts,
            )
        ]
    )
    return outs[:4], list(outs[4:])


def input_back_body(parts, *refs):
    dmid_ref, h_ref, gain = refs[:3]
    y_refs = refs[3 : 3 + parts]
    wide_ref, low_ref = refs[3 + parts :]
    total = y_refs[0][...].astype(F32)
    for k in range(1, parts):
        total = total + y_refs[k][...].astype(F32)
    d_h = dmid_ref[...] + norm_back(h_ref[...].astype(F32), gain[0:1, :], total)[0]
    wide_ref[...] = d_h
    low_ref[...] = d_h.astype(BF)


def input_back(d_mid, h, gain, y_parts):
    parts = len(y_parts)
    rows = h.shape[0]
    return pl.pallas_call(
        functools.partial(input_back_body, parts),
        out_shape=[shape((rows, D), F32), shape((rows, D), BF)],
        in_specs=vm(3 + parts),
        out_specs=vm(2),
        compiler_params=limit(24),
        cost_estimate=cost(1e8, 4e6),
        name="input_back",
    )(d_mid, h, gain, *y_parts)


def expert_grads_body(fwd_own, fwd_other, bwd_own, bwd_other, out):
    for kind in range(2):
        total = dot(fwd_own[0, kind], bwd_own[0, kind], 0, 0)
        total = total + dot(fwd_other[0, kind], bwd_other[0, kind], 0, 0)
        out[kind, 0] = total.astype(BF)


def expert_grads(values):
    columns = values[0].shape[3]
    block = (1, 2, CAP, columns)
    own = pl.BlockSpec(block, lambda i: (i + HALF, 0, 0, 0))
    other = pl.BlockSpec(block, lambda i: (i, 0, 0, 0))
    outs = pl.pallas_call(
        expert_grads_body,
        grid=(HALF,),
        in_specs=[own, other, own, other],
        out_specs=pl.BlockSpec((2, 1, columns, columns), lambda i: (0, i, 0, 0)),
        out_shape=in_hbm((2, HALF, columns, columns), BF),
        compiler_params=limit(28),
        cost_estimate=cost(1e6, 1e5),
        name="expert_grads",
    )(from_hbm(values[0]), from_hbm(values[1]), from_hbm(values[2]), values[3])
    return outs.reshape(2 * HALF, columns, columns)


def out_grads_body(parts, *refs):
    pieces, d_a, outs = refs[:parts], refs[parts], refs[parts + 1 :]
    for k in list(range(1, parts)) + [0]:
        outs[k][...] = dot(pieces[k][...], d_a[...]).astype(BF)


def out_grads(pieces, d_a):
    parts = len(pieces)
    wide = pieces[0].shape[0]
    return pl.pallas_call(
        functools.partial(out_grads_body, parts),
        out_shape=[shape((wide, D), BF)] * parts,
        in_specs=vm(parts + 1),
        out_specs=vm(parts),
        compiler_params=limit(16),
        cost_estimate=cost(1e6, 1e5),
        name="out_grads",
    )(*pieces, d_a)


def attention_grads_body(parts, chunks, place, xn_ref, proj_ref, *refs):
    terms, (send_ref, keep_ref, out) = refs[:parts], refs[parts:]
    wide = terms[0].shape[0]
    rows, taken = D // chunks, wide // chunks
    out[:, : 3 * wide] = dot(xn_ref[...], proj_ref[...], 0, 0)
    total = terms[0][...].astype(F32)
    for k in range(1, parts):
        total = total + terms[k][...].astype(F32)
    for c in range(chunks):
        for b in range(D // wide):
            out[c * rows + b * taken : c * rows + (b + 1) * taken, 3 * wide :] = total[
                c * taken : (c + 1) * taken, b * wide : (b + 1) * wide
            ]
    first = place[1] == 0
    half = D // 2
    left, right = out[:, :half], out[:, half:]
    keep_ref[:, :half] = jnp.where(first, left, right).astype(BF)
    send_ref[:, :half] = jnp.where(first, right, left).astype(BF)


def attention_grads(place, xn, proj, terms):
    parts = len(terms)
    return pl.pallas_call(
        functools.partial(attention_grads_body, parts, lax.axis_size("dp")),
        out_shape=[shape((D, D // 2), BF)] * 2,
        in_specs=[smem()] + vm(2 + parts),
        out_specs=vm(2),
        scratch_shapes=[pltpu.VMEM((D, D), F32)],
        compiler_params=limit(24),
        cost_estimate=cost(1e6, 1e5),
        name="attention_grads",
    )(place, from_hbm(xn), from_hbm(proj), *terms)


def chunks_body(count, place, own, received, *outs):
    rows = outs[0].shape[0]
    for k in range(count):
        where = natural(place[3], k, rows)
        total = own[where, :].astype(F32) + received[where, :].astype(F32)
        outs[k][...] = total.astype(outs[k].dtype)


def scatter_small(place, own, received):
    count = lax.axis_size("dp")
    if count != 4:
        total = (own.astype(F32) + received.astype(F32)).astype(BF)
        return [total]
    dims = (own.shape[0] // count, own.shape[1])
    return pl.pallas_call(
        functools.partial(chunks_body, count),
        out_shape=[shape(dims, F32)] + [shape(dims, BF)] * (count - 1),
        in_specs=[smem()] + vm(2),
        out_specs=vm(count),
        compiler_params=limit(16),
        cost_estimate=cost(1e6, 1e5),
        name="chunks",
    )(place, own, received)


def scatter_end(chunks):
    if len(chunks) == 1:
        return lax.psum_scatter(chunks[0], "dp", scatter_dimension=0, tiled=True).astype(F32)
    others = [exchange(chunk, "dp", k).astype(F32) for k, chunk in enumerate(chunks) if k]
    return functools.reduce(jnp.add, others, chunks[0])


def attention_results(value, wide):
    rows = value.shape[0]
    taken = rows // (D // wide)
    return (
        jnp.stack([value[:, i * wide : (i + 1) * wide] for i in range(3)]),
        jnp.concatenate(
            [value[b * taken : (b + 1) * taken, 3 * wide :] for b in range(D // wide)], axis=1
        ),
    )


def scatter_sum(value, dim):
    return lax.psum_scatter(value, "dp", scatter_dimension=dim, tiled=True)


def phase(*values):
    return lax.optimization_barrier(values)


def sum_small(value, axis):
    count = lax.axis_size(axis)
    if count != 4:
        return lax.psum(value, axis)
    return (value + exchange(value, axis, 1)) + (
        exchange(value, axis, 2) + exchange(value, axis, 3)
    )


def local(
    inputs,
    norm_gains,
    attention_in,
    attention_out,
    bias_table,
    router_weight,
    up_weight,
    down_weight,
    routes,
    piece_starts,
    valid_mask,
    cotangent,
):
    s = lax.axis_index("section")
    t = lax.axis_index("tensor")
    z = lax.axis_index("dp")
    tensor = lax.axis_size("tensor")
    rows = inputs.shape[1]
    wide = attention_in.shape[3]
    heads = wide // HEAD_DIM
    first = s == 0

    def mine(array):
        return lax.dynamic_index_in_dim(array, s, 0, keepdims=False)

    def by_layer(own, other):
        return jnp.where(first, own, other), jnp.where(first, other, own)

    def swap(value):
        return jax.tree.map(lambda a: exchange(a, "section", 1), value)

    def pair(value):
        return value, swap(value)

    h0 = mine(inputs)
    g1 = mine(cotangent)
    place = [
        jnp.stack([t, s, jnp.where(s == layer, 0, 1), z]).astype(jnp.int32) for layer in range(2)
    ]
    selects = [place[layer][2:3] for layer in range(2)]
    order = jnp.where(first, jnp.array([2, 3, 0, 1]), jnp.array([0, 1, 2, 3])).astype(jnp.int32)
    hot = diagonal_one_hot()
    hot_rows = hot.transpose(2, 0, 1).reshape(BUCKETS, -1)

    gain_pair, table_pair = pair(norm_gains[0]), pair(bias_table[0].T)
    w_out_pair = pair(attention_out[0])

    def prepared(layer):
        return prepare(layer, place[layer], gain_pair, table_pair, hot_rows, valid_mask, rows)

    x_parts, first_prepared, gain_pair, table_pair, w_in_pair, w_out, route_pair, router_pair, up, down = phase(
        gather_parts(h0),
        prepared(0),
        gain_pair,
        table_pair,
        pair(jnp.swapaxes(attention_in[0], 1, 2).reshape(3 * wide, D)),
        by_layer(*w_out_pair),
        pair(routes[0, :, :, 0]),
        pair(router_weight[0].T),
        up_weight[0],
        down_weight[0],
    )

    gain, tile, valid_col, valid_own = first_prepared
    gains, tiles = [gain], [tile]
    hidden = [h0, None]
    saved, outputs, stats, w_out_parts = [], [], [], []
    for layer in range(2):
        kept, att_parts = fwd_attention(
            place[layer],
            piece_starts,
            valid_col,
            gains[layer],
            w_in_pair,
            tiles[layer],
            x_parts,
            layer == 0,
        )
        if layer == 0:
            w_out_parts.append(gather_parts(w_out[0]))
            up_pair, down_pair = pair(up), pair(down)
            att_parts, w_out_parts[0] = phase(att_parts, w_out_parts[0])
        else:
            g_parts = [g1] + [exchange(g1, "tensor", k) for k in range(1, tensor - 1)]
            att_parts, g_parts = phase(att_parts, g_parts)
        pieces = swap_parts(att_parts)
        mid, xn_mid, stat = after_attention(
            hidden[layer], gains[layer], valid_own, pieces, w_out_parts[layer]
        )
        if layer == 0:
            xn_mid, route_pair, router_pair, gain_pair, table_pair = phase(
                xn_mid, route_pair, router_pair, gain_pair, table_pair
            )
            targets = make_targets(place[0], route_pair, router_pair, tensor)
            gain, tile = prepared(1)
            gains.append(gain)
            tiles.append(tile)
        xn_parts = gather_parts(xn_mid)
        if layer == 0:
            xn_parts, targets, gains, tiles, up_pair, down_pair, w_out = phase(
                xn_parts, targets, gains, tiles, up_pair, down_pair, w_out
            )
        else:
            xn_parts, g1 = phase(xn_parts, g1)
        row, col, router = targets[layer::2]
        ex, y_parts = fwd_experts(
            selects[layer], order, row, col, router, up_pair, down_pair, xn_parts
        )
        if layer == 0:
            w_out_parts.append(gather_parts(w_out[1]))
            y_parts, w_out_parts[1], ex = phase(y_parts, w_out_parts[1], ex)
            y_parts = swap_parts(y_parts)
            fwd_sent = [ex[0]]
            saved.append([kept, pieces, mid, xn_mid, ex])
            combined, out, xn_next, stat_more = after_experts(
                mid, ex[2], gains[1], valid_own, y_parts
            )
            outputs.append(out)
            stats.append((stat, stat_more))
            saved[0].append(combined)
            hidden[1] = out
            x_parts = gather_parts(xn_next)
        else:
            g_parts.append(exchange(g1, "tensor", tensor - 1))
            y_parts, g_parts, ex = phase(y_parts, g_parts, ex)
            fwd_sent.append(ex[0])
            saved.append([kept, pieces, mid, xn_mid, ex])

    fwd_y_parts = y_parts
    small_1, square_1, expert_sums = None, [], []
    for layer in (1, 0):
        row, col, router = targets[layer::2]
        kept, pieces, mid, xn_mid, ex = saved[layer][:5]
        fwd_halves, slope, gate, probs = ex
        g = g_parts[0]
        bwd_halves, y_parts = bwd_experts(
            selects[layer], order, row, col, gate, slope, up_pair, down_pair, g_parts
        )
        fwd_other = swap(fwd_sent[layer])
        if layer == 1:
            y_parts, bwd_halves, fwd_y_parts, fwd_other = phase(
                y_parts, bwd_halves, swap_parts(fwd_y_parts), fwd_other
            )
            combined, out, _, stat_more = after_experts(
                mid, gate, gains[1], valid_own, fwd_y_parts
            )
            outputs.append(out)
            stats.append((stat, stat_more))
        else:
            y_parts, bwd_halves, fwd_other, square_1 = phase(
                y_parts, bwd_halves, fwd_other, scatter_end(square_1)
            )
            combined = saved[0][5]

        total = expert_grads((fwd_halves, fwd_other, bwd_halves, swap(bwd_halves)))
        y_parts, total, combined = phase(swap_parts(y_parts), total, combined)
        if layer == 0 or 'wa' == "wa":
            expert_sums.append(scatter_sum(total, 1))

        (d_mid, d_a, grad_gain_mid, grad_router), d_pieces = middle_back(
            g,
            combined,
            probs,
            col,
            router,
            mid,
            gains[layer],
            xn_mid,
            y_parts,
            w_out_parts[layer],
        )
        d_pieces, out_terms = phase(swap_parts(d_pieces), out_grads(pieces, d_a))

        xn, qkv, turned, lse = kept
        (d_proj, diag, far, grad_gain_in), x_terms = bwd_attention(
            place[layer],
            piece_starts,
            valid_col,
            gains[layer],
            w_in_pair,
            tiles[layer],
            (xn, qkv, turned, lse),
            d_pieces,
        )
        x_terms, d_proj, diag, far, out_terms = phase(
            x_terms, d_proj, diag, far, swap_parts(out_terms)
        )

        x_terms = swap_parts(x_terms)
        sent, square = attention_grads(place[layer], xn, d_proj, out_terms)
        small = small_sums(
            place[0],
            diag,
            far,
            hot_rows,
            grad_gain_in,
            grad_gain_mid,
            grad_router,
            stats[layer],
            small_1,
        )
        if layer == 1:
            x_terms, small_1, sent, square = phase(x_terms, small, sent, square)
            d_h_1, d_h_low = input_back(d_mid, hidden[1], gains[1], x_terms)
            g_parts, square_1 = phase(
                gather_parts(d_h_low), scatter_small(place[1], square, swap(sent))
            )
            d_h_1 = d_h_low

    def kept_sent(values):
        return jnp.where(first, values[0], values[1]), jnp.where(first, values[1], values[0])

    def placed(own, received, axis=0):
        return jnp.where(
            first,
            jnp.concatenate([own, received], axis=axis),
            jnp.concatenate([received, own], axis=axis),
        )

    x_terms, square, sent, small = phase(x_terms, square, sent, small)

    d_h = input_back(d_mid, hidden[0], gains[0], x_terms)[0]
    out_keep, out_sent = kept_sent(outputs)
    d_h_keep, d_h_sent = kept_sent((d_h, d_h_1.astype(F32)))
    out_moved, d_h_moved, small, square = phase(
        swap(out_sent),
        swap(d_h_sent.astype(BF)),
        (small[0], swap(small[1])),
        scatter_small(place[0], square, swap(sent)),
    )
    small = small[0] + small[1]
    small, shared, square_0 = phase(small, sum_small(small[:8], "tensor"), scatter_end(square))
    small = sum_small(jnp.concatenate([shared, small[8:]], axis=0), "dp")

    layer_out = placed(out_keep[None], out_moved[None])
    input_grad = placed(d_h_keep[None], d_h_moved.astype(F32)[None])
    keep, sent = kept_sent((square_0, square_1))
    square = placed(keep, swap(sent.astype(BF)).astype(F32), axis=1)
    grad_w_in, grad_w_out = attention_results(square, wide)
    keep, sent = kept_sent(expert_sums[::-1])
    experts = placed(*[a.astype(F32).reshape(2, HALF, -1, D) for a in (keep, swap(sent))], axis=1)
    table = small[8 : 8 + heads, :BUCKETS].T
    share = BUCKETS // lax.axis_size("dp")
    stat = small[6]
    root_means = jnp.sqrt(stat[:3] / (stat[3] * D))
    return (
        layer_out[None],
        input_grad[None],
        small[None, 0:2],
        grad_w_in[None],
        grad_w_out[None],
        lax.dynamic_slice_in_dim(table, z * share, share, 0)[None],
        small[2:6].T[None],
        experts[1][None],
        experts[0][None],
        root_means[None],
    )


def solution(mesh):
    placed = (
        P("dp", "tensor", None),
        P("section", None, None),
        P("section", None, None, "tensor"),
        P("section", "tensor", None),
        P("section", None, "tensor"),
        P("section", None, None),
        P("section", None, None, "tensor"),
        P("section", None, "tensor", None),
        P("section", "dp", None, None),
        P("dp", None),
        P("dp", None),
        P("dp", "tensor", None),
    )
    return jax.shard_map(
        local,
        mesh=mesh,
        in_specs=placed,
        out_specs=(
            P("section", "dp", "tensor", None),
            P("section", "dp", "tensor", None),
            P("section", None, None),
            P("section", None, "dp", "tensor"),
            P("section", ("tensor", "dp"), None),
            P("section", "dp", "tensor"),
            P("section", None, None),
            P("section", None, "dp", "tensor"),
            P("section", None, ("tensor", "dp"), None),
            P("section", None),
        ),
        check_vma=False,
    )
```

```python
import functools

import jax
import jax.numpy as jnp
import numpy as np
from jax import lax
from jax.experimental import pallas as pl
from jax.experimental.pallas import tpu as pltpu
from jax.sharding import PartitionSpec as P

D = 768
HEAD_DIM = 64
BUCKETS = 32
EXPERTS = 4
CAP = 320
SEQ = 1024
PIECE = 256
PIECES = 2
SLOTS = EXPERTS * CAP

QB = PIECE
BAND = 128
WIDE = 2 * QB + BAND
DIAGS = 6

epsilon = 1e-06
bucket_edges = (12, 16, 23, 32, 46, 64, 91)
masked_score = -1000000000.0
far_bucket_behind = 15

BF = jnp.bfloat16
F32 = jnp.float32
MIB = 1024 * 1024


def dot(a, b, ca=1, cb=0):
    return lax.dot_general(a, b, (((ca,), (cb,)), ((), ())), preferred_element_type=F32)


def vm(count):
    return [pl.BlockSpec(memory_space=pltpu.VMEM)] * count


def smem():
    return pl.BlockSpec(memory_space=pltpu.SMEM)


def any_space(count):
    return [pl.BlockSpec(memory_space=pl.ANY)] * count


def limit(mib):
    return pltpu.CompilerParams(vmem_limit_bytes=mib * MIB)


def cost(flops, size):
    return pl.CostEstimate(flops=int(flops), bytes_accessed=int(size), transcendentals=0)


def shape(dims, kind):
    return jax.ShapeDtypeStruct(dims, kind)


def in_hbm(dims, kind):
    return pltpu.HBM(dims, kind)


def from_hbm(value):
    return pltpu.with_memory_space_constraint(value, pltpu.HBM)


def choose(select, own_ref, other_ref, to_ref):
    @pl.when(select == 0)
    def _():
        to_ref[...] = own_ref[...]

    @pl.when(select != 0)
    def _():
        to_ref[...] = other_ref[...]


def either(select, step, own, other):
    @pl.when(select == 0)
    def _():
        step(*own)

    @pl.when(select != 0)
    def _():
        step(*other)


def exchange(value, axis, mask):
    count = lax.axis_size(axis)
    return lax.ppermute(value, axis, [(i, i ^ mask) for i in range(count)])


def gather_parts(value):
    return [value] + [exchange(value, "tensor", k) for k in range(1, lax.axis_size("tensor"))]


def swap_parts(parts):
    return [parts[0]] + [exchange(p, "tensor", k) for k, p in enumerate(parts) if k]


def natural(t, k, size):
    return pl.ds(pl.multiple_of(jnp.bitwise_xor(t, k) * size, size), size)


def norm(vector, gain):
    return vector * lax.rsqrt(jnp.mean(vector * vector, axis=-1, keepdims=True) + epsilon) * gain


def total_of(value):
    return jnp.sum(jnp.sum(value, axis=0, keepdims=True), axis=1, keepdims=True)


def offset_buckets(offsets):
    distance = np.abs(offsets)
    far = np.full(offsets.shape, 8, np.int32)
    for edge_value in bucket_edges:
        far = far + (distance >= edge_value)
    return np.where(distance < 8, distance, far) + np.where(offsets > 0, 16, 0)


def diagonal_one_hot():
    lane = np.arange(2 * BAND)
    y = np.where(lane < BAND, lane, lane - 2 * BAND)
    offsets = BAND * (np.arange(DIAGS)[:, None] - 2) - y[None, :]
    hot = offset_buckets(offsets)[:, :, None] == np.arange(BUCKETS)
    hot = hot & (lane != BAND)[None, :, None]
    return hot.astype(np.float32)


def prepare_body(layer, place, own_gain, other_gain, own_table, other_table, hot, valid_ref, *refs):
    s = place[1]
    refs = refs[-5:] if layer == 0 else refs[-3:]
    gain_ref, tile_ref = refs[:2]
    heads = own_table.shape[0]
    own = s == layer
    gain_ref[...] = jnp.where(own, own_gain[...], other_gain[...])
    table = jnp.where(own, own_table[...], other_table[...])
    table = table - table[:, far_bucket_behind : far_bucket_behind + 1]
    by_offset = lax.dot_general(
        table,
        hot[...],
        (((1,), (0,)), ((), ())),
        precision=lax.Precision.HIGHEST,
        preferred_element_type=F32,
    )
    for h in range(heads):
        for d in range(DIAGS):
            row = by_offset[h : h + 1, d * 2 * BAND : (d + 1) * 2 * BAND]
            tile_ref[h * DIAGS + d] = pltpu.roll(
                jnp.broadcast_to(row, (BAND, 2 * BAND)), 0, 1, stride=1, stride_axis=0
            )[:, :BAND]
    if layer == 0:
        key_ref, own_ref, scratch = refs[2], refs[3], refs[4]
        rows = own_ref.shape[0]
        valid = jnp.where(s == 0, valid_ref[0:1, :], valid_ref[1:2, :]).astype(F32)
        column = jnp.broadcast_to(valid, (128, SEQ)).T[:, :1]
        scratch[...] = column
        key_ref[...] = jnp.where(column > 0, 0.0, masked_score)
        own_ref[...] = scratch[pl.ds(pl.multiple_of(place[0] * rows, rows), rows), :]


def prepare(layer, place, gains, tables, hot, valid, rows):
    outs = [shape((2, D), F32), shape((tables[0].shape[0] * DIAGS, BAND, BAND), F32)]
    if layer == 0:
        outs += [shape((SEQ, 1), F32), shape((rows, 1), F32)]
    return pl.pallas_call(
        functools.partial(prepare_body, layer),
        out_shape=outs,
        in_specs=[smem()] + vm(6),
        out_specs=vm(len(outs)),
        scratch_shapes=[pltpu.VMEM((SEQ, 1), F32)],
        compiler_params=limit(16),
        cost_estimate=cost(1e6, 1e5),
        name="prepare",
    )(place, *gains, *tables, hot, valid)


def targets_body(parts, place, own_route, other_route, own_router, other_router, *outs):
    row_refs, col_refs, router_refs, scratch = outs[:2], outs[2:4], outs[4:6], outs[6]
    t, s = place[0], place[1]
    rows = SEQ // parts
    before = lax.broadcasted_iota(jnp.int32, (SEQ, SEQ), 0)
    upto = (before <= lax.broadcasted_iota(jnp.int32, (SEQ, SEQ), 1)).astype(BF)
    expert = lax.broadcasted_iota(jnp.int32, (8, SEQ), 0)
    for layer in range(2):
        own = s == layer
        route = jnp.where(own, own_route[...], other_route[...])
        route = jnp.where(s == 0, route[0:1, :], route[1:2, :])
        hit = route == expert
        count = dot(hit.astype(BF), upto)
        slot = jnp.where(hit, count - 1.0 + (expert * CAP).astype(F32), 0.0)
        scratch[...] = jnp.sum(slot, axis=0, keepdims=True)
        for k in range(parts):
            row_refs[layer][:, k * rows : (k + 1) * rows] = scratch[:, natural(t, k, rows)].astype(
                jnp.int32
            )
        scratch[...] = row_refs[layer][...].astype(F32)
        turned = jnp.broadcast_to(scratch[...], (128, SEQ)).T
        col_refs[layer][...] = turned[:, :1].astype(jnp.int32)
        router_refs[layer][...] = jnp.zeros_like(router_refs[layer])
        router_refs[layer][:EXPERTS, :] = jnp.where(
            own, own_router[...].astype(F32), other_router[...].astype(F32)
        ).astype(BF)


def make_targets(place, routes, routers, parts):
    row, col = shape((1, SEQ), jnp.int32), shape((SEQ, 1), jnp.int32)
    router = shape((128, D), BF)
    return pl.pallas_call(
        functools.partial(targets_body, parts),
        out_shape=[row, row, col, col, router, router],
        in_specs=[smem()] + vm(4),
        out_specs=vm(6),
        scratch_shapes=[pltpu.VMEM((1, SEQ), F32)],
        compiler_params=limit(16),
        cost_estimate=cost(1e6, 1e5),
        name="make_targets",
    )(place, *routes, *routers)


def near_bias(tiles_ref, h, skip, width):
    first, last = skip // BAND, (skip + width) // BAND
    columns = [
        jnp.concatenate([tiles_ref[h * DIAGS + i - j + 1] for i in range(first, last)], axis=0)
        for j in range(QB // BAND)
    ]
    return jnp.concatenate(columns, axis=1)


def block_range(j):
    last = min(SEQ, QB * (j + 2))
    left = max(0, QB * j - BAND)
    return left, last, left - (QB * j - BAND)


def fill_mask(mask_ref, valid_ref, s0, s1, j):
    left, last, _ = block_range(j)
    width = last - left
    key = left + lax.broadcasted_iota(jnp.int32, (width, 1), 0)
    query = QB * j + lax.broadcasted_iota(jnp.int32, (1, QB), 1)

    def label(position, outside):
        second = jnp.where((position >= s1) & (position < s1 + PIECE), 1, outside)
        return jnp.where((position >= s0) & (position < s0 + PIECE), 0, second)

    allowed = (key <= query) | (label(key, -1) == label(query, -2))
    mask_ref[:width, :] = jnp.where(allowed, valid_ref[left:last, :], masked_score)


def fwd_attention_body(parts, norm_inside, *refs):
    place, starts, valid_col, gain, w_own, w_other, tiles_ref = refs[:7]
    x_refs = refs[7 : 7 + parts]
    xn_out, qkv_out, turned_out, lse_ref = refs[7 + parts : 11 + parts]
    out_refs = refs[11 + parts : 11 + 2 * parts]
    w_ref, xn_ref, qkv_ref, turned_ref, vt_ref, att_ref, mask_ref, valid_ref, sems = refs[
        11 + 2 * parts :
    ]
    t, s = place[0], place[1]
    s0, s1 = starts[s, 0], starts[s, 1]
    rows = SEQ // parts
    heads = qkv_ref.shape[1]
    wide = heads * HEAD_DIM

    choose(place[2], w_own, w_other, w_ref)
    valid_ref[...] = jnp.broadcast_to(valid_col[...], (SEQ, QB))
    for k in range(parts):
        where = natural(t, k, rows)
        x = x_refs[k][...]
        if norm_inside:
            x = norm(x.astype(F32), gain[0:1, :]).astype(BF)
        xn_ref[where, :] = x
        projected = dot(x, w_ref[...], 1, 1)
        for i in range(3):
            product = projected[:, i * wide : (i + 1) * wide]
            if i == 0:
                product = product * HEAD_DIM**-0.5
            turned = product.T.astype(BF)
            if i < 2:
                turned_ref[i, :, where] = turned
            else:
                vt_ref[:, where] = turned
            product = product.astype(BF)
            for h in range(heads):
                qkv_ref[i, h, where, :] = product[:, h * HEAD_DIM : (h + 1) * HEAD_DIM]

    copies = [
        pltpu.make_async_copy(a, b, sems.at[i])
        for i, (a, b) in enumerate(
            ((xn_ref, xn_out), (qkv_ref, qkv_out), (turned_ref, turned_out))
        )
    ]
    for copy in copies:
        copy.start()

    for j in range(SEQ // QB):
        left, last, skip = block_range(j)
        width = last - left
        columns = slice(j * QB, (j + 1) * QB)
        fill_mask(mask_ref, valid_ref, s0, s1, j)

        def one_head(h, carry):
            lanes = pl.ds(pl.multiple_of(h * HEAD_DIM, HEAD_DIM), HEAD_DIM)
            scores = dot(qkv_ref[1, h, :last, :], turned_ref[0, lanes, columns])
            near = scores[left:] + near_bias(tiles_ref, h, skip, width) + mask_ref[:width, :]
            highest = jnp.max(near, axis=0, keepdims=True)
            if left:
                far = scores[:left] + valid_ref[:left, :]
                highest = jnp.maximum(highest, jnp.max(far, axis=0, keepdims=True))
            near = jnp.exp(near - highest)
            total = jnp.sum(near, axis=0, keepdims=True)
            out = dot(vt_ref[lanes, left:last], near.astype(BF))
            if left:
                far = jnp.exp(far - highest)
                total = total + jnp.sum(far, axis=0, keepdims=True)
                out = out + dot(vt_ref[lanes, :left], far.astype(BF))
            lse_ref[h, :, columns] = highest + jnp.log(total)
            att_ref[lanes, columns] = (out * (1.0 / total)).astype(BF)
            return carry

        lax.fori_loop(0, heads, one_head, 0)

    for k in range(parts):
        out_refs[k][...] = att_ref[:, natural(t, k, rows)]
    for copy in copies:
        copy.wait()


def fwd_attention(place, starts, valid_col, gain, w_pair, tiles, x_parts, norm_inside):
    parts = len(x_parts)
    rows = SEQ // parts
    wide = w_pair[0].shape[0] // 3
    heads = wide // HEAD_DIM
    kept = [
        shape((SEQ, D), BF),
        shape((3, heads, SEQ, HEAD_DIM), BF),
        shape((2, wide, SEQ), BF),
    ]
    outs = pl.pallas_call(
        functools.partial(fwd_attention_body, parts, norm_inside),
        out_shape=[in_hbm(a.shape, a.dtype) for a in kept]
        + [shape((heads, 1, SEQ), F32)] + [shape((wide, rows), BF)] * parts,
        in_specs=[smem()] * 2 + vm(5 + parts),
        out_specs=any_space(3) + vm(1 + parts),
        scratch_shapes=[pltpu.VMEM((3 * wide, D), BF)]
        + [pltpu.VMEM(a.shape, a.dtype) for a in kept]
        + [
            pltpu.VMEM((wide, SEQ), BF),
            pltpu.VMEM((wide, SEQ), BF),
            pltpu.VMEM((WIDE, QB), F32),
            pltpu.VMEM((SEQ, QB), F32),
            pltpu.SemaphoreType.DMA((3,)),
        ],
        compiler_params=limit(32),
        cost_estimate=cost(9e9, 1e7),
        name="fwd_attention",
    )(place, starts, valid_col, gain, *[from_hbm(a) for a in (*w_pair, tiles)], *x_parts)
    return outs[:4], list(outs[4:])


def bwd_attention_body(parts, *refs):
    place, starts, valid_col, gain, w_own, w_other, tiles_ref, xn_ref = refs[:8]
    qkv_ref, turned_ref, lse_ref = refs[8:11]
    d_refs = refs[11 : 11 + parts]
    refs = refs[11 + parts :]
    proj_ref, sum_ref, far_ref, gain_ref = refs[:4]
    out_refs = refs[4 : 4 + parts]
    w_ref, d_ref, dt_ref, dq_ref, dk_ref, dv_ref, mask_ref, valid_ref = refs[4 + parts :]
    t, s = place[0], place[1]
    s0, s1 = starts[s, 0], starts[s, 1]
    rows = SEQ // parts
    heads = qkv_ref.shape[1]

    choose(place[2], w_own, w_other, w_ref)
    valid_ref[...] = jnp.broadcast_to(valid_col[...], (SEQ, QB))
    for k in range(parts):
        where = natural(t, k, rows)
        block = d_refs[k][...]
        dt_ref[:, where] = block.astype(F32).T.astype(BF)
        for h in range(heads):
            d_ref[h, where, :] = block[:, h * HEAD_DIM : (h + 1) * HEAD_DIM]
    dk_ref[...] = jnp.zeros_like(dk_ref)
    dv_ref[...] = jnp.zeros_like(dv_ref)
    sum_ref[...] = jnp.zeros_like(sum_ref)
    far_ref[...] = jnp.zeros_like(far_ref)

    for j in range(SEQ // QB):
        left, last, skip = block_range(j)
        width = last - left
        columns = slice(j * QB, (j + 1) * QB)
        fill_mask(mask_ref, valid_ref, s0, s1, j)

        def one_head(h, carry):
            lanes = pl.ds(pl.multiple_of(h * HEAD_DIM, HEAD_DIM), HEAD_DIM)
            q_block = qkv_ref[0, h, columns, :]
            d_block = d_ref[h, columns, :]
            lse = lse_ref[h, :, columns]
            scores = dot(qkv_ref[1, h, :last, :], turned_ref[0, lanes, columns])
            slopes = dot(qkv_ref[2, h, :last, :], dt_ref[lanes, columns])
            near = scores[left:] + near_bias(tiles_ref, h, skip, width) + mask_ref[:width, :]
            near = jnp.exp(near - lse)
            near_slope = near * slopes[left:]
            row_dot = jnp.sum(near_slope, axis=0, keepdims=True)
            if left:
                far = jnp.exp(scores[:left] + valid_ref[:left, :] - lse)
                far_slope = far * slopes[:left]
                row_dot = row_dot + jnp.sum(far_slope, axis=0, keepdims=True)
            near_slope = near_slope - near * row_dot
            for i in range(width // BAND):
                for c in range(QB // BAND):
                    sum_ref[h * DIAGS + skip // BAND + i - c + 1] += near_slope[
                        i * BAND : (i + 1) * BAND, c * BAND : (c + 1) * BAND
                    ]
            near_slope = near_slope.astype(BF)
            dk_ref[h, left:last, :] += dot(near_slope, q_block)
            dv_ref[h, left:last, :] += dot(near.astype(BF), d_block)
            dq = dot(turned_ref[1, lanes, left:last], near_slope)
            if left:
                far_slope = far_slope - far * row_dot
                far_ref[h] += jnp.sum(far_slope.reshape(left // 8, 8, QB), axis=0)
                far_slope = far_slope.astype(BF)
                dk_ref[h, :left, :] += dot(far_slope, q_block)
                dv_ref[h, :left, :] += dot(far.astype(BF), d_block)
                dq = dq + dot(turned_ref[1, lanes, :left], far_slope)
            dq_ref[lanes, columns] = dq * HEAD_DIM**-0.5
            return carry

        lax.fori_loop(0, heads, one_head, 0, unroll=True)

    for first in range(0, SEQ, rows):
        where = slice(first, first + rows)
        blocks = [dq_ref[:, where].T.astype(BF)]
        for source in (dk_ref, dv_ref):
            blocks += [source[h, where, :].astype(BF) for h in range(heads)]
        proj_ref[where, :] = jnp.concatenate(blocks, axis=1)
    gain_sum = jnp.zeros((1, D), F32)
    for k in range(parts):
        where = natural(t, k, rows)
        total = dot(proj_ref[where, :], w_ref[...])
        out_refs[k][...] = total.astype(BF)
        gain_sum = gain_sum + jnp.sum(total * xn_ref[where, :].astype(F32), axis=0, keepdims=True)
    gain_ref[...] = gain_sum / gain[0:1, :]


def bwd_attention(place, starts, valid_col, gain, w_pair, tiles, saved, d_parts):
    parts = len(d_parts)
    rows = SEQ // parts
    wide = w_pair[0].shape[0] // 3
    heads = wide // HEAD_DIM
    outs = pl.pallas_call(
        functools.partial(bwd_attention_body, parts),
        out_shape=[
            in_hbm((SEQ, 3 * wide), BF),
            in_hbm((heads * DIAGS, BAND, BAND), F32),
            shape((heads, 8, QB), F32),
            shape((1, D), F32),
        ]
        + [in_hbm((rows, D), BF)] * parts,
        in_specs=[smem()] * 2 + vm(9 + parts),
        out_specs=vm(4 + parts),
        scratch_shapes=[
            pltpu.VMEM((3 * wide, D), BF),
            pltpu.VMEM((heads, SEQ, HEAD_DIM), BF),
            pltpu.VMEM((wide, SEQ), BF),
            pltpu.VMEM((wide, SEQ), F32),
            pltpu.VMEM((heads, SEQ, HEAD_DIM), F32),
            pltpu.VMEM((heads, SEQ, HEAD_DIM), F32),
            pltpu.VMEM((WIDE, QB), F32),
            pltpu.VMEM((SEQ, QB), F32),
        ],
        compiler_params=limit(36),
        cost_estimate=cost(1.8e10, 1e7),
        name="bwd_attention",
    )(
        place,
        starts,
        valid_col,
        gain,
        *w_pair,
        tiles,
        *saved,
        *d_parts,
    )
    return outs[:4], list(outs[4:])


def small_sums_body(paired, place, tiles_ref, far_ref, hot, gain_in, gain_mid, router, *refs):
    stats, refs = refs[:2], refs[2:]
    heads = far_ref.shape[0]
    row = lax.broadcasted_iota(jnp.int32, (BAND, BAND), 0)
    column = lax.broadcasted_iota(jnp.int32, (BAND, BAND), 1)
    flip = (row + column == BAND - 1).astype(F32)
    out = refs[-1]
    out[...] = jnp.zeros_like(out)
    out[0:1, :] = gain_in[...]
    out[1:2, :] = gain_mid[...]
    out[2 : 2 + EXPERTS, :] = router[:EXPERTS, :]
    out[6:7, :128] = stats[0][...] + stats[1][...]
    by_offset = []
    for h in range(heads):
        sums = []
        for d in range(DIAGS):
            tile = lax.dot_general(
                flip,
                tiles_ref[h * DIAGS + d],
                (((1,), (0,)), ((), ())),
                precision=lax.Precision.HIGHEST,
                preferred_element_type=F32,
            )
            tile = jnp.concatenate([tile, jnp.zeros_like(tile)], axis=1)
            tile = pltpu.roll(tile, BAND + 1, 1, stride=1, stride_axis=0)
            sums.append(jnp.sum(tile, axis=0, keepdims=True))
        by_offset.append(jnp.concatenate(sums, axis=1))
    table = lax.dot_general(
        jnp.concatenate(by_offset, axis=0),
        hot[...],
        (((1,), (1,)), ((), ())),
        precision=lax.Precision.HIGHEST,
        preferred_element_type=F32,
    )
    bucket = lax.broadcasted_iota(jnp.int32, (1, BUCKETS), 1)
    for h in range(heads):
        behind = jnp.where(bucket == far_bucket_behind, total_of(far_ref[h]), 0.0)
        out[8 + h : 9 + h, :BUCKETS] = table[h : h + 1, :] + behind
    if paired:
        other, keep, sent = refs[:3]
        first = place[1] == 0
        keep[...] = jnp.where(first, out[...], other[...])
        sent[...] = jnp.where(first, other[...], out[...])


def small_sums(place, tiles, far, hot, gain_in, gain_mid, router, stats, other):
    paired = other is not None
    array = shape((16, D), F32)
    outs = pl.pallas_call(
        functools.partial(small_sums_body, paired),
        out_shape=[array] * (2 if paired else 1),
        in_specs=[smem()] + vm(8 + paired),
        out_specs=vm(2 if paired else 1),
        scratch_shapes=[pltpu.VMEM((16, D), F32)] if paired else [],
        compiler_params=limit(16),
        cost_estimate=cost(1e6, 1e5),
        name="small_sums",
    )(place, from_hbm(tiles), far, hot, gain_in, gain_mid, router, *stats, *([other] if paired else []))
    return outs if paired else outs[0]


def combine(parts, rows, target_col, slots_ref, out_refs):
    slot = lax.broadcasted_iota(jnp.int32, (rows, SLOTS), 1)
    for k in list(range(1, parts)) + [0]:
        hot = (target_col[k * rows : (k + 1) * rows, :] == slot).astype(BF)
        out_refs[k][...] = dot(hot, slots_ref[...]).astype(BF)


def dispatch(e, target_row, tokens_ref):
    slot = e * CAP + lax.broadcasted_iota(jnp.int32, (CAP, SEQ), 0)
    return dot((target_row[...] == slot).astype(BF), tokens_ref[...]).astype(BF)


HALF = EXPERTS // 2


def fwd_experts_body(parts, *refs):
    sel, order, target_row, target_col, router, up_own, up_other, down_own, down_other = refs[:9]
    x_refs = refs[9 : 9 + parts]
    half_ref, slope_ref, gate_ref, probs_ref = refs[9 + parts : 13 + parts]
    out_refs = refs[13 + parts : 13 + 2 * parts]
    x_ref, slots_ref = refs[13 + 2 * parts :]
    rows = SEQ // parts
    step = pl.program_id(0)
    e = order[step]

    @pl.when(step == 0)
    def _():
        lane = lax.broadcasted_iota(jnp.int32, (rows, 128), 1)
        for k in range(parts):
            where = slice(k * rows, (k + 1) * rows)
            x = x_refs[k][...]
            x_ref[where, :] = x
            logits = jnp.where(lane < EXPERTS, dot(x, router[...], 1, 1), -1e30)
            probs = jnp.exp(logits - jnp.max(logits, axis=-1, keepdims=True))
            probs = probs / jnp.sum(probs, axis=-1, keepdims=True)
            target = target_col[where, :]
            hit = (target >= lane * CAP) & (target < lane * CAP + CAP)
            gate_ref[where, :] = jnp.sum(jnp.where(hit, probs, 0.0), axis=-1, keepdims=True)
            if k == 0:
                probs_ref[...] = probs

    def one_expert(up_ref, down_ref):
        expert_in = dispatch(e, target_row, x_ref)
        half_ref[0, 1] = expert_in
        up = dot(expert_in, up_ref[0])
        inner = np.sqrt(2 / np.pi).astype(np.float32)
        square = up * up
        bend = jnp.tanh(inner * (up * (1.0 + 0.044715 * square)))
        half = 0.5 * (1.0 + bend)
        act = (up * half).astype(BF)
        half_ref[0, 0] = act
        slope_ref[0] = half + 0.5 * up * (1.0 - bend * bend) * (
            inner * (1.0 + 3 * 0.044715 * square)
        )
        slots_ref[pl.ds(pl.multiple_of(e * CAP, CAP), CAP), :] = dot(act, down_ref[0]).astype(BF)

    either(sel[0], one_expert, (up_own, down_own), (up_other, down_other))

    @pl.when(step == EXPERTS - 1)
    def _():
        combine(parts, rows, target_col, slots_ref, out_refs)


def expert_specs(block):
    own = pl.BlockSpec(block, lambda i, sel, order: (order[i] * (1 - sel[0]), 0, 0))
    other = pl.BlockSpec(block, lambda i, sel, order: (order[i] * sel[0], 0, 0))
    return [own, other]


def half_spec(columns):
    return pl.BlockSpec((1, 2, CAP, columns), lambda i, sel, order: (i, 0, 0, 0))


def whole(dims):
    return pl.BlockSpec(dims, lambda i, sel, order: (0,) * len(dims))


def fwd_experts(select, order, target_row, target_col, router, up_pair, down_pair, x_parts):
    parts = len(x_parts)
    rows = SEQ // parts
    hidden = up_pair[0].shape[2]
    each_hidden = pl.BlockSpec((1, CAP, hidden), lambda i, sel, order: (i, 0, 0))
    outs = pl.pallas_call(
        functools.partial(fwd_experts_body, parts),
        grid_spec=pltpu.PrefetchScalarGridSpec(
            num_scalar_prefetch=2,
            grid=(EXPERTS,),
            in_specs=[whole((1, SEQ)), whole((SEQ, 1)), whole((128, D))]
            + expert_specs((1, D, hidden))
            + expert_specs((1, hidden, D))
            + [whole((rows, D))] * parts,
            out_specs=[half_spec(D)]
            + [each_hidden, whole((SEQ, 1)), whole((rows, 128))]
            + [whole((rows, D))] * parts,
            scratch_shapes=[
                pltpu.VMEM((SEQ, D), BF),
                pltpu.VMEM((SLOTS, D), BF),
            ],
        ),
        out_shape=[in_hbm((EXPERTS, 2, CAP, D), BF)]
        + [
            in_hbm((EXPERTS, CAP, hidden), F32),
            shape((SEQ, 1), F32),
            shape((rows, 128), F32),
        ]
        + [shape((rows, D), BF)] * parts,
        compiler_params=limit(36),
        cost_estimate=cost(1.2e10, 3e7),
        name="fwd_experts",
    )(
        select,
        order,
        target_row,
        target_col,
        router,
        *[from_hbm(a) for a in (*up_pair, *down_pair)],
        *x_parts,
    )
    return outs[:4], list(outs[4:])


def bwd_experts_body(parts, *refs):
    sel, order, target_row, target_col, gate, slope_ref = refs[:6]
    up_own, up_other, down_own, down_other = refs[6:10]
    g_refs = refs[10 : 10 + parts]
    refs = refs[10 + parts :]
    half_ref = refs[0]
    out_refs = refs[1 : 1 + parts]
    g_ref, slots_ref = refs[1 + parts :]
    rows = SEQ // parts
    step = pl.program_id(0)
    e = order[step]

    @pl.when(step == 0)
    def _():
        for k in range(parts):
            where = slice(k * rows, (k + 1) * rows)
            g_ref[where, :] = (gate[where, :] * g_refs[k][...].astype(F32)).astype(BF)

    def one_expert(up_ref, down_ref):
        d_out = dispatch(e, target_row, g_ref)
        half_ref[0, 0] = d_out
        d_up = (slope_ref[0] * dot(d_out, down_ref[0], 1, 1)).astype(BF)
        half_ref[0, 1] = d_up
        slots_ref[pl.ds(pl.multiple_of(e * CAP, CAP), CAP), :] = dot(d_up, up_ref[0], 1, 1).astype(
            BF
        )

    either(sel[0], one_expert, (up_own, down_own), (up_other, down_other))

    @pl.when(step == EXPERTS - 1)
    def _():
        combine(parts, rows, target_col, slots_ref, out_refs)


def bwd_experts(select, order, target_row, target_col, gate, slope, up_pair, down_pair, g_parts):
    parts = len(g_parts)
    rows = SEQ // parts
    hidden = up_pair[0].shape[2]
    each_hidden = pl.BlockSpec((1, CAP, hidden), lambda i, sel, order: (i, 0, 0))
    outs = pl.pallas_call(
        functools.partial(bwd_experts_body, parts),
        grid_spec=pltpu.PrefetchScalarGridSpec(
            num_scalar_prefetch=2,
            grid=(EXPERTS,),
            in_specs=[whole((1, SEQ)), whole((SEQ, 1)), whole((SEQ, 1)), each_hidden]
            + expert_specs((1, D, hidden))
            + expert_specs((1, hidden, D))
            + [whole((rows, D))] * parts,
            out_specs=[half_spec(D)] + [whole((rows, D))] * parts,
            scratch_shapes=[
                pltpu.VMEM((SEQ, D), BF),
                pltpu.VMEM((SLOTS, D), BF),
            ],
        ),
        out_shape=[in_hbm((EXPERTS, 2, CAP, D), BF)] + [shape((rows, D), BF)] * parts,
        compiler_params=limit(36),
        cost_estimate=cost(1.2e10, 3e7),
        name="bwd_experts",
    )(
        select,
        order,
        target_row,
        target_col,
        gate,
        *[from_hbm(a) for a in (slope, *up_pair, *down_pair)],
        *g_parts,
    )
    return outs[0], list(outs[1:])


def norm_back(vector, gain, grad):
    scale = lax.rsqrt(jnp.mean(vector * vector, axis=-1, keepdims=True) + epsilon)
    unit = vector * scale
    scaled = grad * gain
    inner = jnp.mean(unit * scaled, axis=-1, keepdims=True)
    return scale * (scaled - unit * inner), grad * unit


def after_attention_body(parts, *refs):
    h_ref, gain, valid = refs[:3]
    p_refs, w_refs = refs[3 : 3 + parts], refs[3 + parts : 3 + 2 * parts]
    mid_ref, xn_ref, stat_ref = refs[3 + 2 * parts :]
    branch = dot(p_refs[0][...], w_refs[0][...], 0, 0)
    for k in range(1, parts):
        branch = branch + dot(p_refs[k][...], w_refs[k][...], 0, 0)
    h = h_ref[...].astype(F32)
    mid = h + branch
    mid_ref[...] = mid
    xn_ref[...] = norm(mid, gain[1:2, :]).astype(BF)
    weight = valid[...]
    lane = lax.broadcasted_iota(jnp.int32, (1, 128), 1)
    sums = jnp.where(lane == 0, total_of(weight * h * h), 0.0)
    sums = jnp.where(lane == 1, total_of(weight * branch * branch), sums)
    stat_ref[...] = jnp.where(lane == 3, total_of(weight), sums)


def after_attention(h, gain, valid, pieces, w_parts):
    parts = len(pieces)
    rows = h.shape[0]
    return pl.pallas_call(
        functools.partial(after_attention_body, parts),
        out_shape=[shape((rows, D), F32), shape((rows, D), BF), shape((1, 128), F32)],
        in_specs=vm(3 + 2 * parts),
        out_specs=vm(3),
        compiler_params=limit(24),
        cost_estimate=cost(2e9, 4e6),
        name="after_attention",
    )(h, gain, valid, *pieces, *w_parts)


def after_experts_body(parts, *refs):
    mid_ref, gate, gain, valid = refs[:4]
    y_refs = refs[4 : 4 + parts]
    comb_ref, out_ref, xn_ref, stat_ref = refs[4 + parts :]
    total = y_refs[0][...].astype(F32)
    for k in range(1, parts):
        total = total + y_refs[k][...].astype(F32)
    combined = total.astype(BF)
    comb_ref[...] = combined
    branch = gate[: mid_ref.shape[0], :] * combined.astype(F32)
    out = (mid_ref[...] + branch).astype(BF)
    out_ref[...] = out
    xn_ref[...] = norm(out.astype(F32), gain[0:1, :]).astype(BF)
    lane = lax.broadcasted_iota(jnp.int32, (1, 128), 1)
    stat_ref[...] = jnp.where(lane == 2, total_of(valid[...] * branch * branch), 0.0)


def after_experts(mid, gate, gain, valid, y_parts):
    parts = len(y_parts)
    rows = mid.shape[0]
    return pl.pallas_call(
        functools.partial(after_experts_body, parts),
        out_shape=[shape((rows, D), BF)] * 3 + [shape((1, 128), F32)],
        in_specs=vm(4 + parts),
        out_specs=vm(4),
        compiler_params=limit(24),
        cost_estimate=cost(1e8, 4e6),
        name="after_experts",
    )(mid, gate, gain, valid, *y_parts)


def middle_back_body(parts, *refs):
    g_ref, comb_ref, probs_ref, target_col, router, mid_ref, gain, xn_ref = refs[:8]
    y_refs, w_refs = refs[8 : 8 + parts], refs[8 + parts : 8 + 2 * parts]
    refs = refs[8 + 2 * parts :]
    dmid_ref, da_ref, gain_ref, router_ref = refs[:4]
    out_refs = refs[4:]
    rows = g_ref.shape[0]
    g = g_ref[...].astype(F32)
    total = y_refs[0][...].astype(F32)
    for k in range(1, parts):
        total = total + y_refs[k][...].astype(F32)
    d_in = total.astype(BF).astype(F32)
    d_gate = jnp.sum(g * comb_ref[...].astype(F32), axis=-1, keepdims=True)
    lane = lax.broadcasted_iota(jnp.int32, (rows, 128), 1)
    target = target_col[:rows, :]
    hit = (target >= lane * CAP) & (target < lane * CAP + CAP)
    probs = probs_ref[...]
    chosen = jnp.where(hit, d_gate, 0.0)
    inner = jnp.sum(probs * chosen, axis=-1, keepdims=True)
    d_logits = (probs * (chosen - inner)).astype(BF)
    router_ref[...] = dot(d_logits, xn_ref[...], 0, 0)[:8]
    d_xn = d_in + dot(d_logits, router[...])
    d_norm, d_gain = norm_back(mid_ref[...], gain[1:2, :], d_xn)
    gain_ref[...] = jnp.sum(d_gain, axis=0, keepdims=True)
    d_mid = g + d_norm
    dmid_ref[...] = d_mid
    d_a = d_mid.astype(BF)
    da_ref[...] = d_a
    for k in list(range(1, parts)) + [0]:
        out_refs[k][...] = dot(d_a, w_refs[k][...], 1, 1).astype(BF)


def middle_back(g, combined, probs, target_col, router, mid, gain, xn, y_parts, w_parts):
    parts = len(y_parts)
    rows = g.shape[0]
    wide = w_parts[0].shape[0]
    outs = pl.pallas_call(
        functools.partial(middle_back_body, parts),
        out_shape=[shape((rows, D), F32), shape((rows, D), BF), shape((1, D), F32)]
        + [shape((8, D), F32)]
        + [shape((rows, wide), BF)] * parts,
        in_specs=vm(8 + 2 * parts),
        out_specs=vm(4 + parts),
        compiler_params=limit(24),
        cost_estimate=cost(2e9, 6e6),
        name="middle_back",
    )(
        *[
            from_hbm(a)
            for a in (
                g,
                combined,
                probs,
                target_col,
                router,
                mid,
                gain,
                xn,
                *y_parts,
                *w_parts,
            )
        ]
    )
    return outs[:4], list(outs[4:])


def input_back_body(parts, *refs):
    dmid_ref, h_ref, gain = refs[:3]
    y_refs = refs[3 : 3 + parts]
    wide_ref, low_ref = refs[3 + parts :]
    total = y_refs[0][...].astype(F32)
    for k in range(1, parts):
        total = total + y_refs[k][...].astype(F32)
    d_h = dmid_ref[...] + norm_back(h_ref[...].astype(F32), gain[0:1, :], total)[0]
    wide_ref[...] = d_h
    low_ref[...] = d_h.astype(BF)


def input_back(d_mid, h, gain, y_parts):
    parts = len(y_parts)
    rows = h.shape[0]
    return pl.pallas_call(
        functools.partial(input_back_body, parts),
        out_shape=[shape((rows, D), F32), shape((rows, D), BF)],
        in_specs=vm(3 + parts),
        out_specs=vm(2),
        compiler_params=limit(24),
        cost_estimate=cost(1e8, 4e6),
        name="input_back",
    )(d_mid, h, gain, *y_parts)


def expert_grads_body(fwd_own, fwd_other, bwd_own, bwd_other, out):
    for kind in range(2):
        left = jnp.concatenate([fwd_own[0, kind], fwd_other[0, kind]], axis=0)
        right = jnp.concatenate([bwd_own[0, kind], bwd_other[0, kind]], axis=0)
        out[kind, 0] = dot(left, right, 0, 0).astype(BF)


def expert_grads(values):
    columns = values[0].shape[3]
    block = (1, 2, CAP, columns)
    own = pl.BlockSpec(block, lambda i: (i + HALF, 0, 0, 0))
    other = pl.BlockSpec(block, lambda i: (i, 0, 0, 0))
    outs = pl.pallas_call(
        expert_grads_body,
        grid=(HALF,),
        in_specs=[own, other, own, other],
        out_specs=pl.BlockSpec((2, 1, columns, columns), lambda i: (0, i, 0, 0)),
        out_shape=in_hbm((2, HALF, columns, columns), BF),
        compiler_params=limit(28),
        cost_estimate=cost(1e6, 1e5),
        name="expert_grads",
    )(from_hbm(values[0]), from_hbm(values[1]), from_hbm(values[2]), values[3])
    return outs.reshape(2 * HALF, columns, columns)


def out_grads_body(parts, *refs):
    pieces, d_a, outs = refs[:parts], refs[parts], refs[parts + 1 :]
    for k in list(range(1, parts)) + [0]:
        outs[k][...] = dot(pieces[k][...], d_a[...]).astype(BF)


def out_grads(pieces, d_a):
    parts = len(pieces)
    wide = pieces[0].shape[0]
    return pl.pallas_call(
        functools.partial(out_grads_body, parts),
        out_shape=[shape((wide, D), BF)] * parts,
        in_specs=vm(parts + 1),
        out_specs=vm(parts),
        compiler_params=limit(16),
        cost_estimate=cost(1e6, 1e5),
        name="out_grads",
    )(*pieces, d_a)


def attention_grads_body(parts, chunks, place, xn_ref, proj_ref, *refs):
    terms, (send_ref, keep_ref, out) = refs[:parts], refs[parts:]
    wide = terms[0].shape[0]
    rows, taken = D // chunks, wide // chunks
    out[:, : 3 * wide] = dot(xn_ref[...], proj_ref[...], 0, 0)
    total = terms[0][...].astype(F32)
    for k in range(1, parts):
        total = total + terms[k][...].astype(F32)
    for c in range(chunks):
        for b in range(D // wide):
            out[c * rows + b * taken : c * rows + (b + 1) * taken, 3 * wide :] = total[
                c * taken : (c + 1) * taken, b * wide : (b + 1) * wide
            ]
    first = place[1] == 0
    half = D // 2
    left, right = out[:, :half], out[:, half:]
    keep_ref[:, :half] = jnp.where(first, left, right).astype(BF)
    send_ref[:, :half] = jnp.where(first, right, left).astype(BF)


def attention_grads(place, xn, proj, terms):
    parts = len(terms)
    return pl.pallas_call(
        functools.partial(attention_grads_body, parts, lax.axis_size("dp")),
        out_shape=[shape((D, D // 2), BF)] * 2,
        in_specs=[smem()] + vm(2 + parts),
        out_specs=vm(2),
        scratch_shapes=[pltpu.VMEM((D, D), F32)],
        compiler_params=limit(24),
        cost_estimate=cost(1e6, 1e5),
        name="attention_grads",
    )(place, from_hbm(xn), from_hbm(proj), *terms)


def chunks_body(count, place, own, received, *outs):
    rows = outs[0].shape[0]
    for k in range(count):
        where = natural(place[3], k, rows)
        total = own[where, :].astype(F32) + received[where, :].astype(F32)
        outs[k][...] = total.astype(outs[k].dtype)


def scatter_small(place, own, received):
    count = lax.axis_size("dp")
    if count != 4:
        total = (own.astype(F32) + received.astype(F32)).astype(BF)
        return [total]
    dims = (own.shape[0] // count, own.shape[1])
    return pl.pallas_call(
        functools.partial(chunks_body, count),
        out_shape=[shape(dims, F32)] + [shape(dims, BF)] * (count - 1),
        in_specs=[smem()] + vm(2),
        out_specs=vm(count),
        compiler_params=limit(16),
        cost_estimate=cost(1e6, 1e5),
        name="chunks",
    )(place, own, received)


def scatter_move(chunks):
    return [chunks[0]] + [exchange(chunk, "dp", k) for k, chunk in enumerate(chunks) if k]


def scatter_total(chunks):
    if len(chunks) == 1:
        return lax.psum_scatter(chunks[0], "dp", scatter_dimension=0, tiled=True).astype(F32)
    return functools.reduce(jnp.add, [chunk.astype(F32) for chunk in chunks])


def scatter_end(chunks):
    return scatter_total(scatter_move(chunks))


def attention_results(value, wide):
    rows = value.shape[0]
    taken = rows // (D // wide)
    return (
        jnp.stack([value[:, i * wide : (i + 1) * wide] for i in range(3)]),
        jnp.concatenate(
            [value[b * taken : (b + 1) * taken, 3 * wide :] for b in range(D // wide)], axis=1
        ),
    )


def expert_results_body(place, own_0, moved_0, own_1, moved_1, down_ref, up_ref):
    i = pl.program_id(0)
    first = place[1] == 0
    own = (i < HALF) == first

    def put(value):
        down_ref[...] = value[0].astype(F32)
        up_ref[...] = value[1].astype(F32)

    for layer, own_ref, moved_ref in ((0, own_0, moved_0), (1, own_1, moved_1)):
        kept = first == (layer == 0)
        pl.when(kept & own)(functools.partial(put, own_ref))
        pl.when(kept & jnp.logical_not(own))(functools.partial(put, moved_ref))


def expert_results(place, sums, moved):
    rows, columns = sums[0].shape[1:]
    shaped = [
        a.reshape(2, HALF, rows, columns) for pair in zip(sums, moved) for a in pair
    ]
    block = pl.BlockSpec((2, 1, rows, columns), lambda i, place: (0, i % HALF, 0, 0))
    out = pl.BlockSpec((1, rows, columns), lambda i, place: (i, 0, 0))
    return pl.pallas_call(
        expert_results_body,
        grid_spec=pltpu.PrefetchScalarGridSpec(
            num_scalar_prefetch=1,
            grid=(EXPERTS,),
            in_specs=[block] * 4,
            out_specs=[out, out],
        ),
        out_shape=[shape((EXPERTS, rows, columns), F32)] * 2,
        compiler_params=limit(24),
        cost_estimate=cost(1e6, 1e5),
        name="expert_results",
    )(place, *shaped)


def scatter_sum(value, dim):
    return lax.psum_scatter(value, "dp", scatter_dimension=dim, tiled=True)


def phase(*values):
    return lax.optimization_barrier(values)


def sum_small(value, axis):
    count = lax.axis_size(axis)
    if count != 4:
        return lax.psum(value, axis)
    return (value + exchange(value, axis, 1)) + (
        exchange(value, axis, 2) + exchange(value, axis, 3)
    )


def local(
    inputs,
    norm_gains,
    attention_in,
    attention_out,
    bias_table,
    router_weight,
    up_weight,
    down_weight,
    routes,
    piece_starts,
    valid_mask,
    cotangent,
):
    s = lax.axis_index("section")
    t = lax.axis_index("tensor")
    z = lax.axis_index("dp")
    tensor = lax.axis_size("tensor")
    rows = inputs.shape[1]
    wide = attention_in.shape[3]
    heads = wide // HEAD_DIM
    first = s == 0

    def mine(array):
        return lax.dynamic_index_in_dim(array, s, 0, keepdims=False)

    def by_layer(own, other):
        return jnp.where(first, own, other), jnp.where(first, other, own)

    def swap(value):
        return jax.tree.map(lambda a: exchange(a, "section", 1), value)

    def pair(value):
        return value, swap(value)

    h0 = mine(inputs)
    g1 = mine(cotangent)
    place = [
        jnp.stack([t, s, jnp.where(s == layer, 0, 1), z]).astype(jnp.int32) for layer in range(2)
    ]
    selects = [place[layer][2:3] for layer in range(2)]
    order = jnp.where(first, jnp.array([2, 3, 0, 1]), jnp.array([0, 1, 2, 3])).astype(jnp.int32)
    hot = diagonal_one_hot()
    hot_rows = hot.transpose(2, 0, 1).reshape(BUCKETS, -1)

    gain_pair, table_pair = pair(norm_gains[0]), pair(bias_table[0].T)
    w_out_pair = pair(attention_out[0])

    def prepared(layer):
        return prepare(layer, place[layer], gain_pair, table_pair, hot_rows, valid_mask, rows)

    x_parts, first_prepared, gain_pair, table_pair, w_in_pair, w_out, route_pair, router_pair, up, down = phase(
        gather_parts(h0),
        prepared(0),
        gain_pair,
        table_pair,
        pair(jnp.swapaxes(attention_in[0], 1, 2).reshape(3 * wide, D)),
        by_layer(*w_out_pair),
        pair(routes[0, :, :, 0]),
        pair(router_weight[0].T),
        up_weight[0],
        down_weight[0],
    )

    gain, tile, valid_col, valid_own = first_prepared
    gains, tiles = [gain], [tile]
    hidden = [h0, None]
    saved, outputs, stats, w_out_parts = [], [], [], []
    for layer in range(2):
        kept, att_parts = fwd_attention(
            place[layer],
            piece_starts,
            valid_col,
            gains[layer],
            w_in_pair,
            tiles[layer],
            x_parts,
            layer == 0,
        )
        if layer == 0:
            w_out_parts.append(gather_parts(w_out[0]))
            up_pair, down_pair = pair(up), pair(down)
            att_parts, w_out_parts[0] = phase(att_parts, w_out_parts[0])
        else:
            g_parts = [g1] + [exchange(g1, "tensor", k) for k in range(1, tensor - 1)]
            att_parts, g_parts = phase(att_parts, g_parts)
        pieces = swap_parts(att_parts)
        mid, xn_mid, stat = after_attention(
            hidden[layer], gains[layer], valid_own, pieces, w_out_parts[layer]
        )
        if layer == 0:
            xn_mid, route_pair, router_pair, gain_pair, table_pair = phase(
                xn_mid, route_pair, router_pair, gain_pair, table_pair
            )
            targets = make_targets(place[0], route_pair, router_pair, tensor)
            gain, tile = prepared(1)
            gains.append(gain)
            tiles.append(tile)
        xn_parts = gather_parts(xn_mid)
        if layer == 0:
            xn_parts, targets, gains, tiles, up_pair, down_pair, w_out = phase(
                xn_parts, targets, gains, tiles, up_pair, down_pair, w_out
            )
        else:
            xn_parts, g1 = phase(xn_parts, g1)
        row, col, router = targets[layer::2]
        ex, y_parts = fwd_experts(
            selects[layer], order, row, col, router, up_pair, down_pair, xn_parts
        )
        if layer == 0:
            w_out_parts.append(gather_parts(w_out[1]))
            y_parts, w_out_parts[1], ex = phase(y_parts, w_out_parts[1], ex)
            y_parts = swap_parts(y_parts)
            fwd_sent = [ex[0]]
            saved.append([kept, pieces, mid, xn_mid, ex])
            combined, out, xn_next, stat_more = after_experts(
                mid, ex[2], gains[1], valid_own, y_parts
            )
            outputs.append(out)
            stats.append((stat, stat_more))
            saved[0].append(combined)
            hidden[1] = out
            x_parts = gather_parts(xn_next)
        else:
            g_parts.append(exchange(g1, "tensor", tensor - 1))
            y_parts, g_parts, ex = phase(y_parts, g_parts, ex)
            fwd_sent.append(ex[0])
            saved.append([kept, pieces, mid, xn_mid, ex])

    fwd_y_parts = y_parts
    small_1, square_1, expert_sums = None, [], []
    for layer in (1, 0):
        row, col, router = targets[layer::2]
        kept, pieces, mid, xn_mid, ex = saved[layer][:5]
        fwd_halves, slope, gate, probs = ex
        g = g_parts[0]
        bwd_halves, y_parts = bwd_experts(
            selects[layer], order, row, col, gate, slope, up_pair, down_pair, g_parts
        )
        fwd_other = swap(fwd_sent[layer])
        if layer == 1:
            y_parts, bwd_halves, fwd_y_parts, fwd_other = phase(
                y_parts, bwd_halves, swap_parts(fwd_y_parts), fwd_other
            )
            combined, out, _, stat_more = after_experts(
                mid, gate, gains[1], valid_own, fwd_y_parts
            )
            outputs.append(out)
            stats.append((stat, stat_more))
        else:
            y_parts, bwd_halves, fwd_other, square_1 = phase(
                y_parts, bwd_halves, fwd_other, scatter_move(square_1)
            )
            combined = saved[0][5]

        total = expert_grads((fwd_halves, fwd_other, bwd_halves, swap(bwd_halves)))
        y_parts, total, combined = phase(swap_parts(y_parts), total, combined)
        expert_sums.append(scatter_sum(total, 1))

        (d_mid, d_a, grad_gain_mid, grad_router), d_pieces = middle_back(
            g,
            combined,
            probs,
            col,
            router,
            mid,
            gains[layer],
            xn_mid,
            y_parts,
            w_out_parts[layer],
        )
        d_pieces, out_terms = phase(swap_parts(d_pieces), out_grads(pieces, d_a))

        xn, qkv, turned, lse = kept
        (d_proj, diag, far, grad_gain_in), x_terms = bwd_attention(
            place[layer],
            piece_starts,
            valid_col,
            gains[layer],
            w_in_pair,
            tiles[layer],
            (xn, qkv, turned, lse),
            d_pieces,
        )
        x_terms, d_proj, diag, far, out_terms = phase(
            x_terms, d_proj, diag, far, swap_parts(out_terms)
        )

        x_terms = swap_parts(x_terms)
        sent, square = attention_grads(place[layer], xn, d_proj, out_terms)
        small = small_sums(
            place[0],
            diag,
            far,
            hot_rows,
            grad_gain_in,
            grad_gain_mid,
            grad_router,
            stats[layer],
            small_1,
        )
        if layer == 1:
            x_terms, small_1, sent, square = phase(x_terms, small, sent, square)
            d_h_1, d_h_low = input_back(d_mid, hidden[1], gains[1], x_terms)
            g_parts, square_1 = phase(
                gather_parts(d_h_low), scatter_small(place[1], square, swap(sent))
            )
            d_h_1 = d_h_low

    def kept_sent(values):
        return jnp.where(first, values[0], values[1]), jnp.where(first, values[1], values[0])

    def placed(own, received, axis=0):
        return jnp.where(
            first,
            jnp.concatenate([own, received], axis=axis),
            jnp.concatenate([received, own], axis=axis),
        )

    x_terms, square, sent, small = phase(x_terms, square, sent, small)

    d_h = input_back(d_mid, hidden[0], gains[0], x_terms)[0]
    out_keep, out_sent = kept_sent(outputs)
    d_h_keep, d_h_sent = kept_sent((d_h, d_h_1.astype(F32)))
    small = small[0] + swap(small[1])
    sum_1, sum_0 = expert_sums
    out_moved, d_h_moved, small, shared, square, moved_1 = phase(
        swap(out_sent),
        swap(d_h_sent.astype(BF)),
        small,
        sum_small(small[:8], "tensor"),
        scatter_small(place[0], square, swap(sent)),
        lax.ppermute(sum_1, "section", [(0, 1)]),
    )
    small = sum_small(jnp.concatenate([shared, small[8:]], axis=0), "dp")
    table = small[8 : 8 + heads, :BUCKETS].T
    share = BUCKETS // lax.axis_size("dp")
    stat = small[6]
    layer_out = placed(out_keep[None], out_moved[None])
    input_grad = placed(d_h_keep[None], d_h_moved.astype(F32)[None])
    square_0, layer_out, input_grad, grad_gain, grad_table, grad_router, root_means = phase(
        scatter_end(square),
        layer_out,
        input_grad,
        small[0:2],
        lax.dynamic_slice_in_dim(table, z * share, share, 0),
        small[2:6].T,
        jnp.sqrt(stat[:3] / (stat[3] * D)),
    )
    keep, sent = kept_sent((square_0, scatter_total(square_1)))
    square = placed(keep, swap(sent.astype(BF)).astype(F32), axis=1)
    grad_w_in, grad_w_out = attention_results(square, wide)
    moved_0 = lax.ppermute(sum_0, "section", [(1, 0)])
    experts = expert_results(place[0], (sum_0, sum_1), (moved_0, moved_1))
    return (
        layer_out[None],
        input_grad[None],
        grad_gain[None],
        grad_w_in[None],
        grad_w_out[None],
        grad_table[None],
        grad_router[None],
        experts[1][None],
        experts[0][None],
        root_means[None],
    )


def solution(mesh):
    placed = (
        P("dp", "tensor", None),
        P("section", None, None),
        P("section", None, None, "tensor"),
        P("section", "tensor", None),
        P("section", None, "tensor"),
        P("section", None, None),
        P("section", None, None, "tensor"),
        P("section", None, "tensor", None),
        P("section", "dp", None, None),
        P("dp", None),
        P("dp", None),
        P("dp", "tensor", None),
    )
    return jax.shard_map(
        local,
        mesh=mesh,
        in_specs=placed,
        out_specs=(
            P("section", "dp", "tensor", None),
            P("section", "dp", "tensor", None),
            P("section", None, None),
            P("section", None, "dp", "tensor"),
            P("section", ("tensor", "dp"), None),
            P("section", "dp", "tensor"),
            P("section", None, None),
            P("section", None, "dp", "tensor"),
            P("section", None, ("tensor", "dp"), None),
            P("section", None),
        ),
        check_vma=False,
    )
```

```python
import functools

import jax
import jax.numpy as jnp
import numpy as np
from jax import lax
from jax.experimental import pallas as pl
from jax.experimental.pallas import tpu as pltpu
from jax.sharding import PartitionSpec as P

D = 768
HEAD_DIM = 64
BUCKETS = 32
EXPERTS = 4
CAP = 320
SEQ = 1024
PIECE = 256
PIECES = 2
SLOTS = EXPERTS * CAP

QB = PIECE
BAND = 128
WIDE = 2 * QB + BAND
DIAGS = 6

epsilon = 1e-06
bucket_edges = (12, 16, 23, 32, 46, 64, 91)
masked_score = -1000000000.0
far_bucket_behind = 15

BF = jnp.bfloat16
F32 = jnp.float32
MIB = 1024 * 1024


def dot(a, b, ca=1, cb=0):
    return lax.dot_general(a, b, (((ca,), (cb,)), ((), ())), preferred_element_type=F32)


def vm(count):
    return [pl.BlockSpec(memory_space=pltpu.VMEM)] * count


def smem():
    return pl.BlockSpec(memory_space=pltpu.SMEM)


def any_space(count):
    return [pl.BlockSpec(memory_space=pl.ANY)] * count


def limit(mib):
    return pltpu.CompilerParams(vmem_limit_bytes=mib * MIB)


def cost(flops, size):
    return pl.CostEstimate(flops=int(flops), bytes_accessed=int(size), transcendentals=0)


def shape(dims, kind):
    return jax.ShapeDtypeStruct(dims, kind)


def in_hbm(dims, kind):
    return pltpu.HBM(dims, kind)


def from_hbm(value):
    return pltpu.with_memory_space_constraint(value, pltpu.HBM)


def choose(select, own_ref, other_ref, to_ref):
    @pl.when(select == 0)
    def _():
        to_ref[...] = own_ref[...]

    @pl.when(select != 0)
    def _():
        to_ref[...] = other_ref[...]


def either(select, step, own, other):
    @pl.when(select == 0)
    def _():
        step(*own)

    @pl.when(select != 0)
    def _():
        step(*other)


def exchange(value, axis, mask):
    count = lax.axis_size(axis)
    return lax.ppermute(value, axis, [(i, i ^ mask) for i in range(count)])


def gather_parts(value):
    return [value] + [exchange(value, "tensor", k) for k in range(1, lax.axis_size("tensor"))]


def swap_parts(parts):
    return [parts[0]] + [exchange(p, "tensor", k) for k, p in enumerate(parts) if k]


def natural(t, k, size):
    return pl.ds(pl.multiple_of(jnp.bitwise_xor(t, k) * size, size), size)


def norm(vector, gain):
    return vector * lax.rsqrt(jnp.mean(vector * vector, axis=-1, keepdims=True) + epsilon) * gain


def total_of(value):
    return jnp.sum(jnp.sum(value, axis=0, keepdims=True), axis=1, keepdims=True)


def offset_buckets(offsets):
    distance = np.abs(offsets)
    far = np.full(offsets.shape, 8, np.int32)
    for edge_value in bucket_edges:
        far = far + (distance >= edge_value)
    return np.where(distance < 8, distance, far) + np.where(offsets > 0, 16, 0)


def diagonal_one_hot():
    lane = np.arange(2 * BAND)
    y = np.where(lane < BAND, lane, lane - 2 * BAND)
    offsets = BAND * (np.arange(DIAGS)[:, None] - 2) - y[None, :]
    hot = offset_buckets(offsets)[:, :, None] == np.arange(BUCKETS)
    hot = hot & (lane != BAND)[None, :, None]
    return hot.astype(np.float32)


def prepare_body(layer, place, own_gain, other_gain, own_table, other_table, hot, valid_ref, *refs):
    s = place[1]
    refs = refs[-5:] if layer == 0 else refs[-3:]
    gain_ref, tile_ref = refs[:2]
    heads = own_table.shape[0]
    own = s == layer
    gain_ref[...] = jnp.where(own, own_gain[...], other_gain[...])
    table = jnp.where(own, own_table[...], other_table[...])
    table = table - table[:, far_bucket_behind : far_bucket_behind + 1]
    by_offset = lax.dot_general(
        table,
        hot[...],
        (((1,), (0,)), ((), ())),
        precision=lax.Precision.HIGHEST,
        preferred_element_type=F32,
    )
    for h in range(heads):
        for d in range(DIAGS):
            row = by_offset[h : h + 1, d * 2 * BAND : (d + 1) * 2 * BAND]
            tile_ref[h * DIAGS + d] = pltpu.roll(
                jnp.broadcast_to(row, (BAND, 2 * BAND)), 0, 1, stride=1, stride_axis=0
            )[:, :BAND]
    if layer == 0:
        key_ref, own_ref, scratch = refs[2], refs[3], refs[4]
        rows = own_ref.shape[0]
        valid = jnp.where(s == 0, valid_ref[0:1, :], valid_ref[1:2, :]).astype(F32)
        column = jnp.broadcast_to(valid, (128, SEQ)).T[:, :1]
        scratch[...] = column
        key_ref[...] = jnp.where(column > 0, 0.0, masked_score)
        own_ref[...] = scratch[pl.ds(pl.multiple_of(place[0] * rows, rows), rows), :]


def prepare(layer, place, gains, tables, hot, valid, rows):
    outs = [shape((2, D), F32), shape((tables[0].shape[0] * DIAGS, BAND, BAND), F32)]
    if layer == 0:
        outs += [shape((SEQ, 1), F32), shape((rows, 1), F32)]
    return pl.pallas_call(
        functools.partial(prepare_body, layer),
        out_shape=outs,
        in_specs=[smem()] + vm(6),
        out_specs=vm(len(outs)),
        scratch_shapes=[pltpu.VMEM((SEQ, 1), F32)],
        compiler_params=limit(16),
        cost_estimate=cost(1e6, 1e5),
        name="prepare",
    )(place, *gains, *tables, hot, valid)


def targets_body(parts, place, own_route, other_route, own_router, other_router, *outs):
    row_refs, col_refs, router_refs, scratch = outs[:2], outs[2:4], outs[4:6], outs[6]
    t, s = place[0], place[1]
    rows = SEQ // parts
    before = lax.broadcasted_iota(jnp.int32, (SEQ, SEQ), 0)
    upto = (before <= lax.broadcasted_iota(jnp.int32, (SEQ, SEQ), 1)).astype(BF)
    expert = lax.broadcasted_iota(jnp.int32, (8, SEQ), 0)
    for layer in range(2):
        own = s == layer
        route = jnp.where(own, own_route[...], other_route[...])
        route = jnp.where(s == 0, route[0:1, :], route[1:2, :])
        hit = route == expert
        count = dot(hit.astype(BF), upto)
        slot = jnp.where(hit, count - 1.0 + (expert * CAP).astype(F32), 0.0)
        scratch[...] = jnp.sum(slot, axis=0, keepdims=True)
        for k in range(parts):
            row_refs[layer][:, k * rows : (k + 1) * rows] = scratch[:, natural(t, k, rows)].astype(
                jnp.int32
            )
        scratch[...] = row_refs[layer][...].astype(F32)
        turned = jnp.broadcast_to(scratch[...], (128, SEQ)).T
        col_refs[layer][...] = turned[:, :1].astype(jnp.int32)
        router_refs[layer][...] = jnp.where(
            own, own_router[...].astype(F32), other_router[...].astype(F32)
        ).astype(BF)


def make_targets(place, routes, routers, parts):
    row, col = shape((1, SEQ), jnp.int32), shape((SEQ, 1), jnp.int32)
    router = shape((128, D), BF)
    return pl.pallas_call(
        functools.partial(targets_body, parts),
        out_shape=[row, row, col, col, router, router],
        in_specs=[smem()] + vm(4),
        out_specs=vm(6),
        scratch_shapes=[pltpu.VMEM((1, SEQ), F32)],
        compiler_params=limit(16),
        cost_estimate=cost(1e6, 1e5),
        name="make_targets",
    )(place, *routes, *routers)


def near_bias(tiles_ref, h, skip, width):
    first, last = skip // BAND, (skip + width) // BAND
    columns = [
        jnp.concatenate([tiles_ref[h * DIAGS + i - j + 1] for i in range(first, last)], axis=0)
        for j in range(QB // BAND)
    ]
    return jnp.concatenate(columns, axis=1)


def block_range(j):
    last = min(SEQ, QB * (j + 2))
    left = max(0, QB * j - BAND)
    return left, last, left - (QB * j - BAND)


def fill_mask(mask_ref, valid_ref, s0, s1, j):
    left, last, _ = block_range(j)
    width = last - left
    key = left + lax.broadcasted_iota(jnp.int32, (width, 1), 0)
    query = QB * j + lax.broadcasted_iota(jnp.int32, (1, QB), 1)

    def label(position, outside):
        second = jnp.where((position >= s1) & (position < s1 + PIECE), 1, outside)
        return jnp.where((position >= s0) & (position < s0 + PIECE), 0, second)

    allowed = (key <= query) | (label(key, -1) == label(query, -2))
    mask_ref[:width, :] = jnp.where(allowed, valid_ref[left:last, :], masked_score)


def fwd_attention_body(parts, norm_inside, *refs):
    place, starts, valid_col, gain, w_own, w_other, tiles_ref = refs[:7]
    x_refs = refs[7 : 7 + parts]
    xn_out, qkv_out, turned_out, lse_ref = refs[7 + parts : 11 + parts]
    out_refs = refs[11 + parts : 11 + 2 * parts]
    w_ref, xn_ref, qkv_ref, turned_ref, vt_ref, att_ref, mask_ref, valid_ref, sems = refs[
        11 + 2 * parts :
    ]
    t, s = place[0], place[1]
    s0, s1 = starts[s, 0], starts[s, 1]
    rows = SEQ // parts
    heads = qkv_ref.shape[1]
    wide = heads * HEAD_DIM

    choose(place[2], w_own, w_other, w_ref)
    valid_ref[...] = jnp.broadcast_to(valid_col[...], (SEQ, QB))
    for k in range(parts):
        where = natural(t, k, rows)
        x = x_refs[k][...]
        if norm_inside:
            x = norm(x.astype(F32), gain[0:1, :]).astype(BF)
        xn_ref[where, :] = x
        projected = dot(x, w_ref[...], 1, 1)
        for i in range(3):
            product = projected[:, i * wide : (i + 1) * wide]
            if i == 0:
                product = product * HEAD_DIM**-0.5
            turned = product.T.astype(BF)
            if i < 2:
                turned_ref[i, :, where] = turned
            else:
                vt_ref[:, where] = turned
            product = product.astype(BF)
            for h in range(heads):
                qkv_ref[i, h, where, :] = product[:, h * HEAD_DIM : (h + 1) * HEAD_DIM]

    copies = [
        pltpu.make_async_copy(a, b, sems.at[i])
        for i, (a, b) in enumerate(
            ((xn_ref, xn_out), (qkv_ref, qkv_out), (turned_ref, turned_out))
        )
    ]
    for copy in copies:
        copy.start()

    for j in range(SEQ // QB):
        left, last, skip = block_range(j)
        width = last - left
        columns = slice(j * QB, (j + 1) * QB)
        fill_mask(mask_ref, valid_ref, s0, s1, j)

        def one_head(h, carry):
            lanes = pl.ds(pl.multiple_of(h * HEAD_DIM, HEAD_DIM), HEAD_DIM)
            scores = dot(qkv_ref[1, h, :last, :], turned_ref[0, lanes, columns])
            near = scores[left:] + near_bias(tiles_ref, h, skip, width) + mask_ref[:width, :]
            highest = jnp.max(near, axis=0, keepdims=True)
            if left:
                far = scores[:left] + valid_ref[:left, :]
                highest = jnp.maximum(highest, jnp.max(far, axis=0, keepdims=True))
            near = jnp.exp(near - highest)
            total = jnp.sum(near, axis=0, keepdims=True)
            out = dot(vt_ref[lanes, left:last], near.astype(BF))
            if left:
                far = jnp.exp(far - highest)
                total = total + jnp.sum(far, axis=0, keepdims=True)
                out = out + dot(vt_ref[lanes, :left], far.astype(BF))
            lse_ref[h, :, columns] = highest + jnp.log(total)
            att_ref[lanes, columns] = (out * (1.0 / total)).astype(BF)
            return carry

        lax.fori_loop(0, heads, one_head, 0)

    for k in range(parts):
        out_refs[k][...] = att_ref[:, natural(t, k, rows)]
    for copy in copies:
        copy.wait()


def fwd_attention(place, starts, valid_col, gain, w_pair, tiles, x_parts, norm_inside):
    parts = len(x_parts)
    rows = SEQ // parts
    wide = w_pair[0].shape[0] // 3
    heads = wide // HEAD_DIM
    kept = [
        shape((SEQ, D), BF),
        shape((3, heads, SEQ, HEAD_DIM), BF),
        shape((2, wide, SEQ), BF),
    ]
    outs = pl.pallas_call(
        functools.partial(fwd_attention_body, parts, norm_inside),
        out_shape=[in_hbm(a.shape, a.dtype) for a in kept]
        + [shape((heads, 1, SEQ), F32)] + [shape((wide, rows), BF)] * parts,
        in_specs=[smem()] * 2 + vm(5 + parts),
        out_specs=any_space(3) + vm(1 + parts),
        scratch_shapes=[pltpu.VMEM((3 * wide, D), BF)]
        + [pltpu.VMEM(a.shape, a.dtype) for a in kept]
        + [
            pltpu.VMEM((wide, SEQ), BF),
            pltpu.VMEM((wide, SEQ), BF),
            pltpu.VMEM((WIDE, QB), F32),
            pltpu.VMEM((SEQ, QB), F32),
            pltpu.SemaphoreType.DMA((3,)),
        ],
        compiler_params=limit(32),
        cost_estimate=cost(9e9, 1e7),
        name="fwd_attention",
    )(place, starts, valid_col, gain, *[from_hbm(a) for a in (*w_pair, tiles)], *x_parts)
    return outs[:4], list(outs[4:])


def bwd_attention_body(parts, *refs):
    place, starts, valid_col, gain, w_own, w_other, tiles_ref, xn_ref = refs[:8]
    qkv_ref, turned_ref, lse_ref = refs[8:11]
    d_refs = refs[11 : 11 + parts]
    refs = refs[11 + parts :]
    proj_ref, sum_ref, far_ref, gain_ref = refs[:4]
    out_refs = refs[4 : 4 + parts]
    w_ref, d_ref, dt_ref, dq_ref, dk_ref, dv_ref, mask_ref, valid_ref = refs[4 + parts :]
    t, s = place[0], place[1]
    s0, s1 = starts[s, 0], starts[s, 1]
    rows = SEQ // parts
    heads = qkv_ref.shape[1]

    choose(place[2], w_own, w_other, w_ref)
    valid_ref[...] = jnp.broadcast_to(valid_col[...], (SEQ, QB))
    for k in range(parts):
        where = natural(t, k, rows)
        block = d_refs[k][...]
        dt_ref[:, where] = block.astype(F32).T.astype(BF)
        for h in range(heads):
            d_ref[h, where, :] = block[:, h * HEAD_DIM : (h + 1) * HEAD_DIM]
    dk_ref[...] = jnp.zeros_like(dk_ref)
    dv_ref[...] = jnp.zeros_like(dv_ref)
    sum_ref[...] = jnp.zeros_like(sum_ref)
    far_ref[...] = jnp.zeros_like(far_ref)

    for j in range(SEQ // QB):
        left, last, skip = block_range(j)
        width = last - left
        columns = slice(j * QB, (j + 1) * QB)
        fill_mask(mask_ref, valid_ref, s0, s1, j)

        def one_head(h, carry):
            lanes = pl.ds(pl.multiple_of(h * HEAD_DIM, HEAD_DIM), HEAD_DIM)
            q_block = qkv_ref[0, h, columns, :]
            d_block = d_ref[h, columns, :]
            lse = lse_ref[h, :, columns]
            scores = dot(qkv_ref[1, h, :last, :], turned_ref[0, lanes, columns])
            slopes = dot(qkv_ref[2, h, :last, :], dt_ref[lanes, columns])
            near = scores[left:] + near_bias(tiles_ref, h, skip, width) + mask_ref[:width, :]
            near = jnp.exp(near - lse)
            near_slope = near * slopes[left:]
            row_dot = jnp.sum(near_slope, axis=0, keepdims=True)
            if left:
                far = jnp.exp(scores[:left] + valid_ref[:left, :] - lse)
                far_slope = far * slopes[:left]
                row_dot = row_dot + jnp.sum(far_slope, axis=0, keepdims=True)
            near_slope = near_slope - near * row_dot
            for i in range(width // BAND):
                for c in range(QB // BAND):
                    sum_ref[h * DIAGS + skip // BAND + i - c + 1] += near_slope[
                        i * BAND : (i + 1) * BAND, c * BAND : (c + 1) * BAND
                    ]
            near_slope = near_slope.astype(BF)
            dk_ref[h, left:last, :] += dot(near_slope, q_block)
            dv_ref[h, left:last, :] += dot(near.astype(BF), d_block)
            dq = dot(turned_ref[1, lanes, left:last], near_slope)
            if left:
                far_slope = far_slope - far * row_dot
                far_ref[h] += jnp.sum(far_slope.reshape(left // 8, 8, QB), axis=0)
                far_slope = far_slope.astype(BF)
                dk_ref[h, :left, :] += dot(far_slope, q_block)
                dv_ref[h, :left, :] += dot(far.astype(BF), d_block)
                dq = dq + dot(turned_ref[1, lanes, :left], far_slope)
            dq_ref[lanes, columns] = dq * HEAD_DIM**-0.5
            return carry

        lax.fori_loop(0, heads, one_head, 0, unroll=True)

    for first in range(0, SEQ, rows):
        where = slice(first, first + rows)
        blocks = [dq_ref[:, where].T.astype(BF)]
        for source in (dk_ref, dv_ref):
            blocks += [source[h, where, :].astype(BF) for h in range(heads)]
        proj_ref[where, :] = jnp.concatenate(blocks, axis=1)
    gain_sum = jnp.zeros((1, D), F32)
    for k in range(parts):
        where = natural(t, k, rows)
        total = dot(proj_ref[where, :], w_ref[...])
        out_refs[k][...] = total.astype(BF)
        gain_sum = gain_sum + jnp.sum(total * xn_ref[where, :].astype(F32), axis=0, keepdims=True)
    gain_ref[...] = gain_sum / gain[0:1, :]


def bwd_attention(place, starts, valid_col, gain, w_pair, tiles, saved, d_parts):
    parts = len(d_parts)
    rows = SEQ // parts
    wide = w_pair[0].shape[0] // 3
    heads = wide // HEAD_DIM
    outs = pl.pallas_call(
        functools.partial(bwd_attention_body, parts),
        out_shape=[
            in_hbm((SEQ, 3 * wide), BF),
            in_hbm((heads * DIAGS, BAND, BAND), F32),
            shape((heads, 8, QB), F32),
            shape((1, D), F32),
        ]
        + [in_hbm((rows, D), BF)] * parts,
        in_specs=[smem()] * 2 + vm(9 + parts),
        out_specs=vm(4 + parts),
        scratch_shapes=[
            pltpu.VMEM((3 * wide, D), BF),
            pltpu.VMEM((heads, SEQ, HEAD_DIM), BF),
            pltpu.VMEM((wide, SEQ), BF),
            pltpu.VMEM((wide, SEQ), F32),
            pltpu.VMEM((heads, SEQ, HEAD_DIM), F32),
            pltpu.VMEM((heads, SEQ, HEAD_DIM), F32),
            pltpu.VMEM((WIDE, QB), F32),
            pltpu.VMEM((SEQ, QB), F32),
        ],
        compiler_params=limit(36),
        cost_estimate=cost(1.8e10, 1e7),
        name="bwd_attention",
    )(
        place,
        starts,
        valid_col,
        gain,
        *w_pair,
        tiles,
        *saved,
        *d_parts,
    )
    return outs[:4], list(outs[4:])


def small_sums_body(paired, place, tiles_ref, far_ref, hot, gain_in, gain_mid, router, *refs):
    stats, refs = refs[:2], refs[2:]
    heads = far_ref.shape[0]
    row = lax.broadcasted_iota(jnp.int32, (BAND, BAND), 0)
    column = lax.broadcasted_iota(jnp.int32, (BAND, BAND), 1)
    flip = (row + column == BAND - 1).astype(F32)
    out = refs[-1]
    out[...] = jnp.zeros_like(out)
    out[0:1, :] = gain_in[...]
    out[1:2, :] = gain_mid[...]
    out[2 : 2 + EXPERTS, :] = router[:EXPERTS, :]
    out[6:7, :128] = stats[0][...] + stats[1][...]
    by_offset = []
    for h in range(heads):
        sums = []
        for d in range(DIAGS):
            tile = lax.dot_general(
                flip,
                tiles_ref[h * DIAGS + d],
                (((1,), (0,)), ((), ())),
                precision=lax.Precision.HIGHEST,
                preferred_element_type=F32,
            )
            tile = jnp.concatenate([tile, jnp.zeros_like(tile)], axis=1)
            tile = pltpu.roll(tile, BAND + 1, 1, stride=1, stride_axis=0)
            sums.append(jnp.sum(tile, axis=0, keepdims=True))
        by_offset.append(jnp.concatenate(sums, axis=1))
    table = lax.dot_general(
        jnp.concatenate(by_offset, axis=0),
        hot[...],
        (((1,), (1,)), ((), ())),
        precision=lax.Precision.HIGHEST,
        preferred_element_type=F32,
    )
    bucket = lax.broadcasted_iota(jnp.int32, (1, BUCKETS), 1)
    for h in range(heads):
        behind = jnp.where(bucket == far_bucket_behind, total_of(far_ref[h]), 0.0)
        out[8 + h : 9 + h, :BUCKETS] = table[h : h + 1, :] + behind
    if paired:
        other, keep, sent = refs[:3]
        first = place[1] == 0
        keep[...] = jnp.where(first, out[...], other[...])
        sent[...] = jnp.where(first, other[...], out[...])


def small_sums(place, tiles, far, hot, gain_in, gain_mid, router, stats, other):
    paired = other is not None
    array = shape((16, D), F32)
    outs = pl.pallas_call(
        functools.partial(small_sums_body, paired),
        out_shape=[array] * (2 if paired else 1),
        in_specs=[smem()] + vm(8 + paired),
        out_specs=vm(2 if paired else 1),
        scratch_shapes=[pltpu.VMEM((16, D), F32)] if paired else [],
        compiler_params=limit(16),
        cost_estimate=cost(1e6, 1e5),
        name="small_sums",
    )(place, from_hbm(tiles), far, hot, gain_in, gain_mid, router, *stats, *([other] if paired else []))
    return outs if paired else outs[0]


def combine(parts, rows, target_col, slots_ref, out_refs):
    slot = lax.broadcasted_iota(jnp.int32, (rows, SLOTS), 1)
    for k in list(range(1, parts)) + [0]:
        hot = (target_col[k * rows : (k + 1) * rows, :] == slot).astype(BF)
        out_refs[k][...] = dot(hot, slots_ref[...]).astype(BF)


def dispatch(e, target_row, tokens_ref):
    slot = e * CAP + lax.broadcasted_iota(jnp.int32, (CAP, SEQ), 0)
    return dot((target_row[...] == slot).astype(BF), tokens_ref[...]).astype(BF)


HALF = EXPERTS // 2


def fwd_experts_body(parts, *refs):
    sel, order, target_row, target_col, router, up_own, up_other, down_own, down_other = refs[:9]
    x_refs = refs[9 : 9 + parts]
    half_ref, slope_ref, gate_ref, probs_ref = refs[9 + parts : 13 + parts]
    out_refs = refs[13 + parts : 13 + 2 * parts]
    x_ref, slots_ref = refs[13 + 2 * parts :]
    rows = SEQ // parts
    step = pl.program_id(0)
    e = order[step]

    @pl.when(step == 0)
    def _():
        lane = lax.broadcasted_iota(jnp.int32, (rows, 128), 1)
        for k in range(parts):
            where = slice(k * rows, (k + 1) * rows)
            x = x_refs[k][...]
            x_ref[where, :] = x
            logits = jnp.where(lane < EXPERTS, dot(x, router[...], 1, 1), -1e30)
            probs = jnp.exp(logits - jnp.max(logits, axis=-1, keepdims=True))
            probs = probs / jnp.sum(probs, axis=-1, keepdims=True)
            target = target_col[where, :]
            hit = (target >= lane * CAP) & (target < lane * CAP + CAP)
            gate_ref[where, :] = jnp.sum(jnp.where(hit, probs, 0.0), axis=-1, keepdims=True)
            if k == 0:
                probs_ref[...] = probs

    def one_expert(up_ref, down_ref):
        expert_in = dispatch(e, target_row, x_ref)
        half_ref[0, 1] = expert_in
        up = dot(expert_in, up_ref[0])
        inner = np.sqrt(2 / np.pi).astype(np.float32)
        square = up * up
        bend = jnp.tanh(inner * (up * (1.0 + 0.044715 * square)))
        half = 0.5 * (1.0 + bend)
        act = (up * half).astype(BF)
        half_ref[0, 0] = act
        slope_ref[0] = half + 0.5 * up * (1.0 - bend * bend) * (
            inner * (1.0 + 3 * 0.044715 * square)
        )
        slots_ref[pl.ds(pl.multiple_of(e * CAP, CAP), CAP), :] = dot(act, down_ref[0]).astype(BF)

    either(sel[0], one_expert, (up_own, down_own), (up_other, down_other))

    @pl.when(step == EXPERTS - 1)
    def _():
        combine(parts, rows, target_col, slots_ref, out_refs)


def expert_specs(block):
    own = pl.BlockSpec(block, lambda i, sel, order: (order[i] * (1 - sel[0]), 0, 0))
    other = pl.BlockSpec(block, lambda i, sel, order: (order[i] * sel[0], 0, 0))
    return [own, other]


def half_spec(columns):
    return pl.BlockSpec((1, 2, CAP, columns), lambda i, sel, order: (i, 0, 0, 0))


def whole(dims):
    return pl.BlockSpec(dims, lambda i, sel, order: (0,) * len(dims))


def fwd_experts(select, order, target_row, target_col, router, up_pair, down_pair, x_parts):
    parts = len(x_parts)
    rows = SEQ // parts
    hidden = up_pair[0].shape[2]
    each_hidden = pl.BlockSpec((1, CAP, hidden), lambda i, sel, order: (i, 0, 0))
    outs = pl.pallas_call(
        functools.partial(fwd_experts_body, parts),
        grid_spec=pltpu.PrefetchScalarGridSpec(
            num_scalar_prefetch=2,
            grid=(EXPERTS,),
            in_specs=[whole((1, SEQ)), whole((SEQ, 1)), whole((128, D))]
            + expert_specs((1, D, hidden))
            + expert_specs((1, hidden, D))
            + [whole((rows, D))] * parts,
            out_specs=[half_spec(D)]
            + [each_hidden, whole((SEQ, 1)), whole((rows, 128))]
            + [whole((rows, D))] * parts,
            scratch_shapes=[
                pltpu.VMEM((SEQ, D), BF),
                pltpu.VMEM((SLOTS, D), BF),
            ],
        ),
        out_shape=[in_hbm((EXPERTS, 2, CAP, D), BF)]
        + [
            in_hbm((EXPERTS, CAP, hidden), F32),
            shape((SEQ, 1), F32),
            shape((rows, 128), F32),
        ]
        + [shape((rows, D), BF)] * parts,
        compiler_params=limit(36),
        cost_estimate=cost(1.2e10, 3e7),
        name="fwd_experts",
    )(
        select,
        order,
        target_row,
        target_col,
        router,
        *[from_hbm(a) for a in (*up_pair, *down_pair)],
        *x_parts,
    )
    return outs[:4], list(outs[4:])


def bwd_experts_body(parts, *refs):
    sel, order, target_row, target_col, gate, slope_ref = refs[:6]
    up_own, up_other, down_own, down_other = refs[6:10]
    g_refs = refs[10 : 10 + parts]
    refs = refs[10 + parts :]
    half_ref = refs[0]
    out_refs = refs[1 : 1 + parts]
    g_ref, slots_ref = refs[1 + parts :]
    rows = SEQ // parts
    step = pl.program_id(0)
    e = order[step]

    @pl.when(step == 0)
    def _():
        for k in range(parts):
            where = slice(k * rows, (k + 1) * rows)
            g_ref[where, :] = (gate[where, :] * g_refs[k][...].astype(F32)).astype(BF)

    def one_expert(up_ref, down_ref):
        d_out = dispatch(e, target_row, g_ref)
        half_ref[0, 0] = d_out
        d_up = (slope_ref[0] * dot(d_out, down_ref[0], 1, 1)).astype(BF)
        half_ref[0, 1] = d_up
        slots_ref[pl.ds(pl.multiple_of(e * CAP, CAP), CAP), :] = dot(d_up, up_ref[0], 1, 1).astype(
            BF
        )

    either(sel[0], one_expert, (up_own, down_own), (up_other, down_other))

    @pl.when(step == EXPERTS - 1)
    def _():
        combine(parts, rows, target_col, slots_ref, out_refs)


def bwd_experts(select, order, target_row, target_col, gate, slope, up_pair, down_pair, g_parts):
    parts = len(g_parts)
    rows = SEQ // parts
    hidden = up_pair[0].shape[2]
    each_hidden = pl.BlockSpec((1, CAP, hidden), lambda i, sel, order: (i, 0, 0))
    outs = pl.pallas_call(
        functools.partial(bwd_experts_body, parts),
        grid_spec=pltpu.PrefetchScalarGridSpec(
            num_scalar_prefetch=2,
            grid=(EXPERTS,),
            in_specs=[whole((1, SEQ)), whole((SEQ, 1)), whole((SEQ, 1)), each_hidden]
            + expert_specs((1, D, hidden))
            + expert_specs((1, hidden, D))
            + [whole((rows, D))] * parts,
            out_specs=[half_spec(D)] + [whole((rows, D))] * parts,
            scratch_shapes=[
                pltpu.VMEM((SEQ, D), BF),
                pltpu.VMEM((SLOTS, D), BF),
            ],
        ),
        out_shape=[in_hbm((EXPERTS, 2, CAP, D), BF)] + [shape((rows, D), BF)] * parts,
        compiler_params=limit(36),
        cost_estimate=cost(1.2e10, 3e7),
        name="bwd_experts",
    )(
        select,
        order,
        target_row,
        target_col,
        gate,
        *[from_hbm(a) for a in (slope, *up_pair, *down_pair)],
        *g_parts,
    )
    return outs[0], list(outs[1:])


def norm_back(vector, gain, grad):
    scale = lax.rsqrt(jnp.mean(vector * vector, axis=-1, keepdims=True) + epsilon)
    unit = vector * scale
    scaled = grad * gain
    inner = jnp.mean(unit * scaled, axis=-1, keepdims=True)
    return scale * (scaled - unit * inner), grad * unit


def after_attention_body(parts, *refs):
    h_ref, gain, valid = refs[:3]
    p_refs, w_refs = refs[3 : 3 + parts], refs[3 + parts : 3 + 2 * parts]
    mid_ref, xn_ref, stat_ref = refs[3 + 2 * parts :]
    branch = dot(p_refs[0][...], w_refs[0][...], 0, 0)
    for k in range(1, parts):
        branch = branch + dot(p_refs[k][...], w_refs[k][...], 0, 0)
    h = h_ref[...].astype(F32)
    mid = h + branch
    mid_ref[...] = mid
    xn_ref[...] = norm(mid, gain[1:2, :]).astype(BF)
    weight = valid[...]
    lane = lax.broadcasted_iota(jnp.int32, (1, 128), 1)
    sums = jnp.where(lane == 0, total_of(weight * h * h), 0.0)
    sums = jnp.where(lane == 1, total_of(weight * branch * branch), sums)
    stat_ref[...] = jnp.where(lane == 3, total_of(weight), sums)


def after_attention(h, gain, valid, pieces, w_parts):
    parts = len(pieces)
    rows = h.shape[0]
    return pl.pallas_call(
        functools.partial(after_attention_body, parts),
        out_shape=[shape((rows, D), F32), shape((rows, D), BF), shape((1, 128), F32)],
        in_specs=vm(3 + 2 * parts),
        out_specs=vm(3),
        compiler_params=limit(24),
        cost_estimate=cost(2e9, 4e6),
        name="after_attention",
    )(h, gain, valid, *pieces, *w_parts)


def after_experts_body(parts, *refs):
    mid_ref, gate, gain, valid = refs[:4]
    y_refs = refs[4 : 4 + parts]
    comb_ref, out_ref, xn_ref, stat_ref = refs[4 + parts :]
    total = y_refs[0][...].astype(F32)
    for k in range(1, parts):
        total = total + y_refs[k][...].astype(F32)
    combined = total.astype(BF)
    comb_ref[...] = combined
    branch = gate[: mid_ref.shape[0], :] * combined.astype(F32)
    out = (mid_ref[...] + branch).astype(BF)
    out_ref[...] = out
    xn_ref[...] = norm(out.astype(F32), gain[0:1, :]).astype(BF)
    lane = lax.broadcasted_iota(jnp.int32, (1, 128), 1)
    stat_ref[...] = jnp.where(lane == 2, total_of(valid[...] * branch * branch), 0.0)


def after_experts(mid, gate, gain, valid, y_parts):
    parts = len(y_parts)
    rows = mid.shape[0]
    return pl.pallas_call(
        functools.partial(after_experts_body, parts),
        out_shape=[shape((rows, D), BF)] * 3 + [shape((1, 128), F32)],
        in_specs=vm(4 + parts),
        out_specs=vm(4),
        compiler_params=limit(24),
        cost_estimate=cost(1e8, 4e6),
        name="after_experts",
    )(mid, gate, gain, valid, *y_parts)


def middle_back_body(parts, *refs):
    g_ref, comb_ref, probs_ref, target_col, router, mid_ref, gain, xn_ref = refs[:8]
    y_refs, w_refs = refs[8 : 8 + parts], refs[8 + parts : 8 + 2 * parts]
    refs = refs[8 + 2 * parts :]
    dmid_ref, da_ref, gain_ref, router_ref = refs[:4]
    out_refs = refs[4:]
    rows = g_ref.shape[0]
    g = g_ref[...].astype(F32)
    total = y_refs[0][...].astype(F32)
    for k in range(1, parts):
        total = total + y_refs[k][...].astype(F32)
    d_in = total.astype(BF).astype(F32)
    d_gate = jnp.sum(g * comb_ref[...].astype(F32), axis=-1, keepdims=True)
    lane = lax.broadcasted_iota(jnp.int32, (rows, 128), 1)
    target = target_col[:rows, :]
    hit = (target >= lane * CAP) & (target < lane * CAP + CAP)
    probs = probs_ref[...]
    chosen = jnp.where(hit, d_gate, 0.0)
    inner = jnp.sum(probs * chosen, axis=-1, keepdims=True)
    d_logits = (probs * (chosen - inner)).astype(BF)
    router_ref[...] = dot(d_logits, xn_ref[...], 0, 0)[:8]
    d_xn = d_in + dot(d_logits, router[...])
    d_norm, d_gain = norm_back(mid_ref[...], gain[1:2, :], d_xn)
    gain_ref[...] = jnp.sum(d_gain, axis=0, keepdims=True)
    d_mid = g + d_norm
    dmid_ref[...] = d_mid
    d_a = d_mid.astype(BF)
    da_ref[...] = d_a
    for k in list(range(1, parts)) + [0]:
        out_refs[k][...] = dot(d_a, w_refs[k][...], 1, 1).astype(BF)


def middle_back(g, combined, probs, target_col, router, mid, gain, xn, y_parts, w_parts):
    parts = len(y_parts)
    rows = g.shape[0]
    wide = w_parts[0].shape[0]
    outs = pl.pallas_call(
        functools.partial(middle_back_body, parts),
        out_shape=[shape((rows, D), F32), shape((rows, D), BF), shape((1, D), F32)]
        + [shape((8, D), F32)]
        + [shape((rows, wide), BF)] * parts,
        in_specs=vm(8 + 2 * parts),
        out_specs=vm(4 + parts),
        compiler_params=limit(24),
        cost_estimate=cost(2e9, 6e6),
        name="middle_back",
    )(
        *[
            from_hbm(a)
            for a in (
                g,
                combined,
                probs,
                target_col,
                router,
                mid,
                gain,
                xn,
                *y_parts,
                *w_parts,
            )
        ]
    )
    return outs[:4], list(outs[4:])


def input_back_body(parts, *refs):
    dmid_ref, h_ref, gain = refs[:3]
    y_refs = refs[3 : 3 + parts]
    wide_ref, low_ref = refs[3 + parts :]
    total = y_refs[0][...].astype(F32)
    for k in range(1, parts):
        total = total + y_refs[k][...].astype(F32)
    d_h = dmid_ref[...] + norm_back(h_ref[...].astype(F32), gain[0:1, :], total)[0]
    wide_ref[...] = d_h
    low_ref[...] = d_h.astype(BF)


def input_back(d_mid, h, gain, y_parts):
    parts = len(y_parts)
    rows = h.shape[0]
    return pl.pallas_call(
        functools.partial(input_back_body, parts),
        out_shape=[shape((rows, D), F32), shape((rows, D), BF)],
        in_specs=vm(3 + parts),
        out_specs=vm(2),
        compiler_params=limit(24),
        cost_estimate=cost(1e8, 4e6),
        name="input_back",
    )(d_mid, h, gain, *y_parts)


def expert_grads_body(fwd_own, fwd_other, bwd_own, bwd_other, out):
    for kind in range(2):
        left = jnp.concatenate([fwd_own[0, kind], fwd_other[0, kind]], axis=0)
        right = jnp.concatenate([bwd_own[0, kind], bwd_other[0, kind]], axis=0)
        out[kind, 0] = dot(left, right, 0, 0).astype(BF)


def expert_grads(values):
    columns = values[0].shape[3]
    block = (1, 2, CAP, columns)
    own = pl.BlockSpec(block, lambda i: (i + HALF, 0, 0, 0))
    other = pl.BlockSpec(block, lambda i: (i, 0, 0, 0))
    outs = pl.pallas_call(
        expert_grads_body,
        grid=(HALF,),
        in_specs=[own, other, own, other],
        out_specs=pl.BlockSpec((2, 1, columns, columns), lambda i: (0, i, 0, 0)),
        out_shape=in_hbm((2, HALF, columns, columns), BF),
        compiler_params=limit(28),
        cost_estimate=cost(1e6, 1e5),
        name="expert_grads",
    )(from_hbm(values[0]), from_hbm(values[1]), from_hbm(values[2]), values[3])
    return outs.reshape(2 * HALF, columns, columns)


def out_grads_body(parts, *refs):
    pieces, d_a, outs = refs[:parts], refs[parts], refs[parts + 1 :]
    for k in list(range(1, parts)) + [0]:
        outs[k][...] = dot(pieces[k][...], d_a[...]).astype(BF)


def out_grads(pieces, d_a):
    parts = len(pieces)
    wide = pieces[0].shape[0]
    return pl.pallas_call(
        functools.partial(out_grads_body, parts),
        out_shape=[shape((wide, D), BF)] * parts,
        in_specs=vm(parts + 1),
        out_specs=vm(parts),
        compiler_params=limit(16),
        cost_estimate=cost(1e6, 1e5),
        name="out_grads",
    )(*pieces, d_a)


def attention_grads_body(parts, chunks, place, xn_ref, proj_ref, *refs):
    terms, (send_ref, keep_ref, out) = refs[:parts], refs[parts:]
    wide = terms[0].shape[0]
    rows, taken = D // chunks, wide // chunks
    out[:, : 3 * wide] = dot(xn_ref[...], proj_ref[...], 0, 0)
    total = terms[0][...].astype(F32)
    for k in range(1, parts):
        total = total + terms[k][...].astype(F32)
    for c in range(chunks):
        for b in range(D // wide):
            out[c * rows + b * taken : c * rows + (b + 1) * taken, 3 * wide :] = total[
                c * taken : (c + 1) * taken, b * wide : (b + 1) * wide
            ]
    first = place[1] == 0
    half = D // 2
    left, right = out[:, :half], out[:, half:]
    keep_ref[:, :half] = jnp.where(first, left, right).astype(BF)
    send_ref[:, :half] = jnp.where(first, right, left).astype(BF)


def attention_grads(place, xn, proj, terms):
    parts = len(terms)
    return pl.pallas_call(
        functools.partial(attention_grads_body, parts, lax.axis_size("dp")),
        out_shape=[shape((D, D // 2), BF)] * 2,
        in_specs=[smem()] + vm(2 + parts),
        out_specs=vm(2),
        scratch_shapes=[pltpu.VMEM((D, D), F32)],
        compiler_params=limit(24),
        cost_estimate=cost(1e6, 1e5),
        name="attention_grads",
    )(place, from_hbm(xn), from_hbm(proj), *terms)


def chunks_body(count, place, own, received, *outs):
    rows = outs[0].shape[0]
    for k in range(count):
        where = natural(place[3], k, rows)
        total = own[where, :].astype(F32) + received[where, :].astype(F32)
        outs[k][...] = total.astype(outs[k].dtype)


def scatter_small(place, own, received):
    count = lax.axis_size("dp")
    if count != 4:
        total = (own.astype(F32) + received.astype(F32)).astype(BF)
        return [total]
    dims = (own.shape[0] // count, own.shape[1])
    return pl.pallas_call(
        functools.partial(chunks_body, count),
        out_shape=[shape(dims, F32)] + [shape(dims, BF)] * (count - 1),
        in_specs=[smem()] + vm(2),
        out_specs=vm(count),
        compiler_params=limit(16),
        cost_estimate=cost(1e6, 1e5),
        name="chunks",
    )(place, own, received)


def scatter_move(chunks):
    return [chunks[0]] + [exchange(chunk, "dp", k) for k, chunk in enumerate(chunks) if k]


def scatter_total(chunks):
    if len(chunks) == 1:
        return lax.psum_scatter(chunks[0], "dp", scatter_dimension=0, tiled=True).astype(F32)
    return functools.reduce(jnp.add, [chunk.astype(F32) for chunk in chunks])


def scatter_end(chunks):
    return scatter_total(scatter_move(chunks))


def attention_results(value, wide):
    rows = value.shape[0]
    taken = rows // (D // wide)
    return (
        jnp.stack([value[:, i * wide : (i + 1) * wide] for i in range(3)]),
        jnp.concatenate(
            [value[b * taken : (b + 1) * taken, 3 * wide :] for b in range(D // wide)], axis=1
        ),
    )


def expert_results_body(place, own_0, moved_0, own_1, moved_1, down_ref, up_ref):
    i = pl.program_id(0)
    first = place[1] == 0
    own = (i < HALF) == first

    def put(value):
        down_ref[...] = value[0].astype(F32)
        up_ref[...] = value[1].astype(F32)

    for layer, own_ref, moved_ref in ((0, own_0, moved_0), (1, own_1, moved_1)):
        kept = first == (layer == 0)
        pl.when(kept & own)(functools.partial(put, own_ref))
        pl.when(kept & jnp.logical_not(own))(functools.partial(put, moved_ref))


def expert_results(place, sums, moved):
    rows, columns = sums[0].shape[1:]
    shaped = [
        a.reshape(2, HALF, rows, columns) for pair in zip(sums, moved) for a in pair
    ]
    block = pl.BlockSpec((2, 1, rows, columns), lambda i, place: (0, i % HALF, 0, 0))
    out = pl.BlockSpec((1, rows, columns), lambda i, place: (i, 0, 0))
    return pl.pallas_call(
        expert_results_body,
        grid_spec=pltpu.PrefetchScalarGridSpec(
            num_scalar_prefetch=1,
            grid=(EXPERTS,),
            in_specs=[block] * 4,
            out_specs=[out, out],
        ),
        out_shape=[shape((EXPERTS, rows, columns), F32)] * 2,
        compiler_params=limit(24),
        cost_estimate=cost(1e6, 1e5),
        name="expert_results",
    )(place, *shaped)


def scatter_sum(value, dim):
    return lax.psum_scatter(value, "dp", scatter_dimension=dim, tiled=True)


def phase(*values):
    return lax.optimization_barrier(values)


def sum_small(value, axis):
    count = lax.axis_size(axis)
    if count != 4:
        return lax.psum(value, axis)
    return (value + exchange(value, axis, 1)) + (
        exchange(value, axis, 2) + exchange(value, axis, 3)
    )


def local(
    inputs,
    norm_gains,
    attention_in,
    attention_out,
    bias_table,
    router_weight,
    up_weight,
    down_weight,
    routes,
    piece_starts,
    valid_mask,
    cotangent,
):
    s = lax.axis_index("section")
    t = lax.axis_index("tensor")
    z = lax.axis_index("dp")
    tensor = lax.axis_size("tensor")
    rows = inputs.shape[1]
    wide = attention_in.shape[3]
    heads = wide // HEAD_DIM
    first = s == 0

    def mine(array):
        return lax.dynamic_index_in_dim(array, s, 0, keepdims=False)

    def by_layer(own, other):
        return jnp.where(first, own, other), jnp.where(first, other, own)

    def swap(value):
        return jax.tree.map(lambda a: exchange(a, "section", 1), value)

    def pair(value):
        return value, swap(value)

    h0 = mine(inputs)
    g1 = mine(cotangent)
    place = [
        jnp.stack([t, s, jnp.where(s == layer, 0, 1), z]).astype(jnp.int32) for layer in range(2)
    ]
    selects = [place[layer][2:3] for layer in range(2)]
    order = jnp.where(first, jnp.array([2, 3, 0, 1]), jnp.array([0, 1, 2, 3])).astype(jnp.int32)
    hot = diagonal_one_hot()
    hot_rows = hot.transpose(2, 0, 1).reshape(BUCKETS, -1)

    gain_pair, table_pair = pair(norm_gains[0]), pair(bias_table[0].T)
    w_out_pair = pair(attention_out[0])

    def prepared(layer):
        return prepare(layer, place[layer], gain_pair, table_pair, hot_rows, valid_mask, rows)

    x_parts, first_prepared, gain_pair, table_pair, w_in_pair, w_out, route_pair, router_pair, up, down = phase(
        gather_parts(h0),
        prepared(0),
        gain_pair,
        table_pair,
        pair(jnp.swapaxes(attention_in[0], 1, 2).reshape(3 * wide, D)),
        by_layer(*w_out_pair),
        pair(routes[0, :, :, 0]),
        pair(jnp.pad(router_weight[0].T, ((0, 128 - EXPERTS), (0, 0)))),
        up_weight[0],
        down_weight[0],
    )

    gain, tile, valid_col, valid_own = first_prepared
    gains, tiles = [gain], [tile]
    hidden = [h0, None]
    saved, outputs, stats, w_out_parts = [], [], [], []
    for layer in range(2):
        kept, att_parts = fwd_attention(
            place[layer],
            piece_starts,
            valid_col,
            gains[layer],
            w_in_pair,
            tiles[layer],
            x_parts,
            layer == 0,
        )
        if layer == 0:
            w_out_parts.append(gather_parts(w_out[0]))
            up_pair, down_pair = pair(up), pair(down)
            att_parts, w_out_parts[0] = phase(att_parts, w_out_parts[0])
        else:
            g_parts = [g1] + [exchange(g1, "tensor", k) for k in range(1, tensor - 1)]
            att_parts, g_parts = phase(att_parts, g_parts)
        pieces = swap_parts(att_parts)
        mid, xn_mid, stat = after_attention(
            hidden[layer], gains[layer], valid_own, pieces, w_out_parts[layer]
        )
        if layer == 0:
            xn_mid, route_pair, router_pair, gain_pair, table_pair = phase(
                xn_mid, route_pair, router_pair, gain_pair, table_pair
            )
            targets = make_targets(place[0], route_pair, router_pair, tensor)
            gain, tile = prepared(1)
            gains.append(gain)
            tiles.append(tile)
        xn_parts = gather_parts(xn_mid)
        if layer == 0:
            xn_parts, targets, gains, tiles, up_pair, down_pair, w_out = phase(
                xn_parts, targets, gains, tiles, up_pair, down_pair, w_out
            )
        else:
            xn_parts, g1 = phase(xn_parts, g1)
        row, col, router = targets[layer::2]
        ex, y_parts = fwd_experts(
            selects[layer], order, row, col, router, up_pair, down_pair, xn_parts
        )
        if layer == 0:
            w_out_parts.append(gather_parts(w_out[1]))
            y_parts, w_out_parts[1], ex = phase(y_parts, w_out_parts[1], ex)
            y_parts = swap_parts(y_parts)
            fwd_sent = [ex[0]]
            saved.append([kept, pieces, mid, xn_mid, ex])
            combined, out, xn_next, stat_more = after_experts(
                mid, ex[2], gains[1], valid_own, y_parts
            )
            outputs.append(out)
            stats.append((stat, stat_more))
            saved[0].append(combined)
            hidden[1] = out
            x_parts = gather_parts(xn_next)
        else:
            g_parts.append(exchange(g1, "tensor", tensor - 1))
            y_parts, g_parts, ex = phase(y_parts, g_parts, ex)
            fwd_sent.append(ex[0])
            saved.append([kept, pieces, mid, xn_mid, ex])

    fwd_y_parts = y_parts
    small_1, square_1, expert_sums = None, [], []
    for layer in (1, 0):
        row, col, router = targets[layer::2]
        kept, pieces, mid, xn_mid, ex = saved[layer][:5]
        fwd_halves, slope, gate, probs = ex
        g = g_parts[0]
        bwd_halves, y_parts = bwd_experts(
            selects[layer], order, row, col, gate, slope, up_pair, down_pair, g_parts
        )
        fwd_other = swap(fwd_sent[layer])
        if layer == 1:
            y_parts, bwd_halves, fwd_y_parts, fwd_other = phase(
                y_parts, bwd_halves, swap_parts(fwd_y_parts), fwd_other
            )
            combined, out, _, stat_more = after_experts(
                mid, gate, gains[1], valid_own, fwd_y_parts
            )
            outputs.append(out)
            stats.append((stat, stat_more))
        else:
            y_parts, bwd_halves, fwd_other, square_1 = phase(
                y_parts, bwd_halves, fwd_other, scatter_move(square_1)
            )
            combined = saved[0][5]

        total = expert_grads((fwd_halves, fwd_other, bwd_halves, swap(bwd_halves)))
        y_parts, total, combined = phase(swap_parts(y_parts), total, combined)
        expert_sums.append(scatter_sum(total, 1))

        (d_mid, d_a, grad_gain_mid, grad_router), d_pieces = middle_back(
            g,
            combined,
            probs,
            col,
            router,
            mid,
            gains[layer],
            xn_mid,
            y_parts,
            w_out_parts[layer],
        )
        d_pieces, out_terms = phase(swap_parts(d_pieces), out_grads(pieces, d_a))

        xn, qkv, turned, lse = kept
        (d_proj, diag, far, grad_gain_in), x_terms = bwd_attention(
            place[layer],
            piece_starts,
            valid_col,
            gains[layer],
            w_in_pair,
            tiles[layer],
            (xn, qkv, turned, lse),
            d_pieces,
        )
        x_terms, d_proj, diag, far, out_terms = phase(
            x_terms, d_proj, diag, far, swap_parts(out_terms)
        )

        x_terms = swap_parts(x_terms)
        sent, square = attention_grads(place[layer], xn, d_proj, out_terms)
        small = small_sums(
            place[0],
            diag,
            far,
            hot_rows,
            grad_gain_in,
            grad_gain_mid,
            grad_router,
            stats[layer],
            small_1,
        )
        if layer == 1:
            x_terms, small_1, sent, square = phase(x_terms, small, sent, square)
            d_h_1, d_h_low = input_back(d_mid, hidden[1], gains[1], x_terms)
            g_parts, square_1 = phase(
                gather_parts(d_h_low), scatter_small(place[1], square, swap(sent))
            )
            d_h_1 = d_h_low

    def kept_sent(values):
        return jnp.where(first, values[0], values[1]), jnp.where(first, values[1], values[0])

    def placed(own, received, axis=0):
        return jnp.where(
            first,
            jnp.concatenate([own, received], axis=axis),
            jnp.concatenate([received, own], axis=axis),
        )

    x_terms, square, sent, small = phase(x_terms, square, sent, small)

    d_h = input_back(d_mid, hidden[0], gains[0], x_terms)[0]
    out_keep, out_sent = kept_sent(outputs)
    d_h_keep, d_h_sent = kept_sent((d_h, d_h_1.astype(F32)))
    small = small[0] + swap(small[1])
    sum_1, sum_0 = expert_sums
    out_moved, d_h_moved, small, shared, square, moved_1 = phase(
        swap(out_sent),
        swap(d_h_sent.astype(BF)),
        small,
        sum_small(small[:8], "tensor"),
        scatter_small(place[0], square, swap(sent)),
        lax.ppermute(sum_1, "section", [(0, 1)]),
    )
    small = sum_small(jnp.concatenate([shared, small[8:]], axis=0), "dp")
    table = small[8 : 8 + heads, :BUCKETS].T
    share = BUCKETS // lax.axis_size("dp")
    stat = small[6]
    layer_out = placed(out_keep[None], out_moved[None])
    input_grad = placed(d_h_keep[None], d_h_moved.astype(F32)[None])
    square_0, layer_out, input_grad, grad_gain, grad_table, grad_router, root_means = phase(
        scatter_end(square),
        layer_out,
        input_grad,
        small[0:2],
        lax.dynamic_slice_in_dim(table, z * share, share, 0),
        small[2:6].T,
        jnp.sqrt(stat[:3] / (stat[3] * D)),
    )
    keep, sent = kept_sent((square_0, scatter_total(square_1)))
    square = placed(keep, swap(sent.astype(BF)).astype(F32), axis=1)
    grad_w_in, grad_w_out = attention_results(square, wide)
    moved_0 = lax.ppermute(sum_0, "section", [(1, 0)])
    experts = expert_results(place[0], (sum_0, sum_1), (moved_0, moved_1))
    return (
        layer_out[None],
        input_grad[None],
        grad_gain[None],
        grad_w_in[None],
        grad_w_out[None],
        grad_table[None],
        grad_router[None],
        experts[1][None],
        experts[0][None],
        root_means[None],
    )


def solution(mesh):
    placed = (
        P("dp", "tensor", None),
        P("section", None, None),
        P("section", None, None, "tensor"),
        P("section", "tensor", None),
        P("section", None, "tensor"),
        P("section", None, None),
        P("section", None, None, "tensor"),
        P("section", None, "tensor", None),
        P("section", "dp", None, None),
        P("dp", None),
        P("dp", None),
        P("dp", "tensor", None),
    )
    return jax.shard_map(
        local,
        mesh=mesh,
        in_specs=placed,
        out_specs=(
            P("section", "dp", "tensor", None),
            P("section", "dp", "tensor", None),
            P("section", None, None),
            P("section", None, "dp", "tensor"),
            P("section", ("tensor", "dp"), None),
            P("section", "dp", "tensor"),
            P("section", None, None),
            P("section", None, "dp", "tensor"),
            P("section", None, ("tensor", "dp"), None),
            P("section", None),
        ),
        check_vma=False,
    )
```
